128 devices in a mesh: store: 32 (over x, z, core), batch: 4 (over y).
Axes of the slice: x: 4, y: 4, z: 4, core: 2. Of those that a mesh axis runs over, the one named last changes fastest.
Arguments:
- features: bfloat16 [524288, 768], P(('store', 'batch')), may hold values from -6 to 6
- source_part: int32 [131072], P(('store', 'batch')), may hold values from 0 to 127, as said below
- source_row: int32 [131072], P(('store', 'batch')), may hold values from 0 to 4095
- adj_tiles: bfloat16 [6144, 128, 128], P(('store', 'batch')), may hold values from -0.25 to 0.25
- tile_row: int32 [6144], P(('store', 'batch')), may hold values from 0 to 7, as said below
- tile_col: int32 [6144], P(('store', 'batch')), may hold values from 0 to 7, as said below
- tile_count: int32 [128], P(('store', 'batch')), may hold values from 24 to 48
- labels: int32 [131072], P(('store', 'batch')), may hold values from 0 to 152
- layer_one: bfloat16 [768, 1024], replicated, may hold values from -0.21875 to 0.21875
- layer_two: bfloat16 [1024, 153], replicated
Outputs:
- grad_one: float32 [768, 1024], replicated
- grad_two: float32 [1024, 153], replicated
- loss: float32 [], replicated
The draws below stay inside these ranges and needn't reach their ends.
Inputs may be any that keep to these rules, and one draw needn't show every extreme that they name: `source_part`: within each batch no storage owner appears more than 16 times, and every batch takes exactly 16 nodes from the owner with its own index. Within each batch the first 1024 // 128 tiles are the diagonal ones; the live tiles of a batch have pairwise different (tile_row, tile_col) pairs; entries at and beyond the batch's tile_count are 0. `tile_col`: as tile_row.
All inputs are finite; a program needn't handle non-finite values.
Results may differ from the reference program's by a relative error of at most 0.0065.
Values may be sent and summed in bfloat16 or wider, within the bound.
No kernel may reach another device: no remote copies, remote signals or barrier semaphores. Data moves between devices by JAX's collectives and lax.ppermute only.
A program may use at most 64 MiB of HBM per device.

```python
from functools import partial
import jax
import jax.numpy as jnp
from jax import lax

F = 768
HID = 1024
CLASSES = 153
TILE = 128
NODES_DEV = 1024
TABLE_DEV = 4096
CAP = 16
TILES_MAX = 48
NODES = 131072
N_STORE = 32
N_BATCH = 4
DEVICES = 128


def layout(key):
    devices = NODES // NODES_DEV
    blocks = NODES_DEV // TILE
    lowest = max(blocks, TILES_MAX // 2)
    counts = jax.random.randint(jax.random.fold_in(key, 11), (devices,), lowest, TILES_MAX + 1)
    chosen = jax.random.randint(jax.random.fold_in(key, 12), (), 0, devices)
    counts = jnp.where(jnp.arange(devices) == chosen, TILES_MAX, counts).astype(jnp.int32)
    places = jnp.arange(TILES_MAX, dtype=jnp.int32)[None, :]
    pair_ids = jnp.arange(blocks * blocks, dtype=jnp.int32)
    pair_row = pair_ids // blocks
    pair_col = pair_ids % blocks
    off_ids = jnp.where(pair_row != pair_col, pair_ids, blocks * blocks + pair_ids)
    off_sorted = jnp.sort(off_ids)[:blocks * blocks - blocks]
    extra = TILES_MAX - blocks

    def pick(device):
        order = jax.random.permutation(jax.random.fold_in(jax.random.fold_in(key, 13), device), blocks * blocks - blocks)
        chosen_pairs = off_sorted[order[:extra]]
        whole = jnp.concatenate([jnp.arange(blocks, dtype=jnp.int32) * (blocks + 1), chosen_pairs])
        return (whole // blocks, whole % blocks)
    row_ids, col_ids = jax.vmap(pick)(jnp.arange(devices, dtype=jnp.int32))
    live = places < counts[:, None]
    row_ids = jnp.where(live, row_ids, 0).astype(jnp.int32)
    col_ids = jnp.where(live, col_ids, 0).astype(jnp.int32)
    return (row_ids.reshape(-1), col_ids.reshape(-1), counts)


def draw_tile_row(key, part):
    return layout(key)[0]


def draw_tile_col(key, part):
    return layout(key)[1]


def draw_tile_count(key, part):
    return layout(key)[2]


def draw_source_part(key, part):
    key = jax.random.fold_in(key, 3)
    devices = NODES // NODES_DEV

    def one_batch(device):
        inner = jax.random.fold_in(key, device)
        picks = jax.random.permutation(jax.random.fold_in(inner, 1), (devices - 1) * CAP)[:NODES_DEV - CAP]
        peers = (picks // CAP).astype(jnp.int32)
        peers = peers + (peers >= device).astype(jnp.int32)
        merged = jnp.concatenate([jnp.full((CAP,), device, jnp.int32), peers])
        order = jax.random.permutation(jax.random.fold_in(inner, 2), NODES_DEV)
        return merged[order]
    return jax.vmap(one_batch)(jnp.arange(devices, dtype=jnp.int32)).reshape(-1)


def draw_layer_two(key, part):
    key = jax.random.fold_in(key, 7)
    values = jax.random.normal(jax.random.fold_in(key, 1), (HID, CLASSES), jnp.float32) / jnp.sqrt(HID * 1.0)
    return values.astype(jnp.bfloat16)


def touch_ends(array, stream_key, smallest, high):
    spot = [jax.random.randint(jax.random.fold_in(stream_key, axis), (), 0, length) for axis, length in enumerate(array.shape)]
    longest = array.shape.index(max(array.shape))
    beside = spot[:longest] + [(spot[longest] + 1) % array.shape[longest]] + spot[longest + 1:]
    return array.at[tuple(spot)].set(smallest).at[tuple(beside)].set(high)


def levels(rng, dims, split, smallest, high):
    gain, own = 1.0, jax.random.fold_in(rng, 6)
    for axis_at, blocks in split:
        draws = jnp.exp(jax.random.uniform(jax.random.fold_in(own, axis_at), (blocks,), jnp.float32, smallest / len(split), high / len(split)))
        gain = gain * jnp.repeat(draws, dims[axis_at] // blocks).reshape([-1 if axis == axis_at else 1 for axis in range(len(dims))])
    return gain


def normal_values(rng, shape, deviation, most, cuts=(), kind=jnp.bfloat16):
    gain = levels(rng, shape, cuts, -0.22, 0.18) if cuts else 1.0
    array = jax.random.normal(rng, shape, jnp.float32) * deviation * gain
    return jnp.minimum(jnp.maximum(array, -most), most).astype(kind)


def setup_inputs(seed: int = 0) -> dict:
    streams_of = jax.random.split(jax.random.key(seed), 11)
    return {
        "features": normal_values(streams_of[0], (DEVICES * TABLE_DEV, F), 1.0, 6.0, ((0, 128),)),
        "source_part": draw_source_part(jax.random.fold_in(streams_of[10], 71), 0),
        "source_row": touch_ends(jax.random.randint(streams_of[2], (NODES,), 0, TABLE_DEV), jax.random.fold_in(streams_of[2], 1), 0, TABLE_DEV - 1).astype(jnp.int32),
        "adj_tiles": normal_values(streams_of[3], (DEVICES * TILES_MAX, TILE, TILE), (TILE * 5) ** -0.5, 0.25, ((0, 128),)),
        "tile_row": draw_tile_row(jax.random.fold_in(streams_of[10], 71), 0),
        "tile_col": draw_tile_col(jax.random.fold_in(streams_of[10], 71), 0),
        "tile_count": draw_tile_count(jax.random.fold_in(streams_of[10], 71), 0),
        "labels": touch_ends(jax.random.randint(streams_of[7], (NODES,), 0, CLASSES), jax.random.fold_in(streams_of[7], 1), 0, CLASSES - 1).astype(jnp.int32),
        "layer_one": normal_values(streams_of[8], (F, HID), F ** -0.5, 0.21875),
        "layer_two": draw_layer_two(jax.random.fold_in(streams_of[10], 71), 0),
    }


def spread(adj_tiles, tile_row, tile_col, live_count, values, transpose):
    nodes, width = values.shape
    blocks = values.reshape(nodes // TILE, TILE, width).astype(jnp.float32)
    live = jnp.arange(tile_row.shape[0], dtype=jnp.int32) < live_count
    if transpose:
        picked = blocks[tile_row]
        product = jnp.einsum('tji,tjw->tiw', adj_tiles.astype(jnp.float32), picked, precision=lax.Precision.HIGHEST)
        target = tile_col
    else:
        picked = blocks[tile_col]
        product = jnp.einsum('tij,tjw->tiw', adj_tiles.astype(jnp.float32), picked, precision=lax.Precision.HIGHEST)
        target = tile_row
    member = ((target[None, :] == jnp.arange(nodes // TILE, dtype=jnp.int32)[:, None]) & live[None, :]).astype(jnp.float32)
    summed = jnp.einsum('rt,tiw->riw', member, product, precision=lax.Precision.HIGHEST)
    return summed.reshape(nodes, width)

def local_terms(inputs, adj_tiles, tile_row, tile_col, live_count, labels, layer_one, layer_two):
    mixed = spread(adj_tiles, tile_row, tile_col, live_count, inputs, False).astype(jnp.bfloat16)
    before = jnp.dot(mixed, layer_one, preferred_element_type=jnp.float32)
    hidden = jax.nn.gelu(before, approximate=True).astype(jnp.bfloat16)
    smooth = spread(adj_tiles, tile_row, tile_col, live_count, hidden, False).astype(jnp.bfloat16)
    logits = jnp.dot(smooth, layer_two, preferred_element_type=jnp.float32)
    largest = lax.optimization_barrier(jnp.max(logits, axis=1, keepdims=True))
    logsum = jnp.log(lax.optimization_barrier(jnp.sum(jnp.exp(logits - largest), axis=1, keepdims=True))) + largest
    truth = (labels[:, None] == jnp.arange(logits.shape[1], dtype=jnp.int32)[None, :]).astype(jnp.float32)
    batch_loss = jnp.mean(logsum[:, 0] - lax.optimization_barrier(jnp.sum(truth * logits, axis=1)))
    upstream = ((jnp.exp(logits - logsum) - truth) / logits.shape[0]).astype(jnp.bfloat16)
    grad_two = jnp.dot(smooth.T, upstream, preferred_element_type=jnp.float32)
    back_smooth = jnp.dot(upstream, layer_two.T, preferred_element_type=jnp.float32).astype(jnp.bfloat16)
    back_hidden = spread(adj_tiles, tile_row, tile_col, live_count, back_smooth, True)
    back_before = jax.vjp(partial(jax.nn.gelu, approximate=True), before)[1](back_hidden)[0].astype(jnp.bfloat16)
    grad_one = jnp.dot(mixed.T, back_before, preferred_element_type=jnp.float32)
    return (grad_one, grad_two, batch_loss)

def reference(features, source_part, source_row, adj_tiles, tile_row, tile_col, tile_count, labels, layer_one, layer_two):

    def one_batch(carry, device):
        start = (device * NODES_DEV).astype(jnp.int32)
        first = (device * TILES_MAX).astype(jnp.int32)
        parts = lax.dynamic_slice_in_dim(source_part, start, NODES_DEV)
        rows = lax.dynamic_slice_in_dim(source_row, start, NODES_DEV)
        inputs = features[(parts * TABLE_DEV + rows).astype(jnp.int32)]
        grad_one, grad_two, batch_loss = local_terms(inputs, lax.dynamic_slice_in_dim(adj_tiles, first, TILES_MAX), lax.dynamic_slice_in_dim(tile_row, first, TILES_MAX), lax.dynamic_slice_in_dim(tile_col, first, TILES_MAX), tile_count[device], lax.dynamic_slice_in_dim(labels, start, NODES_DEV), layer_one, layer_two)
        return ((carry[0] + grad_one, carry[1] + grad_two, carry[2] + batch_loss), None)
    initial = (jnp.zeros((F, HID), jnp.float32), jnp.zeros((HID, CLASSES), jnp.float32), jnp.zeros((), jnp.float32))
    totals, unused = lax.scan(one_batch, initial, jnp.arange(N_STORE * N_BATCH, dtype=jnp.int32))
    return (totals[0], totals[1], totals[2])
```

```python
from functools import partial

import jax
import jax.numpy as jnp
from jax import lax
from jax.experimental import pallas as pl
from jax.experimental.pallas import tpu as pltpu
from jax.sharding import PartitionSpec as P

AXES = ("store", "batch")
SIDE = 4
WIDTH = 128
LOSS_ROW = 921
ROWS = 928


def flat(x, y, z, core):
    return ((x * SIDE + z) * 2 + core) * SIDE + y


def shift_pairs(axes, offset):
    pairs = []
    for x in range(SIDE):
        for y in range(SIDE):
            for z in range(SIDE):
                for core in range(2):
                    place = [x, y, z]
                    place[axes[core]] = (place[axes[core]] + offset) % SIDE
                    pairs.append((flat(x, y, z, core), flat(*place, core)))
    return pairs


def swap_pairs():
    return [
        (flat(x, y, z, core), flat(x, y, z, 1 - core))
        for x in range(SIDE)
        for y in range(SIDE)
        for z in range(SIDE)
        for core in range(2)
    ]


FIRST, SECOND, THIRD = (0, 1), (1, 2), (2, 0)


def split_loss(total):
    tail = total[ROWS - 8 :, :]
    row = lax.broadcasted_iota(jnp.int32, tail.shape, 0)
    lane = lax.broadcasted_iota(jnp.int32, tail.shape, 1)
    here = row == LOSS_ROW - (ROWS - 8)
    loss = jnp.sum(jnp.where(here & (lane < 3), tail, 0.0), axis=1, keepdims=True)
    high = loss.astype(jnp.bfloat16).astype(jnp.float32)
    middle = (loss - high).astype(jnp.bfloat16).astype(jnp.float32)
    low = (loss - high - middle).astype(jnp.bfloat16).astype(jnp.float32)
    parts = jnp.where(lane == 0, high, jnp.where(lane == 1, middle, jnp.where(lane == 2, low, 0.0)))
    return jnp.where(here, parts, tail)


def store_total(out, columns, total):
    out[: ROWS - 16, columns] = total[: ROWS - 16].astype(jnp.bfloat16)
    last = jnp.concatenate([total[ROWS - 16 : ROWS - 8], split_loss(total)], axis=0)
    out[ROWS - 16 :, columns] = last.astype(jnp.bfloat16)


def first_add(place, own, arrived, keep, one, two, three):
    for offset, out in ((1, one), (2, two), (3, three), (0, keep)):
        block = lax.rem(place[0] + offset, SIDE)
        columns = pl.ds(pl.multiple_of(block * WIDTH, WIDTH), WIDTH)
        total = own[:, columns].astype(jnp.float32) + arrived[:, columns].astype(jnp.float32)
        store_total(out, slice(None), total)


def four_add(own, one, two, three, out):
    total = (own[...].astype(jnp.float32) + two[...].astype(jnp.float32)) + (
        one[...].astype(jnp.float32) + three[...].astype(jnp.float32)
    )
    store_total(out, slice(None), total)


def place_blocks(place, own, one, two, three, out):
    for offset, block in ((0, own), (1, one), (2, two), (3, three)):
        at = lax.rem(place[0] + SIDE - offset, SIDE)
        out[:, pl.ds(pl.multiple_of(at * WIDTH, WIDTH), WIDTH)] = block[...]


def finish(core, own, other, grad_one, grad_two, loss):
    half = SIDE * WIDTH
    features = grad_one.shape[0]
    classes = grad_two.shape[0]
    for offset, part in ((0, own), (1, other)):
        at = lax.rem(core[0] + offset, 2)
        columns = pl.ds(pl.multiple_of(at * half, half), half)
        grad_one[:, columns] = part[:features, :].astype(jnp.float32)
        grad_two[:, columns] = part[features:, :].astype(jnp.float32)[:classes]

        @pl.when(at == 0)
        def _():
            tail = part[ROWS - 16 :, :WIDTH].astype(jnp.float32)
            row = lax.broadcasted_iota(jnp.int32, tail.shape, 0)
            lane = lax.broadcasted_iota(jnp.int32, tail.shape, 1)
            mine = (row == LOSS_ROW - (ROWS - 16)) & (lane < 3)
            loss[...] = jnp.sum(
                jnp.sum(jnp.where(mine, tail, 0.0), axis=1, keepdims=True), axis=0, keepdims=True
            )


def call(kernel, outs, scalars=0, arrays=0, limit=40 << 20, cost=None):
    vmem = pl.BlockSpec(memory_space=pltpu.VMEM)
    smem = pl.BlockSpec(memory_space=pltpu.SMEM)
    return pl.pallas_call(
        kernel,
        out_shape=outs,
        in_specs=[smem] * scalars + [vmem] * arrays,
        out_specs=jax.tree.map(lambda _: vmem, outs),
        compiler_params=pltpu.CompilerParams(vmem_limit_bytes=limit),
        cost_estimate=cost,
    )


def sum_over_devices(sent, own, features, classes):
    store, batch = lax.axis_index("store"), lax.axis_index("batch")
    core = lax.rem(store, 2)
    place = jnp.where(core == 0, store // (2 * SIDE), batch).astype(jnp.int32).reshape(1)
    core = core.astype(jnp.int32).reshape(1)
    bf = jnp.bfloat16
    block = jax.ShapeDtypeStruct((ROWS, WIDTH), bf)
    arrived = lax.ppermute(sent, AXES, swap_pairs())
    keep, *parts = call(first_add, [block] * 4, 1, 2)(place, own, arrived)
    got = [lax.ppermute(part, AXES, shift_pairs(FIRST, k + 1)) for k, part in enumerate(parts)]
    total = call(four_add, block, 0, 4)(keep, *got)
    for axes in (SECOND, THIRD):
        got = [lax.ppermute(total, AXES, shift_pairs(axes, k)) for k in (1, 2, 3)]
        total = call(four_add, block, 0, 4)(total, *got)
    got = [lax.ppermute(total, AXES, shift_pairs(FIRST, k)) for k in (1, 2, 3)]
    strip = call(place_blocks, jax.ShapeDtypeStruct((ROWS, SIDE * WIDTH), bf), 1, 4)(
        place, total, *got
    )
    other = lax.ppermute(strip, AXES, swap_pairs())
    hidden = 2 * SIDE * WIDTH
    return call(
        finish,
        [
            jax.ShapeDtypeStruct((features, hidden), jnp.float32),
            jax.ShapeDtypeStruct((classes, hidden), jnp.float32),
            jax.ShapeDtypeStruct((1, 1), jnp.float32),
        ],
        1,
        2,
    )(core, strip, other)


def densify(adj_tiles, tile_row, tile_col, live_count, nodes):
    tile = adj_tiles.shape[1]
    blocks = nodes // tile
    live = jnp.arange(tile_row.shape[0], dtype=jnp.int32) < live_count
    masked = jnp.where(live[:, None, None], adj_tiles, jnp.zeros_like(adj_tiles))
    grid = jnp.zeros((blocks, blocks, tile, tile), jnp.bfloat16).at[tile_row, tile_col].add(masked)
    return grid.transpose(0, 2, 1, 3).reshape(nodes, nodes)


def forward_spread(dense, values):
    return jnp.dot(dense, values, preferred_element_type=jnp.float32)


def backward_spread(dense, values):
    return lax.dot_general(
        dense, values, (((0,), (0,)), ((), ())), preferred_element_type=jnp.float32
    )


def on_device(
    features,
    source_part,
    source_row,
    adj_tiles,
    tile_row,
    tile_col,
    tile_count,
    labels,
    layer_one,
    layer_two,
):
    devices = lax.axis_size(("store", "batch"))
    nodes = source_part.shape[0]
    capacity = max(2, 2 * nodes // devices)
    owners = (source_part[:, None] == jnp.arange(devices, dtype=jnp.int32)[None, :]).astype(
        jnp.int32
    )
    ranking = jnp.cumsum(owners, axis=0) - 1
    source_slot = jnp.sum(owners * ranking, axis=1)
    position = source_part * capacity + source_slot
    requests = (
        jnp.zeros((devices * capacity,), jnp.int32)
        .at[position]
        .set(source_row)
        .reshape(devices, capacity)
    )
    found = features[
        lax.all_to_all(requests, ("store", "batch"), split_axis=0, concat_axis=0, tiled=True)
    ]
    arrived = lax.all_to_all(found, ("store", "batch"), split_axis=0, concat_axis=0, tiled=True)
    inputs = arrived.reshape(devices * capacity, features.shape[1])[position]
    dense = densify(adj_tiles, tile_row, tile_col, tile_count[0], nodes)
    mixed = forward_spread(dense, inputs).astype(jnp.bfloat16)
    before = jnp.dot(mixed, layer_one, preferred_element_type=jnp.float32)
    hidden = jax.nn.gelu(before, approximate=True).astype(jnp.bfloat16)
    smooth = forward_spread(dense, hidden).astype(jnp.bfloat16)
    logits = jnp.dot(smooth, layer_two, preferred_element_type=jnp.float32)
    largest = jnp.max(logits, axis=1, keepdims=True)
    logsum = jnp.log(jnp.sum(jnp.exp(logits - largest), axis=1, keepdims=True)) + largest
    truth = (labels[:, None] == jnp.arange(logits.shape[1], dtype=jnp.int32)[None, :]).astype(
        jnp.float32
    )
    batch_loss = jnp.mean(logsum[:, 0] - jnp.sum(truth * logits, axis=1))
    upstream = ((jnp.exp(logits - logsum) - truth) / logits.shape[0]).astype(jnp.bfloat16)
    grad_two = lax.dot_general(
        upstream, smooth, (((0,), (0,)), ((), ())), preferred_element_type=jnp.float32
    )
    back_smooth = jnp.dot(upstream, layer_two.T, preferred_element_type=jnp.float32).astype(
        jnp.bfloat16
    )
    back_hidden = backward_spread(dense, back_smooth)
    back_before = jax.vjp(partial(jax.nn.gelu, approximate=True), before)[1](back_hidden)[0].astype(
        jnp.bfloat16
    )
    grad_one = jnp.dot(mixed.T, back_before, preferred_element_type=jnp.float32)
    width, classes = grad_one.shape[0], grad_two.shape[0]
    high = batch_loss.astype(jnp.bfloat16).astype(jnp.float32)
    middle = (batch_loss - high).astype(jnp.bfloat16).astype(jnp.float32)
    low = batch_loss - high - middle
    loss_row = jnp.pad(jnp.stack([high, middle, low]).reshape(1, 3), ((0, 0), (0, grad_one.shape[1] - 3)))
    stacked = jnp.concatenate(
        [grad_one, grad_two, loss_row, jnp.zeros((ROWS - LOSS_ROW - 1, grad_one.shape[1]), jnp.float32)]
    ).astype(jnp.bfloat16)
    core = lax.rem(lax.axis_index("store"), 2)
    half = SIDE * WIDTH
    own = lax.dynamic_slice_in_dim(stacked, core * half, half, 1)
    sent = lax.dynamic_slice_in_dim(stacked, (1 - core) * half, half, 1)
    grad_one, grad_two, loss = sum_over_devices(sent, own, width, classes)
    return (grad_one, grad_two.T, loss.reshape(()))


def solution(mesh):
    return jax.shard_map(
        on_device,
        mesh=mesh,
        in_specs=(
            P(("store", "batch"), None),
            P(("store", "batch")),
            P(("store", "batch")),
            P(("store", "batch"), None, None),
            P(("store", "batch")),
            P(("store", "batch")),
            P(("store", "batch")),
            P(("store", "batch")),
            P(),
            P(),
        ),
        out_specs=(P(), P(), P()),
        check_vma=False,
    )
```

```python
from functools import partial

import jax
import jax.numpy as jnp
from jax import lax
from jax.experimental import pallas as pl
from jax.experimental.pallas import tpu as pltpu
from jax.sharding import PartitionSpec as P

AXES = ("store", "batch")
SIDE = 4
WIDTH = 128
LOSS_ROW = 921
ROWS = 928


def flat(x, y, z, core):
    return ((x * SIDE + z) * 2 + core) * SIDE + y


def shift_pairs(axes, offset):
    pairs = []
    for x in range(SIDE):
        for y in range(SIDE):
            for z in range(SIDE):
                for core in range(2):
                    place = [x, y, z]
                    place[axes[core]] = (place[axes[core]] + offset) % SIDE
                    pairs.append((flat(x, y, z, core), flat(*place, core)))
    return pairs


def swap_pairs():
    return [
        (flat(x, y, z, core), flat(x, y, z, 1 - core))
        for x in range(SIDE)
        for y in range(SIDE)
        for z in range(SIDE)
        for core in range(2)
    ]


FIRST, SECOND, THIRD = (0, 1), (1, 2), (2, 0)


def split_loss(total):
    tail = total[ROWS - 8 :, :]
    row = lax.broadcasted_iota(jnp.int32, tail.shape, 0)
    lane = lax.broadcasted_iota(jnp.int32, tail.shape, 1)
    here = row == LOSS_ROW - (ROWS - 8)
    loss = jnp.sum(jnp.where(here & (lane < 3), tail, 0.0), axis=1, keepdims=True)
    high = loss.astype(jnp.bfloat16).astype(jnp.float32)
    middle = (loss - high).astype(jnp.bfloat16).astype(jnp.float32)
    low = (loss - high - middle).astype(jnp.bfloat16).astype(jnp.float32)
    parts = jnp.where(lane == 0, high, jnp.where(lane == 1, middle, jnp.where(lane == 2, low, 0.0)))
    return jnp.where(here, parts, tail)


def store_total(out, columns, total):
    out[: ROWS - 16, columns] = total[: ROWS - 16].astype(jnp.bfloat16)
    last = jnp.concatenate([total[ROWS - 16 : ROWS - 8], split_loss(total)], axis=0)
    out[ROWS - 16 :, columns] = last.astype(jnp.bfloat16)


def first_add(place, own, arrived, keep, one, two, three):
    for offset, out in ((1, one), (2, two), (3, three), (0, keep)):
        block = lax.rem(place[0] + offset, SIDE)
        columns = pl.ds(pl.multiple_of(block * WIDTH, WIDTH), WIDTH)
        total = own[:, columns].astype(jnp.float32) + arrived[:, columns].astype(jnp.float32)
        store_total(out, slice(None), total)


def four_add(own, one, two, three, out):
    total = (own[...].astype(jnp.float32) + two[...].astype(jnp.float32)) + (
        one[...].astype(jnp.float32) + three[...].astype(jnp.float32)
    )
    store_total(out, slice(None), total)


def place_blocks(place, own, one, two, three, out):
    for offset, block in ((0, own), (1, one), (2, two), (3, three)):
        at = lax.rem(place[0] + SIDE - offset, SIDE)
        out[:, pl.ds(pl.multiple_of(at * WIDTH, WIDTH), WIDTH)] = block[...]


def finish(core, own, other, grad_one, grad_two, loss):
    half = SIDE * WIDTH
    features = grad_one.shape[0]
    classes = grad_two.shape[0]
    for offset, part in ((0, own), (1, other)):
        at = lax.rem(core[0] + offset, 2)
        columns = pl.ds(pl.multiple_of(at * half, half), half)
        grad_one[:, columns] = part[:features, :].astype(jnp.float32)
        grad_two[:, columns] = part[features:, :].astype(jnp.float32)[:classes]

        @pl.when(at == 0)
        def _():
            tail = part[ROWS - 16 :, :WIDTH].astype(jnp.float32)
            row = lax.broadcasted_iota(jnp.int32, tail.shape, 0)
            lane = lax.broadcasted_iota(jnp.int32, tail.shape, 1)
            mine = (row == LOSS_ROW - (ROWS - 16)) & (lane < 3)
            loss[...] = jnp.sum(
                jnp.sum(jnp.where(mine, tail, 0.0), axis=1, keepdims=True), axis=0, keepdims=True
            )


def call(kernel, outs, scalars=0, arrays=0, limit=40 << 20, cost=None):
    vmem = pl.BlockSpec(memory_space=pltpu.VMEM)
    smem = pl.BlockSpec(memory_space=pltpu.SMEM)
    return pl.pallas_call(
        kernel,
        out_shape=outs,
        in_specs=[smem] * scalars + [vmem] * arrays,
        out_specs=jax.tree.map(lambda _: vmem, outs),
        compiler_params=pltpu.CompilerParams(vmem_limit_bytes=limit),
        cost_estimate=cost,
    )


def sum_over_devices(sent, own, features, classes):
    store, batch = lax.axis_index("store"), lax.axis_index("batch")
    core = lax.rem(store, 2)
    place = jnp.where(core == 0, store // (2 * SIDE), batch).astype(jnp.int32).reshape(1)
    core = core.astype(jnp.int32).reshape(1)
    bf = jnp.bfloat16
    block = jax.ShapeDtypeStruct((ROWS, WIDTH), bf)
    arrived = lax.ppermute(sent, AXES, swap_pairs())
    keep, *parts = call(first_add, [block] * 4, 1, 2)(place, own, arrived)
    got = [lax.ppermute(part, AXES, shift_pairs(FIRST, k + 1)) for k, part in enumerate(parts)]
    total = call(four_add, block, 0, 4)(keep, *got)
    for axes in (SECOND, THIRD):
        got = [lax.ppermute(total, AXES, shift_pairs(axes, k)) for k in (1, 2, 3)]
        total = call(four_add, block, 0, 4)(total, *got)
    got = [lax.ppermute(total, AXES, shift_pairs(FIRST, k)) for k in (1, 2, 3)]
    strip = call(place_blocks, jax.ShapeDtypeStruct((ROWS, SIDE * WIDTH), bf), 1, 4)(
        place, total, *got
    )
    other = lax.ppermute(strip, AXES, swap_pairs())
    hidden = 2 * SIDE * WIDTH
    return call(
        finish,
        [
            jax.ShapeDtypeStruct((features, hidden), jnp.float32),
            jax.ShapeDtypeStruct((classes, hidden), jnp.float32),
            jax.ShapeDtypeStruct((1, 1), jnp.float32),
        ],
        1,
        2,
    )(core, strip, other)


def number_requests(parts, rows, requests, position):
    devices, capacity = requests.shape
    nodes = parts.shape[1]
    piece = 128
    owner = lax.broadcasted_iota(jnp.int32, (devices, nodes), 0)
    mine = jnp.where(owner == parts[...], 1.0, 0.0)
    line = lax.broadcasted_iota(jnp.int32, (piece, piece), 0)
    lane = lax.broadcasted_iota(jnp.int32, (piece, piece), 1)
    earlier = jnp.where(line < lane, 1.0, 0.0).astype(jnp.bfloat16)
    seen = jnp.zeros((devices, 1), jnp.float32)
    slots = []
    for start in range(0, nodes, piece):
        here = mine[:, start : start + piece]
        rank = jnp.dot(here.astype(jnp.bfloat16), earlier, preferred_element_type=jnp.float32)
        slots.append(jnp.sum(here * (rank + seen), axis=0, keepdims=True))
        seen = seen + jnp.sum(here, axis=1, keepdims=True)
    slot = jnp.concatenate(slots, axis=1).astype(jnp.int32)
    position[...] = parts[...] * capacity + slot
    placed = lax.broadcasted_iota(jnp.int32, (capacity, nodes), 0) == slot
    total = jnp.zeros((devices, capacity), jnp.float32)
    for scale, digit in ((64.0, lax.shift_right_logical(rows[...], 6)), (1.0, rows[...] & 63)):
        values = jnp.where(placed, digit.astype(jnp.float32), 0.0).astype(jnp.bfloat16)
        total += scale * lax.dot_general(
            mine.astype(jnp.bfloat16),
            values,
            (((1,), (1,)), ((), ())),
            preferred_element_type=jnp.float32,
        )
    requests[...] = total.astype(jnp.int32)


def build_spread(row, column, count, tiles, position, dense, turned, moved):
    nodes = dense.shape[0]
    tile = tiles.shape[1]
    dense[...] = jnp.zeros_like(dense)
    turned[...] = jnp.zeros_like(turned)

    @pl.loop(0, count[0])
    def _(t):
        at_row = pl.ds(pl.multiple_of(row[t] * tile, tile), tile)
        at_column = pl.ds(pl.multiple_of(column[t] * tile, tile), tile)
        values = tiles[t]
        dense[at_row, at_column] = values
        turned[at_column, at_row] = values.T

    width = 256

    @pl.loop(0, moved.shape[1] // width)
    def _(step):
        start = pl.multiple_of(step * width, width)
        slot = lax.broadcasted_iota(jnp.int32, (width, nodes), 0) + start
        chosen = jnp.where(slot == position[...], 1.0, 0.0).astype(jnp.bfloat16)
        moved[:, pl.ds(start, width)] = lax.dot_general(
            dense[...], chosen, (((1,), (1,)), ((), ())), preferred_element_type=jnp.float32
        ).astype(jnp.bfloat16)


def train(
    core,
    arrived,
    moved,
    dense,
    turned,
    layer_one,
    layer_two,
    labels,
    sent,
    own,
    mixed_turned,
    slope,
    hidden,
    smooth,
    upstream,
    upstream_turned,
    *,
    classes,
):
    nodes = dense.shape[0]
    features = mixed_turned.shape[0]
    step = 256
    for start in range(0, nodes, step):
        rows = slice(start, start + step)
        mixed = jnp.dot(moved[rows, :], arrived[...], preferred_element_type=jnp.float32).astype(
            jnp.bfloat16
        )
        mixed_turned[:, rows] = mixed.T
        before = jnp.dot(mixed, layer_one[...], preferred_element_type=jnp.float32)
        square = before * before
        rate = 0.7978845608028654
        bend = jnp.tanh(rate * before * (1.0 + 0.044715 * square))
        rise = 0.5 * (1.0 + bend)
        hidden[rows, :] = (before * rise).astype(jnp.bfloat16)
        slope[rows, :] = rise + 0.5 * before * (1.0 - bend * bend) * (
            rate + (3.0 * 0.044715 * rate) * square
        )
    loss = jnp.zeros((1, 1), jnp.float32)
    for start in range(0, nodes, step):
        rows = slice(start, start + step)
        spread = jnp.dot(dense[rows, :], hidden[...], preferred_element_type=jnp.float32).astype(
            jnp.bfloat16
        )
        smooth[rows, :] = spread
        logits = lax.dot_general(
            spread, layer_two[...], (((1,), (1,)), ((), ())), preferred_element_type=jnp.float32
        )
        lane = lax.broadcasted_iota(jnp.int32, logits.shape, 1)
        logits = jnp.where(lane < classes, logits, -jnp.inf)
        largest = jnp.max(logits, axis=1, keepdims=True)
        logsum = jnp.log(jnp.sum(jnp.exp(logits - largest), axis=1, keepdims=True)) + largest
        truth = lane == labels[rows, :]
        picked = jnp.sum(jnp.where(truth, logits, 0.0), axis=1, keepdims=True)
        loss += jnp.sum(logsum - picked, axis=0, keepdims=True)
        gap = (jnp.exp(logits - logsum) - jnp.where(truth, 1.0, 0.0)) * (1.0 / nodes)
        upstream[rows, :] = gap.astype(jnp.bfloat16)
        upstream_turned[:, rows] = gap.astype(jnp.bfloat16).T
    loss = loss * (1.0 / nodes)
    high = loss.astype(jnp.bfloat16).astype(jnp.float32)
    middle = (loss - high).astype(jnp.bfloat16).astype(jnp.float32)
    low = loss - high - middle
    half = SIDE * WIDTH
    for offset, out in ((1, sent), (0, own)):
        part = lax.rem(core[0] + offset, 2)
        for start in range(0, half, step):
            columns = pl.ds(pl.multiple_of(part * half + start, step), step)
            place = slice(start, start + step)
            second = jnp.dot(
                upstream_turned[: ROWS - features, :],
                smooth[:, columns],
                preferred_element_type=jnp.float32,
            )
            if start == 0:
                row = lax.broadcasted_iota(jnp.int32, second.shape, 0)
                lane = lax.broadcasted_iota(jnp.int32, second.shape, 1)
                here = (row == LOSS_ROW - features) & (part == 0)
                second += jnp.where(here & (lane == 0), high, 0.0)
                second += jnp.where(here & (lane == 1), middle, 0.0)
                second += jnp.where(here & (lane == 2), low, 0.0)
            out[features:, place] = second.astype(out.dtype)
            back = jnp.dot(
                upstream[...], layer_two[:, columns], preferred_element_type=jnp.float32
            ).astype(jnp.bfloat16)
            back = jnp.dot(turned[...], back, preferred_element_type=jnp.float32)
            back = (slope[:, columns] * back).astype(jnp.bfloat16)
            out[:features, place] = jnp.dot(
                mixed_turned[...], back, preferred_element_type=jnp.float32
            ).astype(out.dtype)


def on_device(
    features,
    source_part,
    source_row,
    adj_tiles,
    tile_row,
    tile_col,
    tile_count,
    labels,
    layer_one,
    layer_two,
):
    devices = lax.axis_size(AXES)
    nodes = source_part.shape[0]
    width, hidden = layer_one.shape
    classes = layer_two.shape[1]
    capacity = max(2, 2 * nodes // devices)
    slots = devices * capacity
    bf = jnp.bfloat16
    requests, position = call(
        number_requests,
        [
            jax.ShapeDtypeStruct((devices, capacity), jnp.int32),
            jax.ShapeDtypeStruct((1, nodes), jnp.int32),
        ],
        0,
        2,
    )(source_part.reshape(1, nodes), source_row.reshape(1, nodes))
    found = features[lax.all_to_all(requests, AXES, split_axis=0, concat_axis=0, tiled=True)]
    arrived = lax.all_to_all(found, AXES, split_axis=0, concat_axis=0, tiled=True)
    dense, turned, moved = call(
        build_spread,
        [
            jax.ShapeDtypeStruct((nodes, nodes), bf),
            jax.ShapeDtypeStruct((nodes, nodes), bf),
            jax.ShapeDtypeStruct((nodes, slots), bf),
        ],
        3,
        2,
        cost=pl.CostEstimate(
            flops=2 * nodes * nodes * slots, bytes_accessed=12 << 20, transcendentals=0
        ),
    )(tile_row, tile_col, tile_count, adj_tiles, position)
    padded = jnp.pad(layer_two.T, ((0, 256 - classes), (0, 0)))
    core = lax.rem(lax.axis_index("store"), 2).astype(jnp.int32).reshape(1)
    half = SIDE * WIDTH
    vmem = pl.BlockSpec(memory_space=pltpu.VMEM)
    sent, own = pl.pallas_call(
        partial(train, classes=classes),
        out_shape=[
            jax.ShapeDtypeStruct((ROWS, half), bf),
            jax.ShapeDtypeStruct((ROWS, half), jnp.float32),
        ],
        in_specs=[pl.BlockSpec(memory_space=pltpu.SMEM)] + [vmem] * 7,
        out_specs=[vmem] * 2,
        scratch_shapes=[
            pltpu.VMEM((width, nodes), bf),
            pltpu.VMEM((nodes, hidden), jnp.float32),
            pltpu.VMEM((nodes, hidden), bf),
            pltpu.VMEM((nodes, hidden), bf),
            pltpu.VMEM((nodes, 256), bf),
            pltpu.VMEM((256, nodes), bf),
        ],
        compiler_params=pltpu.CompilerParams(vmem_limit_bytes=56 << 20),
        cost_estimate=pl.CostEstimate(
            flops=12 * nodes * nodes * hidden, bytes_accessed=16 << 20, transcendentals=nodes * hidden
        ),
    )(
        core,
        arrived.reshape(slots, width),
        moved,
        dense,
        turned,
        layer_one,
        padded,
        labels.reshape(nodes, 1),
    )
    grad_one, grad_two, loss = sum_over_devices(sent, own, width, classes)
    return (grad_one, grad_two.T, loss.reshape(()))


def solution(mesh):
    return jax.shard_map(
        on_device,
        mesh=mesh,
        in_specs=(
            P(("store", "batch"), None),
            P(("store", "batch")),
            P(("store", "batch")),
            P(("store", "batch"), None, None),
            P(("store", "batch")),
            P(("store", "batch")),
            P(("store", "batch")),
            P(("store", "batch")),
            P(),
            P(),
        ),
        out_specs=(P(), P(), P()),
        check_vma=False,
    )
```

```python
from functools import partial

import jax
import jax.numpy as jnp
from jax import lax
from jax.experimental import pallas as pl
from jax.experimental.pallas import tpu as pltpu
from jax.sharding import PartitionSpec as P

AXES = ("store", "batch")
SIDE = 4
WIDTH = 128
LOSS_ROW = 921
ROWS = 928


def flat(x, y, z, core):
    return ((x * SIDE + z) * 2 + core) * SIDE + y


def shift_pairs(axes, offset):
    pairs = []
    for x in range(SIDE):
        for y in range(SIDE):
            for z in range(SIDE):
                for core in range(2):
                    place = [x, y, z]
                    place[axes[core]] = (place[axes[core]] + offset) % SIDE
                    pairs.append((flat(x, y, z, core), flat(*place, core)))
    return pairs


def swap_pairs():
    return [
        (flat(x, y, z, core), flat(x, y, z, 1 - core))
        for x in range(SIDE)
        for y in range(SIDE)
        for z in range(SIDE)
        for core in range(2)
    ]


FIRST, SECOND, THIRD = (0, 1), (1, 2), (2, 0)


def split_loss(total):
    tail = total[ROWS - 8 :, :]
    row = lax.broadcasted_iota(jnp.int32, tail.shape, 0)
    lane = lax.broadcasted_iota(jnp.int32, tail.shape, 1)
    here = row == LOSS_ROW - (ROWS - 8)
    loss = jnp.sum(jnp.where(here & (lane < 3), tail, 0.0), axis=1, keepdims=True)
    high = loss.astype(jnp.bfloat16).astype(jnp.float32)
    middle = (loss - high).astype(jnp.bfloat16).astype(jnp.float32)
    low = (loss - high - middle).astype(jnp.bfloat16).astype(jnp.float32)
    parts = jnp.where(lane == 0, high, jnp.where(lane == 1, middle, jnp.where(lane == 2, low, 0.0)))
    return jnp.where(here, parts, tail)


def store_total(out, columns, total):
    out[: ROWS - 16, columns] = total[: ROWS - 16].astype(jnp.bfloat16)
    last = jnp.concatenate([total[ROWS - 16 : ROWS - 8], split_loss(total)], axis=0)
    out[ROWS - 16 :, columns] = last.astype(jnp.bfloat16)


def first_add(place, own, arrived, keep, one, two, three):
    for offset, out in ((1, one), (2, two), (3, three), (0, keep)):
        block = lax.rem(place[0] + offset, SIDE)
        columns = pl.ds(pl.multiple_of(block * WIDTH, WIDTH), WIDTH)
        total = own[:, columns].astype(jnp.float32) + arrived[:, columns].astype(jnp.float32)
        store_total(out, slice(None), total)


def four_add(own, one, two, three, out):
    total = (own[...].astype(jnp.float32) + two[...].astype(jnp.float32)) + (
        one[...].astype(jnp.float32) + three[...].astype(jnp.float32)
    )
    store_total(out, slice(None), total)


def place_blocks(place, own, one, two, three, out):
    for offset, block in ((0, own), (1, one), (2, two), (3, three)):
        at = lax.rem(place[0] + SIDE - offset, SIDE)
        out[:, pl.ds(pl.multiple_of(at * WIDTH, WIDTH), WIDTH)] = block[...]


def write_half(at, part, one_far, two_far, one, two, leaving):
    half = part.shape[1]
    features = one.shape[0]
    classes = two.shape[0]
    columns = pl.ds(pl.multiple_of(at * half, half), half)
    one[...] = part[:features, :].astype(jnp.float32)
    first = pltpu.make_async_copy(one, one_far.at[:, columns], leaving.at[0])
    first.start()
    two[...] = part[features:, :].astype(jnp.float32)[:classes]
    second = pltpu.make_async_copy(two, two_far.at[:, columns], leaving.at[1])
    second.start()
    return first, second


def read_loss(part):
    tail = part[ROWS - 16 :, :WIDTH].astype(jnp.float32)
    row = lax.broadcasted_iota(jnp.int32, tail.shape, 0)
    lane = lax.broadcasted_iota(jnp.int32, tail.shape, 1)
    mine = (row == LOSS_ROW - (ROWS - 16)) & (lane < 3)
    return jnp.sum(jnp.sum(jnp.where(mine, tail, 0.0), axis=1, keepdims=True), axis=0, keepdims=True)


def write_own(core, own, one_far, two_far, one, two, leaving):
    for copy in write_half(core[0], own, one_far, two_far, one, two, leaving):
        copy.wait()


def write_other(core, own, other, one_in, two_in, one_far, two_far, loss, one, two, leaving):
    copies = write_half(1 - core[0], other, one_far, two_far, one, two, leaving)
    loss[...] = jnp.where(core[0] == 0, read_loss(own), read_loss(other))
    for copy in copies:
        copy.wait()


def call(kernel, outs, scalars=0, arrays=0, limit=16 << 20, cost=None, scratch=()):
    vmem = pl.BlockSpec(memory_space=pltpu.VMEM)
    smem = pl.BlockSpec(memory_space=pltpu.SMEM)
    return pl.pallas_call(
        kernel,
        out_shape=outs,
        in_specs=[smem] * scalars + [vmem] * arrays,
        out_specs=jax.tree.map(lambda _: vmem, outs),
        scratch_shapes=list(scratch),
        compiler_params=pltpu.CompilerParams(vmem_limit_bytes=limit),
        cost_estimate=cost,
    )


def sum_over_devices(sent, own, features, classes):
    store, batch = lax.axis_index("store"), lax.axis_index("batch")
    core = lax.rem(store, 2)
    place = jnp.where(core == 0, store // (2 * SIDE), batch).astype(jnp.int32).reshape(1)
    core = core.astype(jnp.int32).reshape(1)
    bf = jnp.bfloat16
    block = jax.ShapeDtypeStruct((ROWS, WIDTH), bf)
    arrived = lax.ppermute(sent, AXES, swap_pairs())
    keep, *parts = call(first_add, [block] * 4, 1, 2)(place, own, arrived)
    got = [lax.ppermute(part, AXES, shift_pairs(FIRST, k + 1)) for k, part in enumerate(parts)]
    total = call(four_add, block, 0, 4)(keep, *got)
    for axes in (SECOND, THIRD):
        got = [lax.ppermute(total, AXES, shift_pairs(axes, k)) for k in (1, 2, 3)]
        total = call(four_add, block, 0, 4)(total, *got)
    got = [lax.ppermute(total, AXES, shift_pairs(FIRST, k)) for k in (1, 2, 3)]
    strip = call(place_blocks, jax.ShapeDtypeStruct((ROWS, SIDE * WIDTH), bf), 1, 4)(
        place, total, *got
    )
    other = lax.ppermute(strip, AXES, swap_pairs())
    half = SIDE * WIDTH
    grads = [
        jax.ShapeDtypeStruct((features, 2 * half), jnp.float32),
        jax.ShapeDtypeStruct((classes, 2 * half), jnp.float32),
    ]
    anywhere = pl.BlockSpec(memory_space=pl.ANY)
    vmem = pl.BlockSpec(memory_space=pltpu.VMEM)
    smem = pl.BlockSpec(memory_space=pltpu.SMEM)
    scratch = [
        pltpu.VMEM((features, half), jnp.float32),
        pltpu.VMEM((classes, half), jnp.float32),
        pltpu.SemaphoreType.DMA((2,)),
    ]
    params = pltpu.CompilerParams(vmem_limit_bytes=16 << 20)
    grad_one, grad_two = pl.pallas_call(
        write_own,
        out_shape=grads,
        in_specs=[smem, vmem],
        out_specs=[anywhere] * 2,
        scratch_shapes=scratch,
        compiler_params=params,
    )(core, strip)
    return pl.pallas_call(
        write_other,
        out_shape=[*grads, jax.ShapeDtypeStruct((1, 1), jnp.float32)],
        in_specs=[smem, vmem, vmem, anywhere, anywhere],
        out_specs=[anywhere, anywhere, vmem],
        scratch_shapes=scratch,
        input_output_aliases={3: 0, 4: 1},
        compiler_params=params,
    )(core, strip, other, grad_one, grad_two)


def number_requests(parts, rows, requests, position):
    devices, capacity = requests.shape
    nodes = parts.shape[1]
    piece = 128
    owner = lax.broadcasted_iota(jnp.int32, (devices, nodes), 0)
    mine = jnp.where(owner == parts[...], 1.0, 0.0)
    line = lax.broadcasted_iota(jnp.int32, (piece, piece), 0)
    lane = lax.broadcasted_iota(jnp.int32, (piece, piece), 1)
    earlier = jnp.where(line < lane, 1.0, 0.0).astype(jnp.bfloat16)
    seen = jnp.zeros((devices, 1), jnp.float32)
    slots = []
    for start in range(0, nodes, piece):
        here = mine[:, start : start + piece]
        rank = jnp.dot(here.astype(jnp.bfloat16), earlier, preferred_element_type=jnp.float32)
        slots.append(jnp.sum(here * (rank + seen), axis=0, keepdims=True))
        seen = seen + jnp.sum(here, axis=1, keepdims=True)
    slot = jnp.concatenate(slots, axis=1).astype(jnp.int32)
    position[...] = parts[...] * capacity + slot
    placed = lax.broadcasted_iota(jnp.int32, (capacity, nodes), 0) == slot
    total = jnp.zeros((devices, capacity), jnp.float32)
    for scale, digit in ((64.0, lax.shift_right_logical(rows[...], 6)), (1.0, rows[...] & 63)):
        values = jnp.where(placed, digit.astype(jnp.float32), 0.0).astype(jnp.bfloat16)
        total += scale * lax.dot_general(
            mine.astype(jnp.bfloat16),
            values,
            (((1,), (1,)), ((), ())),
            preferred_element_type=jnp.float32,
        )
    requests[...] = total.astype(jnp.int32)


def fetch_rows(wanted, table, far, narrow, wide, some, out, arrival, leaving):
    stored, width = table.shape
    step = stored // arrival.shape[0]

    def load(block):
        rows = pl.ds(block * step, step)
        return pltpu.make_async_copy(table.at[rows, :], narrow.at[rows, :], arrival.at[block])

    for block in range(arrival.shape[0]):
        load(block).start()
    for block in range(arrival.shape[0]):
        load(block).wait()
        for start in range(block * step, (block + 1) * step, 128):
            rows = slice(start, start + 128)
            wide[rows, :] = narrow[rows, :].astype(jnp.float32)

    devices, capacity = wanted.shape
    owners = some.shape[0] // capacity

    def send(block):
        rows = pl.ds(pl.multiple_of(block * some.shape[0], some.shape[0]), some.shape[0])
        return pltpu.make_async_copy(out.at[rows, :], far.at[rows, :], leaving.at[block])

    @pl.loop(0, devices // owners)
    def _(block):
        for owner in range(owners):
            for slot in range(capacity):
                row = wanted[block * owners + owner, slot]
                some[pl.ds(owner * capacity + slot, 1), :] = wide[pl.ds(row, 1), :]
        rows = pl.ds(pl.multiple_of(block * some.shape[0], some.shape[0]), some.shape[0])
        out[rows, :] = some[...].astype(jnp.bfloat16)
        send(block).start()

    @pl.loop(0, devices // owners)
    def _(block):
        send(block).wait()


def build_spread(row, column, count, tiles, position, dense, turned, moved):
    nodes = dense.shape[0]
    tile = tiles.shape[1]
    dense[...] = jnp.zeros_like(dense)
    turned[...] = jnp.zeros_like(turned)

    @pl.loop(0, count[0])
    def _(t):
        at_row = pl.ds(pl.multiple_of(row[t] * tile, tile), tile)
        at_column = pl.ds(pl.multiple_of(column[t] * tile, tile), tile)
        values = tiles[t]
        dense[at_row, at_column] = values
        turned[at_column, at_row] = values.T

    width = 256

    @pl.loop(0, moved.shape[1] // width)
    def _(step):
        start = pl.multiple_of(step * width, width)
        slot = lax.broadcasted_iota(jnp.int32, (width, nodes), 0) + start
        chosen = jnp.where(slot == position[...], 1.0, 0.0).astype(jnp.bfloat16)
        moved[:, pl.ds(start, width)] = lax.dot_general(
            dense[...], chosen, (((1,), (1,)), ((), ())), preferred_element_type=jnp.float32
        ).astype(jnp.bfloat16)


def train(
    core,
    arrived_far,
    moved_far,
    dense_far,
    turned_far,
    one_far,
    two_far,
    labels_far,
    sent_far,
    own_far,
    arrived,
    moved,
    dense,
    turned,
    layer_one,
    layer_two,
    labels,
    sent,
    own,
    mixed_turned,
    slope,
    hidden,
    smooth,
    upstream,
    upstream_turned,
    arrival,
    leaving,
    *,
    classes,
):
    nodes = dense.shape[0]
    features = mixed_turned.shape[0]
    step = 256
    tiles = range(0, nodes, step)

    def load(index, far, near):
        return pltpu.make_async_copy(far, near, arrival.at[index])

    get_arrived = load(0, arrived_far, arrived)
    get_one = load(1, one_far, layer_one)
    get_dense = load(2, dense_far, dense)
    get_two = load(3, two_far, layer_two)
    get_labels = load(4, labels_far, labels)
    get_turned = load(5, turned_far, turned)
    get_moved = [
        load(6 + at, moved_far.at[pl.ds(start, step), :], moved.at[pl.ds(start, step), :])
        for at, start in enumerate(tiles)
    ]
    get_arrived.start()
    get_moved[0].start()
    get_one.start()
    get_arrived.wait()
    get_moved[0].wait()
    for copy in get_moved[1:]:
        copy.start()
    for at, start in enumerate(tiles):
        rows = slice(start, start + step)
        if at > 0:
            get_moved[at].wait()
        mixed = jnp.dot(moved[rows, :], arrived[...], preferred_element_type=jnp.float32).astype(
            jnp.bfloat16
        )
        mixed_turned[:, rows] = mixed.T
        if at == 0:
            get_one.wait()
            get_dense.start()
            get_two.start()
            get_labels.start()
            get_turned.start()
        before = jnp.dot(mixed, layer_one[...], preferred_element_type=jnp.float32)
        square = before * before
        rate = 0.7978845608028654
        bend = jnp.tanh(rate * before * (1.0 + 0.044715 * square))
        rise = 0.5 * (1.0 + bend)
        hidden[rows, :] = (before * rise).astype(jnp.bfloat16)
        slope[rows, :] = rise + 0.5 * before * (1.0 - bend * bend) * (
            rate + (3.0 * 0.044715 * rate) * square
        )
    get_dense.wait()
    get_two.wait()
    get_labels.wait()
    loss = jnp.zeros((1, 1), jnp.float32)
    for start in tiles:
        rows = slice(start, start + step)
        spread = jnp.dot(dense[rows, :], hidden[...], preferred_element_type=jnp.float32).astype(
            jnp.bfloat16
        )
        smooth[rows, :] = spread
        logits = lax.dot_general(
            spread, layer_two[...], (((1,), (1,)), ((), ())), preferred_element_type=jnp.float32
        )
        lane = lax.broadcasted_iota(jnp.int32, logits.shape, 1)
        logits = jnp.where(lane < classes, logits, -jnp.inf)
        largest = jnp.max(logits, axis=1, keepdims=True)
        logsum = jnp.log(jnp.sum(jnp.exp(logits - largest), axis=1, keepdims=True)) + largest
        truth = lane == labels[rows, :]
        picked = jnp.sum(jnp.where(truth, logits, 0.0), axis=1, keepdims=True)
        loss += jnp.sum(logsum - picked, axis=0, keepdims=True)
        gap = (jnp.exp(logits - logsum) - jnp.where(truth, 1.0, 0.0)) * (1.0 / nodes)
        upstream[rows, :] = gap.astype(jnp.bfloat16)
        upstream_turned[:, rows] = gap.astype(jnp.bfloat16).T
    loss = loss * (1.0 / nodes)
    high = loss.astype(jnp.bfloat16).astype(jnp.float32)
    middle = (loss - high).astype(jnp.bfloat16).astype(jnp.float32)
    low = loss - high - middle
    half = SIDE * WIDTH
    get_turned.wait()
    stores = []
    for offset, out, far in ((1, sent, sent_far), (0, own, own_far)):
        part = lax.rem(core[0] + offset, 2)
        columns = pl.ds(pl.multiple_of(part * half, half), half)
        second = jnp.dot(
            upstream_turned[: ROWS - features, :],
            smooth[:, columns],
            preferred_element_type=jnp.float32,
        )
        row = lax.broadcasted_iota(jnp.int32, second.shape, 0)
        lane = lax.broadcasted_iota(jnp.int32, second.shape, 1)
        here = (row == LOSS_ROW - features) & (part == 0)
        second += jnp.where(here & (lane == 0), high, 0.0)
        second += jnp.where(here & (lane == 1), middle, 0.0)
        second += jnp.where(here & (lane == 2), low, 0.0)
        out[features:, :] = second.astype(out.dtype)
        back = jnp.dot(
            upstream[...], layer_two[:, columns], preferred_element_type=jnp.float32
        ).astype(jnp.bfloat16)
        back = jnp.dot(turned[...], back, preferred_element_type=jnp.float32)
        back = (slope[:, columns] * back).astype(jnp.bfloat16)
        out[:features, :] = jnp.dot(
            mixed_turned[...], back, preferred_element_type=jnp.float32
        ).astype(out.dtype)
        stores.append(pltpu.make_async_copy(out, far, leaving.at[len(stores)]))
        stores[-1].start()
    for copy in stores:
        copy.wait()


def on_device(
    features,
    source_part,
    source_row,
    adj_tiles,
    tile_row,
    tile_col,
    tile_count,
    labels,
    layer_one,
    layer_two,
):
    devices = lax.axis_size(AXES)
    nodes = source_part.shape[0]
    width, hidden = layer_one.shape
    classes = layer_two.shape[1]
    capacity = max(2, 2 * nodes // devices)
    slots = devices * capacity
    bf = jnp.bfloat16
    requests, position = call(
        number_requests,
        [
            jax.ShapeDtypeStruct((devices, capacity), jnp.int32),
            jax.ShapeDtypeStruct((1, nodes), jnp.int32),
        ],
        0,
        2,
        limit=56 << 20,
    )(source_part.reshape(1, nodes), source_row.reshape(1, nodes))
    wanted = lax.all_to_all(requests, AXES, split_axis=0, concat_axis=0, tiled=True)
    anywhere = pl.BlockSpec(memory_space=pl.ANY)
    vmem = pl.BlockSpec(memory_space=pltpu.VMEM)
    smem = pl.BlockSpec(memory_space=pltpu.SMEM)
    found = pl.pallas_call(
        fetch_rows,
        out_shape=jax.ShapeDtypeStruct((slots, width), bf),
        in_specs=[smem, anywhere],
        out_specs=anywhere,
        scratch_shapes=[
            pltpu.VMEM(features.shape, bf),
            pltpu.VMEM(features.shape, jnp.float32),
            pltpu.VMEM((64, width), jnp.float32),
            pltpu.VMEM((slots, width), bf),
            pltpu.SemaphoreType.DMA((8,)),
            pltpu.SemaphoreType.DMA((slots // 64,)),
        ],
        compiler_params=pltpu.CompilerParams(vmem_limit_bytes=56 << 20),
    )(wanted, features)
    arrived = lax.all_to_all(found, AXES, split_axis=0, concat_axis=0, tiled=True)
    dense, turned, moved = call(
        build_spread,
        [
            jax.ShapeDtypeStruct((nodes, nodes), bf),
            jax.ShapeDtypeStruct((nodes, nodes), bf),
            jax.ShapeDtypeStruct((nodes, slots), bf),
        ],
        3,
        2,
        cost=pl.CostEstimate(
            flops=2 * nodes * nodes * slots, bytes_accessed=12 << 20, transcendentals=0
        ),
    )(tile_row, tile_col, tile_count, adj_tiles, position)
    padded = jnp.pad(layer_two.T, ((0, 256 - classes), (0, 0)))
    core = lax.rem(lax.axis_index("store"), 2).astype(jnp.int32).reshape(1)
    half = SIDE * WIDTH
    sent, own = pl.pallas_call(
        partial(train, classes=classes),
        out_shape=[
            jax.ShapeDtypeStruct((ROWS, half), bf),
            jax.ShapeDtypeStruct((ROWS, half), bf),
        ],
        in_specs=[smem] + [anywhere] * 7,
        out_specs=[anywhere] * 2,
        scratch_shapes=[
            pltpu.VMEM((slots, width), bf),
            pltpu.VMEM((nodes, slots), bf),
            pltpu.VMEM((nodes, nodes), bf),
            pltpu.VMEM((nodes, nodes), bf),
            pltpu.VMEM((width, hidden), bf),
            pltpu.VMEM((256, hidden), bf),
            pltpu.VMEM((nodes, 1), jnp.int32),
            pltpu.VMEM((ROWS, half), bf),
            pltpu.VMEM((ROWS, half), bf),
            pltpu.VMEM((width, nodes), bf),
            pltpu.VMEM((nodes, hidden), jnp.float32),
            pltpu.VMEM((nodes, hidden), bf),
            pltpu.VMEM((nodes, hidden), bf),
            pltpu.VMEM((nodes, 256), bf),
            pltpu.VMEM((256, nodes), bf),
            pltpu.SemaphoreType.DMA((10,)),
            pltpu.SemaphoreType.DMA((2,)),
        ],
        compiler_params=pltpu.CompilerParams(vmem_limit_bytes=56 << 20),
        cost_estimate=pl.CostEstimate(
            flops=12 * nodes * nodes * hidden, bytes_accessed=16 << 20, transcendentals=nodes * hidden
        ),
    )(
        core,
        arrived.reshape(slots, width),
        moved,
        dense,
        turned,
        layer_one,
        padded,
        labels.reshape(nodes, 1),
    )
    grad_one, grad_two, loss = sum_over_devices(sent, own, width, classes)
    return (grad_one, grad_two.T, loss.reshape(()))


def solution(mesh):
    return jax.shard_map(
        on_device,
        mesh=mesh,
        in_specs=(
            P(("store", "batch"), None),
            P(("store", "batch")),
            P(("store", "batch")),
            P(("store", "batch"), None, None),
            P(("store", "batch")),
            P(("store", "batch")),
            P(("store", "batch")),
            P(("store", "batch")),
            P(),
            P(),
        ),
        out_specs=(P(), P(), P()),
        check_vma=False,
    )
```

```python
from functools import partial

import jax
import jax.numpy as jnp
from jax import lax
from jax.experimental import pallas as pl
from jax.experimental.pallas import tpu as pltpu
from jax.sharding import PartitionSpec as P

AXES = ("store", "batch")
SIDE = 4
WIDTH = 128
LOSS_ROW = 921
ROWS = 928


def flat(x, y, z, core):
    return ((x * SIDE + z) * 2 + core) * SIDE + y


def shift_pairs(axes, offset):
    pairs = []
    for x in range(SIDE):
        for y in range(SIDE):
            for z in range(SIDE):
                for core in range(2):
                    place = [x, y, z]
                    place[axes[core]] = (place[axes[core]] + offset) % SIDE
                    pairs.append((flat(x, y, z, core), flat(*place, core)))
    return pairs


def swap_pairs():
    return [
        (flat(x, y, z, core), flat(x, y, z, 1 - core))
        for x in range(SIDE)
        for y in range(SIDE)
        for z in range(SIDE)
        for core in range(2)
    ]


FIRST, SECOND, THIRD = (0, 1), (1, 2), (2, 0)


def split_loss(total):
    tail = total[ROWS - 8 :, :]
    row = lax.broadcasted_iota(jnp.int32, tail.shape, 0)
    lane = lax.broadcasted_iota(jnp.int32, tail.shape, 1)
    here = row == LOSS_ROW - (ROWS - 8)
    loss = jnp.sum(jnp.where(here & (lane < 3), tail, 0.0), axis=1, keepdims=True)
    high = loss.astype(jnp.bfloat16).astype(jnp.float32)
    middle = (loss - high).astype(jnp.bfloat16).astype(jnp.float32)
    low = (loss - high - middle).astype(jnp.bfloat16).astype(jnp.float32)
    parts = jnp.where(lane == 0, high, jnp.where(lane == 1, middle, jnp.where(lane == 2, low, 0.0)))
    return jnp.where(here, parts, tail)


def store_total(out, columns, total):
    out[: ROWS - 16, columns] = total[: ROWS - 16].astype(jnp.bfloat16)
    last = jnp.concatenate([total[ROWS - 16 : ROWS - 8], split_loss(total)], axis=0)
    out[ROWS - 16 :, columns] = last.astype(jnp.bfloat16)


def first_add(place, own, arrived, keep, one, two, three):
    for offset, out in ((1, one), (2, two), (3, three), (0, keep)):
        block = lax.rem(place[0] + offset, SIDE)
        columns = pl.ds(pl.multiple_of(block * WIDTH, WIDTH), WIDTH)
        total = own[:, columns].astype(jnp.float32) + arrived[:, columns].astype(jnp.float32)
        store_total(out, slice(None), total)


def four_add(own, one, two, three, out):
    total = (own[...].astype(jnp.float32) + two[...].astype(jnp.float32)) + (
        one[...].astype(jnp.float32) + three[...].astype(jnp.float32)
    )
    store_total(out, slice(None), total)


def place_blocks(place, own, one, two, three, out):
    for offset, block in ((0, own), (1, one), (2, two), (3, three)):
        at = lax.rem(place[0] + SIDE - offset, SIDE)
        out[:, pl.ds(pl.multiple_of(at * WIDTH, WIDTH), WIDTH)] = block[...]


def write_half(at, part, one_far, two_far, one, two, leaving):
    half = part.shape[1]
    features = one.shape[0]
    classes = two.shape[0]
    columns = pl.ds(pl.multiple_of(at * half, half), half)
    two[...] = part[features:, :].astype(jnp.float32)[:classes]
    copies = [pltpu.make_async_copy(two, two_far.at[:, columns], leaving.at[0])]
    copies[0].start()
    step = features // 4
    for index in range(4):
        rows = slice(index * step, (index + 1) * step)
        one[rows, :] = part[rows, :].astype(jnp.float32)
        lines = pl.ds(index * step, step)
        copies.append(
            pltpu.make_async_copy(
                one.at[lines, :], one_far.at[lines, columns], leaving.at[index + 1]
            )
        )
        copies[-1].start()
    return copies


def read_loss(part):
    tail = part[ROWS - 16 :, :WIDTH].astype(jnp.float32)
    row = lax.broadcasted_iota(jnp.int32, tail.shape, 0)
    lane = lax.broadcasted_iota(jnp.int32, tail.shape, 1)
    mine = (row == LOSS_ROW - (ROWS - 16)) & (lane < 3)
    return jnp.sum(jnp.sum(jnp.where(mine, tail, 0.0), axis=1, keepdims=True), axis=0, keepdims=True)


def write_own(core, own, one_far, two_far, one, two, leaving):
    for copy in write_half(core[0], own, one_far, two_far, one, two, leaving):
        copy.wait()


def write_other(core, own, other, one_in, two_in, one_far, two_far, loss, one, two, leaving):
    copies = write_half(1 - core[0], other, one_far, two_far, one, two, leaving)
    loss[...] = jnp.where(core[0] == 0, read_loss(own), read_loss(other))
    for copy in copies:
        copy.wait()


def call(kernel, outs, scalars=0, arrays=0, limit=16 << 20, cost=None, scratch=()):
    vmem = pl.BlockSpec(memory_space=pltpu.VMEM)
    smem = pl.BlockSpec(memory_space=pltpu.SMEM)
    return pl.pallas_call(
        kernel,
        out_shape=outs,
        in_specs=[smem] * scalars + [vmem] * arrays,
        out_specs=jax.tree.map(lambda _: vmem, outs),
        scratch_shapes=list(scratch),
        compiler_params=pltpu.CompilerParams(vmem_limit_bytes=limit),
        cost_estimate=cost,
    )


def sum_over_devices(sent, own, features, classes):
    store, batch = lax.axis_index("store"), lax.axis_index("batch")
    core = lax.rem(store, 2)
    place = jnp.where(core == 0, store // (2 * SIDE), batch).astype(jnp.int32).reshape(1)
    core = core.astype(jnp.int32).reshape(1)
    bf = jnp.bfloat16
    block = jax.ShapeDtypeStruct((ROWS, WIDTH), bf)
    arrived = lax.ppermute(sent, AXES, swap_pairs())
    keep, *parts = call(first_add, [block] * 4, 1, 2)(place, own, arrived)
    got = [lax.ppermute(part, AXES, shift_pairs(FIRST, k + 1)) for k, part in enumerate(parts)]
    total = call(four_add, block, 0, 4)(keep, *got)
    for axes in (SECOND, THIRD):
        got = [lax.ppermute(total, AXES, shift_pairs(axes, k)) for k in (1, 2, 3)]
        total = call(four_add, block, 0, 4)(total, *got)
    got = [lax.ppermute(total, AXES, shift_pairs(FIRST, k)) for k in (1, 2, 3)]
    strip = call(place_blocks, jax.ShapeDtypeStruct((ROWS, SIDE * WIDTH), bf), 1, 4)(
        place, total, *got
    )
    other = lax.ppermute(strip, AXES, swap_pairs())
    half = SIDE * WIDTH
    grads = [
        jax.ShapeDtypeStruct((features, 2 * half), jnp.float32),
        jax.ShapeDtypeStruct((classes, 2 * half), jnp.float32),
    ]
    anywhere = pl.BlockSpec(memory_space=pl.ANY)
    vmem = pl.BlockSpec(memory_space=pltpu.VMEM)
    smem = pl.BlockSpec(memory_space=pltpu.SMEM)
    scratch = [
        pltpu.VMEM((features, half), jnp.float32),
        pltpu.VMEM((classes, half), jnp.float32),
        pltpu.SemaphoreType.DMA((5,)),
    ]
    params = pltpu.CompilerParams(vmem_limit_bytes=16 << 20)
    grad_one, grad_two = pl.pallas_call(
        write_own,
        out_shape=grads,
        in_specs=[smem, vmem],
        out_specs=[anywhere] * 2,
        scratch_shapes=scratch,
        compiler_params=params,
    )(core, strip)
    return pl.pallas_call(
        write_other,
        out_shape=[*grads, jax.ShapeDtypeStruct((1, 1), jnp.float32)],
        in_specs=[smem, vmem, vmem, anywhere, anywhere],
        out_specs=[anywhere, anywhere, vmem],
        scratch_shapes=scratch,
        input_output_aliases={3: 0, 4: 1},
        compiler_params=params,
    )(core, strip, other, grad_one, grad_two)


def number_requests(parts, rows, requests, position):
    devices, capacity = requests.shape
    nodes = parts.shape[1]
    piece = 128
    owner = lax.broadcasted_iota(jnp.int32, (devices, nodes), 0)
    mine = jnp.where(owner == parts[...], 1.0, 0.0)
    line = lax.broadcasted_iota(jnp.int32, (piece, piece), 0)
    lane = lax.broadcasted_iota(jnp.int32, (piece, piece), 1)
    earlier = jnp.where(line < lane, 1.0, 0.0).astype(jnp.bfloat16)
    seen = jnp.zeros((devices, 1), jnp.float32)
    slots = []
    for start in range(0, nodes, piece):
        here = mine[:, start : start + piece]
        rank = jnp.dot(here.astype(jnp.bfloat16), earlier, preferred_element_type=jnp.float32)
        slots.append(jnp.sum(here * (rank + seen), axis=0, keepdims=True))
        seen = seen + jnp.sum(here, axis=1, keepdims=True)
    slot = jnp.concatenate(slots, axis=1).astype(jnp.int32)
    position[...] = parts[...] * capacity + slot
    placed = lax.broadcasted_iota(jnp.int32, (capacity, nodes), 0) == slot
    total = jnp.zeros((devices, capacity), jnp.float32)
    for scale, digit in ((64.0, lax.shift_right_logical(rows[...], 6)), (1.0, rows[...] & 63)):
        values = jnp.where(placed, digit.astype(jnp.float32), 0.0).astype(jnp.bfloat16)
        total += scale * lax.dot_general(
            mine.astype(jnp.bfloat16),
            values,
            (((1,), (1,)), ((), ())),
            preferred_element_type=jnp.float32,
        )
    requests[...] = total.astype(jnp.int32)


def fetch_rows(wanted_far, table, far, wanted, narrow, wide, some, out, listed, arrival, leaving):
    stored, width = table.shape
    step = stored // arrival.shape[0]

    def load(block):
        rows = pl.ds(block * step, step)
        return pltpu.make_async_copy(table.at[rows, :], narrow.at[rows, :], arrival.at[block])

    listing = pltpu.make_async_copy(wanted_far, wanted, listed)
    listing.start()
    for block in range(arrival.shape[0]):
        load(block).start()
    for block in range(arrival.shape[0]):
        load(block).wait()
        for start in range(block * step, (block + 1) * step, 128):
            rows = slice(start, start + 128)
            wide[rows, :] = narrow[rows, :].astype(jnp.float32)

    listing.wait()
    devices, capacity = wanted.shape
    owners = some.shape[0] // capacity

    def send(block):
        rows = pl.ds(pl.multiple_of(block * some.shape[0], some.shape[0]), some.shape[0])
        return pltpu.make_async_copy(out.at[rows, :], far.at[rows, :], leaving.at[block])

    @pl.loop(0, devices // owners)
    def _(block):
        for owner in range(owners):
            for slot in range(capacity):
                row = wanted[block * owners + owner, slot]
                some[pl.ds(owner * capacity + slot, 1), :] = wide[pl.ds(row, 1), :]
        rows = pl.ds(pl.multiple_of(block * some.shape[0], some.shape[0]), some.shape[0])
        out[rows, :] = some[...].astype(jnp.bfloat16)
        send(block).start()

    @pl.loop(0, devices // owners)
    def _(block):
        send(block).wait()


def build_spread(row, column, count, tiles, position, dense, turned, moved):
    nodes = dense.shape[0]
    tile = tiles.shape[1]
    dense[...] = jnp.zeros_like(dense)
    turned[...] = jnp.zeros_like(turned)

    @pl.loop(0, count[0])
    def _(t):
        at_row = pl.ds(pl.multiple_of(row[t] * tile, tile), tile)
        at_column = pl.ds(pl.multiple_of(column[t] * tile, tile), tile)
        values = tiles[t]
        dense[at_row, at_column] = values
        turned[at_column, at_row] = values.T

    width = 256

    @pl.loop(0, moved.shape[1] // width)
    def _(step):
        start = pl.multiple_of(step * width, width)
        slot = lax.broadcasted_iota(jnp.int32, (width, nodes), 0) + start
        chosen = jnp.where(slot == position[...], 1.0, 0.0).astype(jnp.bfloat16)
        moved[:, pl.ds(start, width)] = lax.dot_general(
            dense[...], chosen, (((1,), (1,)), ((), ())), preferred_element_type=jnp.float32
        ).astype(jnp.bfloat16)


def train(
    core,
    arrived_far,
    moved_far,
    dense_far,
    turned_far,
    one_far,
    two_far,
    labels_far,
    sent_far,
    own_far,
    arrived,
    moved,
    dense,
    turned,
    layer_one,
    layer_two,
    labels,
    sent,
    own,
    mixed_turned,
    slope,
    hidden,
    smooth,
    upstream,
    upstream_turned,
    arrival,
    leaving,
    *,
    classes,
):
    nodes = dense.shape[0]
    features = mixed_turned.shape[0]
    step = 256
    tiles = range(0, nodes, step)

    def load(index, far, near):
        return pltpu.make_async_copy(far, near, arrival.at[index])

    part = arrived.shape[0] // SIDE
    get_arrived = [
        load(at, arrived_far.at[pl.ds(at * part, part), :], arrived.at[pl.ds(at * part, part), :])
        for at in range(SIDE)
    ]
    get_one = load(4, one_far, layer_one)
    get_dense = load(5, dense_far, dense)
    get_two = load(6, two_far, layer_two)
    get_labels = load(7, labels_far, labels)
    get_turned = load(8, turned_far, turned)
    get_moved = [
        load(9 + at, moved_far.at[pl.ds(start, step), :], moved.at[pl.ds(start, step), :])
        for at, start in enumerate(tiles)
    ]
    get_moved[0].start()
    for copy in get_arrived:
        copy.start()
    get_one.start()
    get_moved[0].wait()
    for at, start in enumerate(tiles):
        rows = slice(start, start + step)
        if at > 0:
            get_moved[at].wait()
            mixed = jnp.dot(moved[rows, :], arrived[...], preferred_element_type=jnp.float32)
        else:
            mixed = 0.0
            for index, copy in enumerate(get_arrived):
                copy.wait()
                slots = slice(index * part, (index + 1) * part)
                mixed += jnp.dot(
                    moved[rows, slots], arrived[slots, :], preferred_element_type=jnp.float32
                )
            for copy in get_moved[1:]:
                copy.start()
        mixed = mixed.astype(jnp.bfloat16)
        mixed_turned[:, rows] = mixed.T
        if at == 0:
            get_one.wait()
            get_dense.start()
            get_two.start()
            get_labels.start()
            get_turned.start()
        before = jnp.dot(mixed, layer_one[...], preferred_element_type=jnp.float32)
        square = before * before
        rate = 0.7978845608028654
        bend = jnp.tanh(rate * before * (1.0 + 0.044715 * square))
        rise = 0.5 * (1.0 + bend)
        hidden[rows, :] = (before * rise).astype(jnp.bfloat16)
        slope[rows, :] = rise + 0.5 * before * (1.0 - bend * bend) * (
            rate + (3.0 * 0.044715 * rate) * square
        )
    get_dense.wait()
    get_two.wait()
    get_labels.wait()
    loss = jnp.zeros((1, 1), jnp.float32)
    for start in tiles:
        rows = slice(start, start + step)
        spread = jnp.dot(dense[rows, :], hidden[...], preferred_element_type=jnp.float32).astype(
            jnp.bfloat16
        )
        smooth[rows, :] = spread
        logits = lax.dot_general(
            spread, layer_two[...], (((1,), (1,)), ((), ())), preferred_element_type=jnp.float32
        )
        lane = lax.broadcasted_iota(jnp.int32, logits.shape, 1)
        logits = jnp.where(lane < classes, logits, -jnp.inf)
        largest = jnp.max(logits, axis=1, keepdims=True)
        logsum = jnp.log(jnp.sum(jnp.exp(logits - largest), axis=1, keepdims=True)) + largest
        truth = lane == labels[rows, :]
        picked = jnp.sum(jnp.where(truth, logits, 0.0), axis=1, keepdims=True)
        loss += jnp.sum(logsum - picked, axis=0, keepdims=True)
        gap = (jnp.exp(logits - logsum) - jnp.where(truth, 1.0, 0.0)) * (1.0 / nodes)
        upstream[rows, :] = gap.astype(jnp.bfloat16)
        upstream_turned[:, rows] = gap.astype(jnp.bfloat16).T
    loss = loss * (1.0 / nodes)
    high = loss.astype(jnp.bfloat16).astype(jnp.float32)
    middle = (loss - high).astype(jnp.bfloat16).astype(jnp.float32)
    low = loss - high - middle
    half = SIDE * WIDTH
    get_turned.wait()
    stores = []
    for offset, out, far in ((1, sent, sent_far), (0, own, own_far)):
        part = lax.rem(core[0] + offset, 2)
        columns = pl.ds(pl.multiple_of(part * half, half), half)
        second = jnp.dot(
            upstream_turned[: ROWS - features, :],
            smooth[:, columns],
            preferred_element_type=jnp.float32,
        )
        row = lax.broadcasted_iota(jnp.int32, second.shape, 0)
        lane = lax.broadcasted_iota(jnp.int32, second.shape, 1)
        here = (row == LOSS_ROW - features) & (part == 0)
        second += jnp.where(here & (lane == 0), high, 0.0)
        second += jnp.where(here & (lane == 1), middle, 0.0)
        second += jnp.where(here & (lane == 2), low, 0.0)
        out[features:, :] = second.astype(out.dtype)
        back = jnp.dot(
            upstream[...], layer_two[:, columns], preferred_element_type=jnp.float32
        ).astype(jnp.bfloat16)
        back = jnp.dot(turned[...], back, preferred_element_type=jnp.float32)
        back = (slope[:, columns] * back).astype(jnp.bfloat16)
        out[:features, :] = jnp.dot(
            mixed_turned[...], back, preferred_element_type=jnp.float32
        ).astype(out.dtype)
        stores.append(pltpu.make_async_copy(out, far, leaving.at[len(stores)]))
        stores[-1].start()
    for copy in stores:
        copy.wait()


def on_device(
    features,
    source_part,
    source_row,
    adj_tiles,
    tile_row,
    tile_col,
    tile_count,
    labels,
    layer_one,
    layer_two,
):
    devices = lax.axis_size(AXES)
    nodes = source_part.shape[0]
    width, hidden = layer_one.shape
    classes = layer_two.shape[1]
    capacity = max(2, 2 * nodes // devices)
    slots = devices * capacity
    bf = jnp.bfloat16
    requests, position = call(
        number_requests,
        [
            jax.ShapeDtypeStruct((devices, capacity), jnp.int32),
            jax.ShapeDtypeStruct((1, nodes), jnp.int32),
        ],
        0,
        2,
        limit=56 << 20,
    )(source_part.reshape(1, nodes), source_row.reshape(1, nodes))
    wanted = lax.all_to_all(requests, AXES, split_axis=0, concat_axis=0, tiled=True)
    anywhere = pl.BlockSpec(memory_space=pl.ANY)
    vmem = pl.BlockSpec(memory_space=pltpu.VMEM)
    smem = pl.BlockSpec(memory_space=pltpu.SMEM)
    found = pl.pallas_call(
        fetch_rows,
        out_shape=jax.ShapeDtypeStruct((slots, width), bf),
        in_specs=[anywhere, anywhere],
        out_specs=anywhere,
        scratch_shapes=[
            pltpu.SMEM(wanted.shape, jnp.int32),
            pltpu.VMEM(features.shape, bf),
            pltpu.VMEM(features.shape, jnp.float32),
            pltpu.VMEM((64, width), jnp.float32),
            pltpu.VMEM((slots, width), bf),
            pltpu.SemaphoreType.DMA,
            pltpu.SemaphoreType.DMA((8,)),
            pltpu.SemaphoreType.DMA((slots // 64,)),
        ],
        compiler_params=pltpu.CompilerParams(vmem_limit_bytes=56 << 20),
    )(wanted, features)
    arrived = lax.all_to_all(found, AXES, split_axis=0, concat_axis=0, tiled=True)
    dense, turned, moved = call(
        build_spread,
        [
            jax.ShapeDtypeStruct((nodes, nodes), bf),
            jax.ShapeDtypeStruct((nodes, nodes), bf),
            jax.ShapeDtypeStruct((nodes, slots), bf),
        ],
        3,
        2,
        cost=pl.CostEstimate(
            flops=2 * nodes * nodes * slots, bytes_accessed=12 << 20, transcendentals=0
        ),
    )(tile_row, tile_col, tile_count, adj_tiles, position)
    padded = jnp.pad(layer_two.T, ((0, 256 - classes), (0, 0)))
    core = lax.rem(lax.axis_index("store"), 2).astype(jnp.int32).reshape(1)
    half = SIDE * WIDTH
    sent, own = pl.pallas_call(
        partial(train, classes=classes),
        out_shape=[
            jax.ShapeDtypeStruct((ROWS, half), bf),
            jax.ShapeDtypeStruct((ROWS, half), bf),
        ],
        in_specs=[smem] + [anywhere] * 7,
        out_specs=[anywhere] * 2,
        scratch_shapes=[
            pltpu.VMEM((slots, width), bf),
            pltpu.VMEM((nodes, slots), bf),
            pltpu.VMEM((nodes, nodes), bf),
            pltpu.VMEM((nodes, nodes), bf),
            pltpu.VMEM((width, hidden), bf),
            pltpu.VMEM((256, hidden), bf),
            pltpu.VMEM((nodes, 1), jnp.int32),
            pltpu.VMEM((ROWS, half), bf),
            pltpu.VMEM((ROWS, half), bf),
            pltpu.VMEM((width, nodes), bf),
            pltpu.VMEM((nodes, hidden), jnp.float32),
            pltpu.VMEM((nodes, hidden), bf),
            pltpu.VMEM((nodes, hidden), bf),
            pltpu.VMEM((nodes, 256), bf),
            pltpu.VMEM((256, nodes), bf),
            pltpu.SemaphoreType.DMA((13,)),
            pltpu.SemaphoreType.DMA((2,)),
        ],
        compiler_params=pltpu.CompilerParams(vmem_limit_bytes=56 << 20),
        cost_estimate=pl.CostEstimate(
            flops=12 * nodes * nodes * hidden, bytes_accessed=16 << 20, transcendentals=nodes * hidden
        ),
    )(
        core,
        arrived.reshape(slots, width),
        moved,
        dense,
        turned,
        layer_one,
        padded,
        labels.reshape(nodes, 1),
    )
    grad_one, grad_two, loss = sum_over_devices(sent, own, width, classes)
    return (grad_one, grad_two.T, loss.reshape(()))


def solution(mesh):
    return jax.shard_map(
        on_device,
        mesh=mesh,
        in_specs=(
            P(("store", "batch"), None),
            P(("store", "batch")),
            P(("store", "batch")),
            P(("store", "batch"), None, None),
            P(("store", "batch")),
            P(("store", "batch")),
            P(("store", "batch")),
            P(("store", "batch")),
            P(),
            P(),
        ),
        out_specs=(P(), P(), P()),
        check_vma=False,
    )
```

```python
from functools import partial

import jax
import jax.numpy as jnp
from jax import lax
from jax.experimental import pallas as pl
from jax.experimental.pallas import tpu as pltpu
from jax.sharding import PartitionSpec as P

AXES = ("store", "batch")
SIDE = 4
WIDTH = 128
LOSS_ROW = 921
ROWS = 928


def flat(x, y, z, core):
    return ((x * SIDE + z) * 2 + core) * SIDE + y


def shift_pairs(axes, offset):
    pairs = []
    for x in range(SIDE):
        for y in range(SIDE):
            for z in range(SIDE):
                for core in range(2):
                    place = [x, y, z]
                    place[axes[core]] = (place[axes[core]] + offset) % SIDE
                    pairs.append((flat(x, y, z, core), flat(*place, core)))
    return pairs


def swap_pairs():
    return [
        (flat(x, y, z, core), flat(x, y, z, 1 - core))
        for x in range(SIDE)
        for y in range(SIDE)
        for z in range(SIDE)
        for core in range(2)
    ]


FIRST, SECOND, THIRD = (0, 1), (1, 2), (2, 0)


def split_loss(total):
    tail = total[ROWS - 8 :, :]
    row = lax.broadcasted_iota(jnp.int32, tail.shape, 0)
    lane = lax.broadcasted_iota(jnp.int32, tail.shape, 1)
    here = row == LOSS_ROW - (ROWS - 8)
    loss = jnp.sum(jnp.where(here & (lane < 3), tail, 0.0), axis=1, keepdims=True)
    high = loss.astype(jnp.bfloat16).astype(jnp.float32)
    middle = (loss - high).astype(jnp.bfloat16).astype(jnp.float32)
    low = (loss - high - middle).astype(jnp.bfloat16).astype(jnp.float32)
    parts = jnp.where(lane == 0, high, jnp.where(lane == 1, middle, jnp.where(lane == 2, low, 0.0)))
    return jnp.where(here, parts, tail)


def store_total(out, columns, total):
    out[: ROWS - 16, columns] = total[: ROWS - 16].astype(jnp.bfloat16)
    last = jnp.concatenate([total[ROWS - 16 : ROWS - 8], split_loss(total)], axis=0)
    out[ROWS - 16 :, columns] = last.astype(jnp.bfloat16)


def pick_blocks(place, far, near, arrival):
    copies = []
    for index, offset in enumerate((1, 2, 3, 0)):
        block = lax.rem(place[0] + offset, SIDE)
        columns = pl.ds(pl.multiple_of(block * WIDTH, WIDTH), WIDTH)
        copies.append(
            pltpu.make_async_copy(far.at[:, columns], near.at[index], arrival.at[index])
        )
        copies[-1].start()
    for copy in copies:
        copy.wait()


def first_add(place, own, arrived, keep, one, two, three):
    for index, (offset, out) in enumerate(((1, one), (2, two), (3, three), (0, keep))):
        block = lax.rem(place[0] + offset, SIDE)
        columns = pl.ds(pl.multiple_of(block * WIDTH, WIDTH), WIDTH)
        total = own[index].astype(jnp.float32) + arrived[:, columns].astype(jnp.float32)
        store_total(out, slice(None), total)


def four_add(own, one, two, three, out):
    total = (own[...].astype(jnp.float32) + two[...].astype(jnp.float32)) + (
        one[...].astype(jnp.float32) + three[...].astype(jnp.float32)
    )
    store_total(out, slice(None), total)


def place_blocks(place, own, one, two, three, out):
    for offset, block in ((0, own), (1, one), (2, two), (3, three)):
        at = lax.rem(place[0] + SIDE - offset, SIDE)
        out[:, pl.ds(pl.multiple_of(at * WIDTH, WIDTH), WIDTH)] = block[...]


def write_half(at, part, one_far, two_far, one, two, leaving):
    half = part.shape[1]
    features = one.shape[0]
    classes = two.shape[0]
    columns = pl.ds(pl.multiple_of(at * half, half), half)
    two[...] = part[features:, :].astype(jnp.float32)[:classes]
    copies = [pltpu.make_async_copy(two, two_far.at[:, columns], leaving.at[0])]
    copies[0].start()
    step = features // 4
    for index in range(4):
        rows = slice(index * step, (index + 1) * step)
        one[rows, :] = part[rows, :].astype(jnp.float32)
        lines = pl.ds(index * step, step)
        copies.append(
            pltpu.make_async_copy(
                one.at[lines, :], one_far.at[lines, columns], leaving.at[index + 1]
            )
        )
        copies[-1].start()
    return copies


def read_loss(part):
    tail = part[ROWS - 16 :, :WIDTH].astype(jnp.float32)
    row = lax.broadcasted_iota(jnp.int32, tail.shape, 0)
    lane = lax.broadcasted_iota(jnp.int32, tail.shape, 1)
    mine = (row == LOSS_ROW - (ROWS - 16)) & (lane < 3)
    return jnp.sum(jnp.sum(jnp.where(mine, tail, 0.0), axis=1, keepdims=True), axis=0, keepdims=True)


def write_own(core, own, one_far, two_far, one, two, leaving):
    for copy in write_half(core[0], own, one_far, two_far, one, two, leaving):
        copy.wait()


def write_other(core, own, other, one_in, two_in, one_far, two_far, loss, one, two, leaving):
    copies = write_half(1 - core[0], other, one_far, two_far, one, two, leaving)
    loss[...] = jnp.where(core[0] == 0, read_loss(own), read_loss(other))
    for copy in copies:
        copy.wait()


def call(kernel, outs, scalars=0, arrays=0, limit=16 << 20, cost=None, scratch=()):
    vmem = pl.BlockSpec(memory_space=pltpu.VMEM)
    smem = pl.BlockSpec(memory_space=pltpu.SMEM)
    return pl.pallas_call(
        kernel,
        out_shape=outs,
        in_specs=[smem] * scalars + [vmem] * arrays,
        out_specs=jax.tree.map(lambda _: vmem, outs),
        scratch_shapes=list(scratch),
        compiler_params=pltpu.CompilerParams(vmem_limit_bytes=limit),
        cost_estimate=cost,
    )


def sum_over_devices(sent, own, features, classes):
    store, batch = lax.axis_index("store"), lax.axis_index("batch")
    core = lax.rem(store, 2)
    place = jnp.where(core == 0, store // (2 * SIDE), batch).astype(jnp.int32).reshape(1)
    core = core.astype(jnp.int32).reshape(1)
    bf = jnp.bfloat16
    block = jax.ShapeDtypeStruct((ROWS, WIDTH), bf)
    arrived = lax.ppermute(sent, AXES, swap_pairs())
    picked = pl.pallas_call(
        pick_blocks,
        out_shape=jax.ShapeDtypeStruct((SIDE, ROWS, WIDTH), bf),
        in_specs=[pl.BlockSpec(memory_space=pltpu.SMEM), pl.BlockSpec(memory_space=pl.ANY)],
        out_specs=pl.BlockSpec(memory_space=pltpu.VMEM),
        scratch_shapes=[pltpu.SemaphoreType.DMA((SIDE,))],
        compiler_params=pltpu.CompilerParams(vmem_limit_bytes=16 << 20),
    )(place, own)
    keep, *parts = call(first_add, [block] * 4, 1, 2)(place, picked, arrived)
    got = [lax.ppermute(part, AXES, shift_pairs(FIRST, k + 1)) for k, part in enumerate(parts)]
    total = call(four_add, block, 0, 4)(keep, *got)
    for axes in (SECOND, THIRD):
        got = [lax.ppermute(total, AXES, shift_pairs(axes, k)) for k in (1, 2, 3)]
        total = call(four_add, block, 0, 4)(total, *got)
    got = [lax.ppermute(total, AXES, shift_pairs(FIRST, k)) for k in (1, 2, 3)]
    strip = call(place_blocks, jax.ShapeDtypeStruct((ROWS, SIDE * WIDTH), bf), 1, 4)(
        place, total, *got
    )
    other = lax.ppermute(strip, AXES, swap_pairs())
    half = SIDE * WIDTH
    grads = [
        jax.ShapeDtypeStruct((features, 2 * half), jnp.float32),
        jax.ShapeDtypeStruct((classes, 2 * half), jnp.float32),
    ]
    anywhere = pl.BlockSpec(memory_space=pl.ANY)
    vmem = pl.BlockSpec(memory_space=pltpu.VMEM)
    smem = pl.BlockSpec(memory_space=pltpu.SMEM)
    scratch = [
        pltpu.VMEM((features, half), jnp.float32),
        pltpu.VMEM((classes, half), jnp.float32),
        pltpu.SemaphoreType.DMA((5,)),
    ]
    params = pltpu.CompilerParams(vmem_limit_bytes=16 << 20)
    grad_one, grad_two = pl.pallas_call(
        write_own,
        out_shape=grads,
        in_specs=[smem, vmem],
        out_specs=[anywhere] * 2,
        scratch_shapes=scratch,
        compiler_params=params,
    )(core, strip)
    return pl.pallas_call(
        write_other,
        out_shape=[*grads, jax.ShapeDtypeStruct((1, 1), jnp.float32)],
        in_specs=[smem, vmem, vmem, anywhere, anywhere],
        out_specs=[anywhere, anywhere, vmem],
        scratch_shapes=scratch,
        input_output_aliases={3: 0, 4: 1},
        compiler_params=params,
    )(core, strip, other, grad_one, grad_two)


def number_requests(parts, rows, requests, position):
    devices, capacity = requests.shape
    nodes = parts.shape[1]
    piece = 128
    owner = lax.broadcasted_iota(jnp.int32, (devices, nodes), 0)
    mine = jnp.where(owner == parts[...], 1.0, 0.0)
    line = lax.broadcasted_iota(jnp.int32, (piece, piece), 0)
    lane = lax.broadcasted_iota(jnp.int32, (piece, piece), 1)
    earlier = jnp.where(line < lane, 1.0, 0.0).astype(jnp.bfloat16)
    seen = jnp.zeros((devices, 1), jnp.float32)
    slots = []
    for start in range(0, nodes, piece):
        here = mine[:, start : start + piece]
        rank = jnp.dot(here.astype(jnp.bfloat16), earlier, preferred_element_type=jnp.float32)
        slots.append(jnp.sum(here * (rank + seen), axis=0, keepdims=True))
        seen = seen + jnp.sum(here, axis=1, keepdims=True)
    slot = jnp.concatenate(slots, axis=1).astype(jnp.int32)
    position[...] = parts[...] * capacity + slot
    placed = lax.broadcasted_iota(jnp.int32, (capacity, nodes), 0) == slot
    total = jnp.zeros((devices, capacity), jnp.float32)
    for scale, digit in ((64.0, lax.shift_right_logical(rows[...], 6)), (1.0, rows[...] & 63)):
        values = jnp.where(placed, digit.astype(jnp.float32), 0.0).astype(jnp.bfloat16)
        total += scale * lax.dot_general(
            mine.astype(jnp.bfloat16),
            values,
            (((1,), (1,)), ((), ())),
            preferred_element_type=jnp.float32,
        )
    requests[...] = total.astype(jnp.int32)


def fetch_rows(wanted_far, table, far, wanted, narrow, wide, some, out, listed, arrival, leaving):
    stored, width = table.shape
    step = stored // arrival.shape[0]

    def load(block):
        rows = pl.ds(block * step, step)
        return pltpu.make_async_copy(table.at[rows, :], narrow.at[rows, :], arrival.at[block])

    listing = pltpu.make_async_copy(wanted_far, wanted, listed)
    listing.start()
    for block in range(arrival.shape[0]):
        load(block).start()
    for block in range(arrival.shape[0]):
        load(block).wait()
        for start in range(block * step, (block + 1) * step, 128):
            rows = slice(start, start + 128)
            wide[rows, :] = narrow[rows, :].astype(jnp.float32)

    listing.wait()
    devices, capacity = wanted.shape
    owners = some.shape[0] // capacity

    def send(block):
        rows = pl.ds(pl.multiple_of(block * some.shape[0], some.shape[0]), some.shape[0])
        return pltpu.make_async_copy(out.at[rows, :], far.at[rows, :], leaving.at[block])

    @pl.loop(0, devices // owners)
    def _(block):
        for owner in range(owners):
            for slot in range(capacity):
                row = wanted[block * owners + owner, slot]
                some[pl.ds(owner * capacity + slot, 1), :] = wide[pl.ds(row, 1), :]
        rows = pl.ds(pl.multiple_of(block * some.shape[0], some.shape[0]), some.shape[0])
        out[rows, :] = some[...].astype(jnp.bfloat16)
        send(block).start()

    @pl.loop(0, devices // owners)
    def _(block):
        send(block).wait()


def build_spread(row, column, count, tiles, position, dense, turned, moved):
    nodes = dense.shape[0]
    tile = tiles.shape[1]
    dense[...] = jnp.zeros_like(dense)
    turned[...] = jnp.zeros_like(turned)

    @pl.loop(0, count[0])
    def _(t):
        at_row = pl.ds(pl.multiple_of(row[t] * tile, tile), tile)
        at_column = pl.ds(pl.multiple_of(column[t] * tile, tile), tile)
        values = tiles[t]
        dense[at_row, at_column] = values
        turned[at_column, at_row] = values.T

    width = 256

    @pl.loop(0, moved.shape[1] // width)
    def _(step):
        start = pl.multiple_of(step * width, width)
        slot = lax.broadcasted_iota(jnp.int32, (width, nodes), 0) + start
        chosen = jnp.where(slot == position[...], 1.0, 0.0).astype(jnp.bfloat16)
        moved[:, pl.ds(start, width)] = lax.dot_general(
            dense[...], chosen, (((1,), (1,)), ((), ())), preferred_element_type=jnp.float32
        ).astype(jnp.bfloat16)


def train(
    core,
    arrived_far,
    moved_far,
    dense_far,
    turned_far,
    one_far,
    two_far,
    labels_far,
    sent_far,
    own_far,
    arrived,
    moved,
    dense,
    turned,
    layer_one,
    layer_two,
    labels,
    sent,
    own,
    mixed_turned,
    slope,
    hidden,
    smooth,
    upstream,
    upstream_turned,
    arrival,
    leaving,
    *,
    classes,
):
    nodes = dense.shape[0]
    features = mixed_turned.shape[0]
    step = 256
    tiles = range(0, nodes, step)

    def load(index, far, near):
        return pltpu.make_async_copy(far, near, arrival.at[index])

    part = arrived.shape[0] // SIDE
    get_arrived = [
        load(at, arrived_far.at[pl.ds(at * part, part), :], arrived.at[pl.ds(at * part, part), :])
        for at in range(SIDE)
    ]
    get_one = load(4, one_far, layer_one)
    get_dense = load(5, dense_far, dense)
    get_two = load(6, two_far, layer_two)
    get_labels = load(7, labels_far, labels)
    get_turned = load(8, turned_far, turned)
    get_moved = [
        load(9 + at, moved_far.at[pl.ds(start, step), :], moved.at[pl.ds(start, step), :])
        for at, start in enumerate(tiles)
    ]
    get_moved[0].start()
    for copy in get_arrived:
        copy.start()
    get_one.start()
    get_moved[0].wait()
    for at, start in enumerate(tiles):
        rows = slice(start, start + step)
        if at > 0:
            get_moved[at].wait()
            mixed = jnp.dot(moved[rows, :], arrived[...], preferred_element_type=jnp.float32)
        else:
            mixed = 0.0
            for index, copy in enumerate(get_arrived):
                copy.wait()
                slots = slice(index * part, (index + 1) * part)
                mixed += jnp.dot(
                    moved[rows, slots], arrived[slots, :], preferred_element_type=jnp.float32
                )
            for copy in get_moved[1:]:
                copy.start()
        mixed = mixed.astype(jnp.bfloat16)
        mixed_turned[:, rows] = mixed.T
        if at == 0:
            get_one.wait()
            get_dense.start()
            get_two.start()
            get_labels.start()
            get_turned.start()
        before = jnp.dot(mixed, layer_one[...], preferred_element_type=jnp.float32)
        square = before * before
        rate = 0.7978845608028654
        bend = jnp.tanh(rate * before * (1.0 + 0.044715 * square))
        rise = 0.5 * (1.0 + bend)
        hidden[rows, :] = (before * rise).astype(jnp.bfloat16)
        slope[rows, :] = rise + 0.5 * before * (1.0 - bend * bend) * (
            rate + (3.0 * 0.044715 * rate) * square
        )
    get_dense.wait()
    get_two.wait()
    get_labels.wait()
    loss = jnp.zeros((1, 1), jnp.float32)
    for start in tiles:
        rows = slice(start, start + step)
        spread = jnp.dot(dense[rows, :], hidden[...], preferred_element_type=jnp.float32).astype(
            jnp.bfloat16
        )
        smooth[rows, :] = spread
        logits = lax.dot_general(
            spread, layer_two[...], (((1,), (1,)), ((), ())), preferred_element_type=jnp.float32
        )
        lane = lax.broadcasted_iota(jnp.int32, logits.shape, 1)
        logits = jnp.where(lane < classes, logits, -jnp.inf)
        largest = jnp.max(logits, axis=1, keepdims=True)
        logsum = jnp.log(jnp.sum(jnp.exp(logits - largest), axis=1, keepdims=True)) + largest
        truth = lane == labels[rows, :]
        picked = jnp.sum(jnp.where(truth, logits, 0.0), axis=1, keepdims=True)
        loss += jnp.sum(logsum - picked, axis=0, keepdims=True)
        gap = (jnp.exp(logits - logsum) - jnp.where(truth, 1.0, 0.0)) * (1.0 / nodes)
        upstream[rows, :] = gap.astype(jnp.bfloat16)
        upstream_turned[:, rows] = gap.astype(jnp.bfloat16).T
    loss = loss * (1.0 / nodes)
    high = loss.astype(jnp.bfloat16).astype(jnp.float32)
    middle = (loss - high).astype(jnp.bfloat16).astype(jnp.float32)
    low = loss - high - middle
    half = SIDE * WIDTH
    get_turned.wait()
    stores = []
    for offset, out, far in ((1, sent, sent_far), (0, own, own_far)):
        part = lax.rem(core[0] + offset, 2)
        columns = pl.ds(pl.multiple_of(part * half, half), half)
        second = jnp.dot(
            upstream_turned[: ROWS - features, :],
            smooth[:, columns],
            preferred_element_type=jnp.float32,
        )
        row = lax.broadcasted_iota(jnp.int32, second.shape, 0)
        lane = lax.broadcasted_iota(jnp.int32, second.shape, 1)
        here = (row == LOSS_ROW - features) & (part == 0)
        second += jnp.where(here & (lane == 0), high, 0.0)
        second += jnp.where(here & (lane == 1), middle, 0.0)
        second += jnp.where(here & (lane == 2), low, 0.0)
        out[features:, :] = second.astype(out.dtype)
        back = jnp.dot(
            upstream[...], layer_two[:, columns], preferred_element_type=jnp.float32
        ).astype(jnp.bfloat16)
        back = jnp.dot(turned[...], back, preferred_element_type=jnp.float32)
        back = (slope[:, columns] * back).astype(jnp.bfloat16)
        out[:features, :] = jnp.dot(
            mixed_turned[...], back, preferred_element_type=jnp.float32
        ).astype(out.dtype)
        stores.append(pltpu.make_async_copy(out, far, leaving.at[len(stores)]))
        stores[-1].start()
    for copy in stores:
        copy.wait()


def on_device(
    features,
    source_part,
    source_row,
    adj_tiles,
    tile_row,
    tile_col,
    tile_count,
    labels,
    layer_one,
    layer_two,
):
    devices = lax.axis_size(AXES)
    nodes = source_part.shape[0]
    width, hidden = layer_one.shape
    classes = layer_two.shape[1]
    capacity = max(2, 2 * nodes // devices)
    slots = devices * capacity
    bf = jnp.bfloat16
    requests, position = call(
        number_requests,
        [
            jax.ShapeDtypeStruct((devices, capacity), jnp.int32),
            jax.ShapeDtypeStruct((1, nodes), jnp.int32),
        ],
        0,
        2,
        limit=56 << 20,
    )(source_part.reshape(1, nodes), source_row.reshape(1, nodes))
    wanted = lax.all_to_all(requests, AXES, split_axis=0, concat_axis=0, tiled=True)
    anywhere = pl.BlockSpec(memory_space=pl.ANY)
    vmem = pl.BlockSpec(memory_space=pltpu.VMEM)
    smem = pl.BlockSpec(memory_space=pltpu.SMEM)
    found = pl.pallas_call(
        fetch_rows,
        out_shape=jax.ShapeDtypeStruct((slots, width), bf),
        in_specs=[anywhere, anywhere],
        out_specs=anywhere,
        scratch_shapes=[
            pltpu.SMEM(wanted.shape, jnp.int32),
            pltpu.VMEM(features.shape, bf),
            pltpu.VMEM(features.shape, jnp.float32),
            pltpu.VMEM((64, width), jnp.float32),
            pltpu.VMEM((slots, width), bf),
            pltpu.SemaphoreType.DMA,
            pltpu.SemaphoreType.DMA((8,)),
            pltpu.SemaphoreType.DMA((slots // 64,)),
        ],
        compiler_params=pltpu.CompilerParams(vmem_limit_bytes=56 << 20),
    )(wanted, features)
    arrived = lax.all_to_all(found, AXES, split_axis=0, concat_axis=0, tiled=True)
    dense, turned, moved = call(
        build_spread,
        [
            jax.ShapeDtypeStruct((nodes, nodes), bf),
            jax.ShapeDtypeStruct((nodes, nodes), bf),
            jax.ShapeDtypeStruct((nodes, slots), bf),
        ],
        3,
        2,
        cost=pl.CostEstimate(
            flops=2 * nodes * nodes * slots, bytes_accessed=12 << 20, transcendentals=0
        ),
    )(tile_row, tile_col, tile_count, adj_tiles, position)
    padded = jnp.pad(layer_two.T, ((0, 256 - classes), (0, 0)))
    core = lax.rem(lax.axis_index("store"), 2).astype(jnp.int32).reshape(1)
    half = SIDE * WIDTH
    sent, own = pl.pallas_call(
        partial(train, classes=classes),
        out_shape=[
            jax.ShapeDtypeStruct((ROWS, half), bf),
            jax.ShapeDtypeStruct((ROWS, half), bf),
        ],
        in_specs=[smem] + [anywhere] * 7,
        out_specs=[anywhere] * 2,
        scratch_shapes=[
            pltpu.VMEM((slots, width), bf),
            pltpu.VMEM((nodes, slots), bf),
            pltpu.VMEM((nodes, nodes), bf),
            pltpu.VMEM((nodes, nodes), bf),
            pltpu.VMEM((width, hidden), bf),
            pltpu.VMEM((256, hidden), bf),
            pltpu.VMEM((nodes, 1), jnp.int32),
            pltpu.VMEM((ROWS, half), bf),
            pltpu.VMEM((ROWS, half), bf),
            pltpu.VMEM((width, nodes), bf),
            pltpu.VMEM((nodes, hidden), jnp.float32),
            pltpu.VMEM((nodes, hidden), bf),
            pltpu.VMEM((nodes, hidden), bf),
            pltpu.VMEM((nodes, 256), bf),
            pltpu.VMEM((256, nodes), bf),
            pltpu.SemaphoreType.DMA((13,)),
            pltpu.SemaphoreType.DMA((2,)),
        ],
        compiler_params=pltpu.CompilerParams(vmem_limit_bytes=56 << 20),
        cost_estimate=pl.CostEstimate(
            flops=12 * nodes * nodes * hidden, bytes_accessed=16 << 20, transcendentals=nodes * hidden
        ),
    )(
        core,
        arrived.reshape(slots, width),
        moved,
        dense,
        turned,
        layer_one,
        padded,
        labels.reshape(nodes, 1),
    )
    grad_one, grad_two, loss = sum_over_devices(sent, own, width, classes)
    return (grad_one, grad_two.T, loss.reshape(()))


def solution(mesh):
    return jax.shard_map(
        on_device,
        mesh=mesh,
        in_specs=(
            P(("store", "batch"), None),
            P(("store", "batch")),
            P(("store", "batch")),
            P(("store", "batch"), None, None),
            P(("store", "batch")),
            P(("store", "batch")),
            P(("store", "batch")),
            P(("store", "batch")),
            P(),
            P(),
        ),
        out_specs=(P(), P(), P()),
        check_vma=False,
    )
```

```python
from functools import partial

import jax
import jax.numpy as jnp
from jax import lax
from jax.experimental import pallas as pl
from jax.experimental.pallas import tpu as pltpu
from jax.sharding import PartitionSpec as P

AXES = ("store", "batch")
SIDE = 4
WIDTH = 128
LOSS_ROW = 921
ROWS = 928
PITCH = 7


def flat(x, y, z, core):
    return ((x * SIDE + z) * 2 + core) * SIDE + y


def shift_pairs(axes, offset):
    pairs = []
    for x in range(SIDE):
        for y in range(SIDE):
            for z in range(SIDE):
                for core in range(2):
                    place = [x, y, z]
                    place[axes[core]] = (place[axes[core]] + offset) % SIDE
                    pairs.append((flat(x, y, z, core), flat(*place, core)))
    return pairs


def swap_pairs():
    return [
        (flat(x, y, z, core), flat(x, y, z, 1 - core))
        for x in range(SIDE)
        for y in range(SIDE)
        for z in range(SIDE)
        for core in range(2)
    ]


FIRST, SECOND, THIRD = (0, 1), (1, 2), (2, 0)


def split_loss(total):
    tail = total[ROWS - 8 :, :]
    row = lax.broadcasted_iota(jnp.int32, tail.shape, 0)
    lane = lax.broadcasted_iota(jnp.int32, tail.shape, 1)
    here = row == LOSS_ROW - (ROWS - 8)
    loss = jnp.sum(jnp.where(here & (lane < 3), tail, 0.0), axis=1, keepdims=True)
    high = loss.astype(jnp.bfloat16).astype(jnp.float32)
    middle = (loss - high).astype(jnp.bfloat16).astype(jnp.float32)
    low = (loss - high - middle).astype(jnp.bfloat16).astype(jnp.float32)
    parts = jnp.where(lane == 0, high, jnp.where(lane == 1, middle, jnp.where(lane == 2, low, 0.0)))
    return jnp.where(here, parts, tail)


def store_total(out, columns, total):
    out[: ROWS - 16, columns] = total[: ROWS - 16].astype(jnp.bfloat16)
    last = jnp.concatenate([total[ROWS - 16 : ROWS - 8], split_loss(total)], axis=0)
    out[ROWS - 16 :, columns] = last.astype(jnp.bfloat16)


def pick_blocks(place, far, near, arrival):
    copies = []
    for index, offset in enumerate((1, 2, 3, 0)):
        block = lax.rem(place[0] + offset, SIDE)
        columns = pl.ds(pl.multiple_of(block * WIDTH, WIDTH), WIDTH)
        copies.append(
            pltpu.make_async_copy(far.at[:, columns], near.at[index], arrival.at[index])
        )
        copies[-1].start()
    for copy in copies:
        copy.wait()


def first_add(place, own, arrived, keep, one, two, three):
    for index, (offset, out) in enumerate(((1, one), (2, two), (3, three), (0, keep))):
        block = lax.rem(place[0] + offset, SIDE)
        columns = pl.ds(pl.multiple_of(block * WIDTH, WIDTH), WIDTH)
        total = own[index].astype(jnp.float32) + arrived[:, columns].astype(jnp.float32)
        store_total(out, slice(None), total)


def four_add(own, one, two, three, out):
    total = (own[...].astype(jnp.float32) + two[...].astype(jnp.float32)) + (
        one[...].astype(jnp.float32) + three[...].astype(jnp.float32)
    )
    store_total(out, slice(None), total)


def place_blocks(place, own, one, two, three, out):
    for offset, block in ((0, own), (1, one), (2, two), (3, three)):
        at = lax.rem(place[0] + SIDE - offset, SIDE)
        out[:, pl.ds(pl.multiple_of(at * WIDTH, WIDTH), WIDTH)] = block[...]


def write_half(at, part, one_far, two_far, one, two, leaving):
    half = part.shape[1]
    features = one.shape[0]
    classes = two.shape[0]
    columns = pl.ds(pl.multiple_of(at * half, half), half)
    two[...] = part[features:, :].astype(jnp.float32)[:classes]
    copies = [pltpu.make_async_copy(two, two_far.at[:, columns], leaving.at[0])]
    copies[0].start()
    step = features // 4
    for index in range(4):
        rows = slice(index * step, (index + 1) * step)
        one[rows, :] = part[rows, :].astype(jnp.float32)
        lines = pl.ds(index * step, step)
        copies.append(
            pltpu.make_async_copy(
                one.at[lines, :], one_far.at[lines, columns], leaving.at[index + 1]
            )
        )
        copies[-1].start()
    return copies


def read_loss(part):
    tail = part[ROWS - 16 :, :WIDTH].astype(jnp.float32)
    row = lax.broadcasted_iota(jnp.int32, tail.shape, 0)
    lane = lax.broadcasted_iota(jnp.int32, tail.shape, 1)
    mine = (row == LOSS_ROW - (ROWS - 16)) & (lane < 3)
    return jnp.sum(jnp.sum(jnp.where(mine, tail, 0.0), axis=1, keepdims=True), axis=0, keepdims=True)


def write_own(core, own, one_far, two_far, one, two, leaving):
    for copy in write_half(core[0], own, one_far, two_far, one, two, leaving):
        copy.wait()


def write_other(core, own, other, one_in, two_in, one_far, two_far, loss, one, two, leaving):
    copies = write_half(1 - core[0], other, one_far, two_far, one, two, leaving)
    loss[...] = jnp.where(core[0] == 0, read_loss(own), read_loss(other))
    for copy in copies:
        copy.wait()


def call(kernel, outs, scalars=0, arrays=0, limit=16 << 20, cost=None, scratch=()):
    vmem = pl.BlockSpec(memory_space=pltpu.VMEM)
    smem = pl.BlockSpec(memory_space=pltpu.SMEM)
    return pl.pallas_call(
        kernel,
        out_shape=outs,
        in_specs=[smem] * scalars + [vmem] * arrays,
        out_specs=jax.tree.map(lambda _: vmem, outs),
        scratch_shapes=list(scratch),
        compiler_params=pltpu.CompilerParams(vmem_limit_bytes=limit),
        cost_estimate=cost,
    )


def sum_over_devices(sent, own, features, classes):
    store, batch = lax.axis_index("store"), lax.axis_index("batch")
    core = lax.rem(store, 2)
    place = jnp.where(core == 0, store // (2 * SIDE), batch).astype(jnp.int32).reshape(1)
    core = core.astype(jnp.int32).reshape(1)
    bf = jnp.bfloat16
    block = jax.ShapeDtypeStruct((ROWS, WIDTH), bf)
    arrived = lax.ppermute(sent, AXES, swap_pairs())
    picked = pl.pallas_call(
        pick_blocks,
        out_shape=jax.ShapeDtypeStruct((SIDE, ROWS, WIDTH), bf),
        in_specs=[pl.BlockSpec(memory_space=pltpu.SMEM), pl.BlockSpec(memory_space=pl.ANY)],
        out_specs=pl.BlockSpec(memory_space=pltpu.VMEM),
        scratch_shapes=[pltpu.SemaphoreType.DMA((SIDE,))],
        compiler_params=pltpu.CompilerParams(vmem_limit_bytes=16 << 20),
    )(place, own)
    keep, *parts = call(first_add, [block] * 4, 1, 2)(place, picked, arrived)
    got = [lax.ppermute(part, AXES, shift_pairs(FIRST, k + 1)) for k, part in enumerate(parts)]
    total = call(four_add, block, 0, 4)(keep, *got)
    for axes in (SECOND, THIRD):
        got = [lax.ppermute(total, AXES, shift_pairs(axes, k)) for k in (1, 2, 3)]
        total = call(four_add, block, 0, 4)(total, *got)
    got = [lax.ppermute(total, AXES, shift_pairs(FIRST, k)) for k in (1, 2, 3)]
    strip = call(place_blocks, jax.ShapeDtypeStruct((ROWS, SIDE * WIDTH), bf), 1, 4)(
        place, total, *got
    )
    other = lax.ppermute(strip, AXES, swap_pairs())
    half = SIDE * WIDTH
    grads = [
        jax.ShapeDtypeStruct((features, 2 * half), jnp.float32),
        jax.ShapeDtypeStruct((classes, 2 * half), jnp.float32),
    ]
    anywhere = pl.BlockSpec(memory_space=pl.ANY)
    vmem = pl.BlockSpec(memory_space=pltpu.VMEM)
    smem = pl.BlockSpec(memory_space=pltpu.SMEM)
    scratch = [
        pltpu.VMEM((features, half), jnp.float32),
        pltpu.VMEM((classes, half), jnp.float32),
        pltpu.SemaphoreType.DMA((5,)),
    ]
    params = pltpu.CompilerParams(vmem_limit_bytes=16 << 20)
    grad_one, grad_two = pl.pallas_call(
        write_own,
        out_shape=grads,
        in_specs=[smem, vmem],
        out_specs=[anywhere] * 2,
        scratch_shapes=scratch,
        compiler_params=params,
    )(core, strip)
    return pl.pallas_call(
        write_other,
        out_shape=[*grads, jax.ShapeDtypeStruct((1, 1), jnp.float32)],
        in_specs=[smem, vmem, vmem, anywhere, anywhere],
        out_specs=[anywhere, anywhere, vmem],
        scratch_shapes=scratch,
        input_output_aliases={3: 0, 4: 1},
        compiler_params=params,
    )(core, strip, other, grad_one, grad_two)


def number_requests(parts, rows, requests, position):
    devices, capacity = requests.shape
    nodes = parts.shape[1]
    piece = 128
    owner = lax.broadcasted_iota(jnp.int32, (devices, nodes), 0)
    mine = jnp.where(owner == parts[...], 1.0, 0.0)
    line = lax.broadcasted_iota(jnp.int32, (piece, piece), 0)
    lane = lax.broadcasted_iota(jnp.int32, (piece, piece), 1)
    earlier = jnp.where(line < lane, 1.0, 0.0).astype(jnp.bfloat16)
    seen = jnp.zeros((devices, 1), jnp.float32)
    slots = []
    for start in range(0, nodes, piece):
        here = mine[:, start : start + piece]
        rank = jnp.dot(here.astype(jnp.bfloat16), earlier, preferred_element_type=jnp.float32)
        slots.append(jnp.sum(here * (rank + seen), axis=0, keepdims=True))
        seen = seen + jnp.sum(here, axis=1, keepdims=True)
    slot = jnp.concatenate(slots, axis=1).astype(jnp.int32)
    position[...] = parts[...] * capacity + slot
    placed = lax.broadcasted_iota(jnp.int32, (capacity, nodes), 0) == slot
    total = jnp.zeros((devices, capacity), jnp.float32)
    for scale, digit in ((64.0, lax.shift_right_logical(rows[...], 6)), (1.0, rows[...] & 63)):
        values = jnp.where(placed, digit.astype(jnp.float32), 0.0).astype(jnp.bfloat16)
        total += scale * lax.dot_general(
            mine.astype(jnp.bfloat16),
            values,
            (((1,), (1,)), ((), ())),
            preferred_element_type=jnp.float32,
        )
    requests[...] = total.astype(jnp.int32)


def fetch_rows(wanted_far, table, far, wanted, narrow, wide, some, out, listed, arrival, leaving):
    stored, width = table.shape
    pieces = width // 128
    step = stored // arrival.shape[0]

    def load(block):
        rows = pl.ds(block * step, step)
        return pltpu.make_async_copy(table.at[rows, :], narrow.at[rows, :], arrival.at[block])

    listing = pltpu.make_async_copy(wanted_far, wanted, listed)
    listing.start()
    for block in range(arrival.shape[0]):
        load(block).start()
    for block in range(arrival.shape[0]):
        load(block).wait()

        @pl.loop(0, step // 64)
        def _(part):
            start = pl.multiple_of(block * step + part * 64, 64)
            values = narrow[pl.ds(start, 64), :].astype(jnp.float32)
            for line in range(0, 64, 8):
                for piece in range(pieces):
                    lines = pl.ds((start + line) * PITCH + piece, 8, stride=PITCH)
                    wide[lines, :] = values[line : line + 8, piece * 128 : (piece + 1) * 128]

    listing.wait()
    devices, capacity = wanted.shape
    group = out.shape[0] // leaving.shape[0]
    owners = group // capacity

    def send(block):
        rows = pl.ds(pl.multiple_of(block * group, group), group)
        return pltpu.make_async_copy(out.at[rows, :], far.at[rows, :], leaving.at[block])

    @pl.loop(0, devices // owners)
    def _(block):
        for line in range(group):
            row = wanted[block * owners + line // capacity, line % capacity]
            some[pl.ds(line * PITCH, pieces), :] = wide[pl.ds(row * PITCH, pieces), :]
        for line in range(0, group, 16):
            rows = pl.ds(pl.multiple_of(block * group + line, 16), 16)
            for piece in range(pieces):
                halves = [
                    some[pl.ds((line + half) * PITCH + piece, 8, stride=PITCH), :] for half in (0, 8)
                ]
                out[rows, piece * 128 : (piece + 1) * 128] = jnp.concatenate(halves, axis=0).astype(
                    jnp.bfloat16
                )
        send(block).start()

    @pl.loop(0, devices // owners)
    def _(block):
        send(block).wait()


def build_spread(row, column, count, tiles, position, dense, turned, moved):
    nodes = dense.shape[0]
    tile = tiles.shape[1]
    dense[...] = jnp.zeros_like(dense)
    turned[...] = jnp.zeros_like(turned)

    @pl.loop(0, count[0])
    def _(t):
        at_row = pl.ds(pl.multiple_of(row[t] * tile, tile), tile)
        at_column = pl.ds(pl.multiple_of(column[t] * tile, tile), tile)
        values = tiles[t]
        dense[at_row, at_column] = values
        turned[at_column, at_row] = values.T

    width = 256

    @pl.loop(0, moved.shape[1] // width)
    def _(step):
        start = pl.multiple_of(step * width, width)
        slot = lax.broadcasted_iota(jnp.int32, (width, nodes), 0) + start
        chosen = jnp.where(slot == position[...], 1.0, 0.0).astype(jnp.bfloat16)
        moved[:, pl.ds(start, width)] = lax.dot_general(
            dense[...], chosen, (((1,), (1,)), ((), ())), preferred_element_type=jnp.float32
        ).astype(jnp.bfloat16)


def train(
    core,
    arrived_far,
    moved_far,
    dense_far,
    turned_far,
    one_far,
    two_far,
    labels_far,
    sent_far,
    own_far,
    arrived,
    moved,
    dense,
    turned,
    layer_one,
    layer_two,
    labels,
    sent,
    own,
    mixed_turned,
    slope,
    hidden,
    smooth,
    upstream,
    upstream_turned,
    arrival,
    leaving,
    *,
    classes,
):
    nodes = dense.shape[0]
    features = mixed_turned.shape[0]
    step = 256
    tiles = range(0, nodes, step)

    def load(index, far, near):
        return pltpu.make_async_copy(far, near, arrival.at[index])

    part = arrived.shape[0] // SIDE
    get_arrived = [
        load(at, arrived_far.at[pl.ds(at * part, part), :], arrived.at[pl.ds(at * part, part), :])
        for at in range(SIDE)
    ]
    get_one = load(4, one_far, layer_one)
    get_dense = load(5, dense_far, dense)
    get_two = load(6, two_far, layer_two)
    get_labels = load(7, labels_far, labels)
    get_turned = load(8, turned_far, turned)
    get_moved = [
        load(9 + at, moved_far.at[pl.ds(start, step), :], moved.at[pl.ds(start, step), :])
        for at, start in enumerate(tiles)
    ]
    get_moved[0].start()
    for copy in get_arrived:
        copy.start()
    get_one.start()
    get_moved[0].wait()
    for at, start in enumerate(tiles):
        rows = slice(start, start + step)
        if at > 0:
            get_moved[at].wait()
            mixed = jnp.dot(moved[rows, :], arrived[...], preferred_element_type=jnp.float32)
        else:
            mixed = 0.0
            for index, copy in enumerate(get_arrived):
                copy.wait()
                slots = slice(index * part, (index + 1) * part)
                mixed += jnp.dot(
                    moved[rows, slots], arrived[slots, :], preferred_element_type=jnp.float32
                )
            for copy in get_moved[1:]:
                copy.start()
        mixed = mixed.astype(jnp.bfloat16)
        mixed_turned[:, rows] = mixed.T
        if at == 0:
            get_one.wait()
            get_dense.start()
            get_two.start()
            get_labels.start()
            get_turned.start()
        before = jnp.dot(mixed, layer_one[...], preferred_element_type=jnp.float32)
        square = before * before
        rate = 0.7978845608028654
        bend = jnp.tanh(rate * before * (1.0 + 0.044715 * square))
        rise = 0.5 * (1.0 + bend)
        hidden[rows, :] = (before * rise).astype(jnp.bfloat16)
        slope[rows, :] = rise + 0.5 * before * (1.0 - bend * bend) * (
            rate + (3.0 * 0.044715 * rate) * square
        )
    get_dense.wait()
    get_two.wait()
    get_labels.wait()
    loss = jnp.zeros((1, 1), jnp.float32)
    for start in tiles:
        rows = slice(start, start + step)
        spread = jnp.dot(dense[rows, :], hidden[...], preferred_element_type=jnp.float32).astype(
            jnp.bfloat16
        )
        smooth[rows, :] = spread
        logits = lax.dot_general(
            spread, layer_two[...], (((1,), (1,)), ((), ())), preferred_element_type=jnp.float32
        )
        lane = lax.broadcasted_iota(jnp.int32, logits.shape, 1)
        logits = jnp.where(lane < classes, logits, -jnp.inf)
        largest = jnp.max(logits, axis=1, keepdims=True)
        logsum = jnp.log(jnp.sum(jnp.exp(logits - largest), axis=1, keepdims=True)) + largest
        truth = lane == labels[rows, :]
        picked = jnp.sum(jnp.where(truth, logits, 0.0), axis=1, keepdims=True)
        loss += jnp.sum(logsum - picked, axis=0, keepdims=True)
        gap = (jnp.exp(logits - logsum) - jnp.where(truth, 1.0, 0.0)) * (1.0 / nodes)
        upstream[rows, :] = gap.astype(jnp.bfloat16)
        upstream_turned[:, rows] = gap.astype(jnp.bfloat16).T
    loss = loss * (1.0 / nodes)
    high = loss.astype(jnp.bfloat16).astype(jnp.float32)
    middle = (loss - high).astype(jnp.bfloat16).astype(jnp.float32)
    low = loss - high - middle
    half = SIDE * WIDTH
    get_turned.wait()
    stores = []
    for offset, out, far in ((1, sent, sent_far), (0, own, own_far)):
        part = lax.rem(core[0] + offset, 2)
        columns = pl.ds(pl.multiple_of(part * half, half), half)
        second = jnp.dot(
            upstream_turned[: ROWS - features, :],
            smooth[:, columns],
            preferred_element_type=jnp.float32,
        )
        row = lax.broadcasted_iota(jnp.int32, second.shape, 0)
        lane = lax.broadcasted_iota(jnp.int32, second.shape, 1)
        here = (row == LOSS_ROW - features) & (part == 0)
        second += jnp.where(here & (lane == 0), high, 0.0)
        second += jnp.where(here & (lane == 1), middle, 0.0)
        second += jnp.where(here & (lane == 2), low, 0.0)
        out[features:, :] = second.astype(out.dtype)
        back = jnp.dot(
            upstream[...], layer_two[:, columns], preferred_element_type=jnp.float32
        ).astype(jnp.bfloat16)
        back = jnp.dot(turned[...], back, preferred_element_type=jnp.float32)
        back = (slope[:, columns] * back).astype(jnp.bfloat16)
        out[:features, :] = jnp.dot(
            mixed_turned[...], back, preferred_element_type=jnp.float32
        ).astype(out.dtype)
        stores.append(pltpu.make_async_copy(out, far, leaving.at[len(stores)]))
        stores[-1].start()
    for copy in stores:
        copy.wait()


def on_device(
    features,
    source_part,
    source_row,
    adj_tiles,
    tile_row,
    tile_col,
    tile_count,
    labels,
    layer_one,
    layer_two,
):
    devices = lax.axis_size(AXES)
    nodes = source_part.shape[0]
    width, hidden = layer_one.shape
    classes = layer_two.shape[1]
    capacity = max(2, 2 * nodes // devices)
    slots = devices * capacity
    bf = jnp.bfloat16
    requests, position = call(
        number_requests,
        [
            jax.ShapeDtypeStruct((devices, capacity), jnp.int32),
            jax.ShapeDtypeStruct((1, nodes), jnp.int32),
        ],
        0,
        2,
        limit=56 << 20,
    )(source_part.reshape(1, nodes), source_row.reshape(1, nodes))
    wanted = lax.all_to_all(requests, AXES, split_axis=0, concat_axis=0, tiled=True)
    anywhere = pl.BlockSpec(memory_space=pl.ANY)
    vmem = pl.BlockSpec(memory_space=pltpu.VMEM)
    smem = pl.BlockSpec(memory_space=pltpu.SMEM)
    found = pl.pallas_call(
        fetch_rows,
        out_shape=jax.ShapeDtypeStruct((slots, width), bf),
        in_specs=[anywhere, anywhere],
        out_specs=anywhere,
        scratch_shapes=[
            pltpu.SMEM(wanted.shape, jnp.int32),
            pltpu.VMEM(features.shape, bf),
            pltpu.VMEM((features.shape[0] * PITCH + 64, 128), jnp.float32),
            pltpu.VMEM((128 * PITCH + 64, 128), jnp.float32),
            pltpu.VMEM((slots, width), bf),
            pltpu.SemaphoreType.DMA,
            pltpu.SemaphoreType.DMA((8,)),
            pltpu.SemaphoreType.DMA((slots // 128,)),
        ],
        compiler_params=pltpu.CompilerParams(vmem_limit_bytes=56 << 20),
    )(wanted, features)
    arrived = lax.all_to_all(found, AXES, split_axis=0, concat_axis=0, tiled=True)
    dense, turned, moved = call(
        build_spread,
        [
            jax.ShapeDtypeStruct((nodes, nodes), bf),
            jax.ShapeDtypeStruct((nodes, nodes), bf),
            jax.ShapeDtypeStruct((nodes, slots), bf),
        ],
        3,
        2,
        cost=pl.CostEstimate(
            flops=2 * nodes * nodes * slots, bytes_accessed=12 << 20, transcendentals=0
        ),
    )(tile_row, tile_col, tile_count, adj_tiles, position)
    padded = jnp.pad(layer_two.T, ((0, 256 - classes), (0, 0)))
    core = lax.rem(lax.axis_index("store"), 2).astype(jnp.int32).reshape(1)
    half = SIDE * WIDTH
    sent, own = pl.pallas_call(
        partial(train, classes=classes),
        out_shape=[
            jax.ShapeDtypeStruct((ROWS, half), bf),
            jax.ShapeDtypeStruct((ROWS, half), bf),
        ],
        in_specs=[smem] + [anywhere] * 7,
        out_specs=[anywhere] * 2,
        scratch_shapes=[
            pltpu.VMEM((slots, width), bf),
            pltpu.VMEM((nodes, slots), bf),
            pltpu.VMEM((nodes, nodes), bf),
            pltpu.VMEM((nodes, nodes), bf),
            pltpu.VMEM((width, hidden), bf),
            pltpu.VMEM((256, hidden), bf),
            pltpu.VMEM((nodes, 1), jnp.int32),
            pltpu.VMEM((ROWS, half), bf),
            pltpu.VMEM((ROWS, half), bf),
            pltpu.VMEM((width, nodes), bf),
            pltpu.VMEM((nodes, hidden), jnp.float32),
            pltpu.VMEM((nodes, hidden), bf),
            pltpu.VMEM((nodes, hidden), bf),
            pltpu.VMEM((nodes, 256), bf),
            pltpu.VMEM((256, nodes), bf),
            pltpu.SemaphoreType.DMA((13,)),
            pltpu.SemaphoreType.DMA((2,)),
        ],
        compiler_params=pltpu.CompilerParams(vmem_limit_bytes=56 << 20),
        cost_estimate=pl.CostEstimate(
            flops=12 * nodes * nodes * hidden, bytes_accessed=16 << 20, transcendentals=nodes * hidden
        ),
    )(
        core,
        arrived.reshape(slots, width),
        moved,
        dense,
        turned,
        layer_one,
        padded,
        labels.reshape(nodes, 1),
    )
    grad_one, grad_two, loss = sum_over_devices(sent, own, width, classes)
    return (grad_one, grad_two.T, loss.reshape(()))


def solution(mesh):
    return jax.shard_map(
        on_device,
        mesh=mesh,
        in_specs=(
            P(("store", "batch"), None),
            P(("store", "batch")),
            P(("store", "batch")),
            P(("store", "batch"), None, None),
            P(("store", "batch")),
            P(("store", "batch")),
            P(("store", "batch")),
            P(("store", "batch")),
            P(),
            P(),
        ),
        out_specs=(P(), P(), P()),
        check_vma=False,
    )
```

```python
from functools import partial

import jax
import jax.numpy as jnp
from jax import lax
from jax.experimental import pallas as pl
from jax.experimental.pallas import tpu as pltpu
from jax.sharding import PartitionSpec as P

AXES = ("store", "batch")
SIDE = 4
WIDTH = 128
LOSS_ROW = 921
ROWS = 928
PITCH = 7


def flat(x, y, z, core):
    return ((x * SIDE + z) * 2 + core) * SIDE + y


def shift_pairs(axes, offset):
    pairs = []
    for x in range(SIDE):
        for y in range(SIDE):
            for z in range(SIDE):
                for core in range(2):
                    place = [x, y, z]
                    place[axes[core]] = (place[axes[core]] + offset) % SIDE
                    pairs.append((flat(x, y, z, core), flat(*place, core)))
    return pairs


def swap_pairs():
    return [
        (flat(x, y, z, core), flat(x, y, z, 1 - core))
        for x in range(SIDE)
        for y in range(SIDE)
        for z in range(SIDE)
        for core in range(2)
    ]


FIRST, SECOND, THIRD = (0, 1), (1, 2), (2, 0)


def split_loss(total):
    tail = total[ROWS - 8 :, :]
    row = lax.broadcasted_iota(jnp.int32, tail.shape, 0)
    lane = lax.broadcasted_iota(jnp.int32, tail.shape, 1)
    here = row == LOSS_ROW - (ROWS - 8)
    loss = jnp.sum(jnp.where(here & (lane < 3), tail, 0.0), axis=1, keepdims=True)
    high = loss.astype(jnp.bfloat16).astype(jnp.float32)
    middle = (loss - high).astype(jnp.bfloat16).astype(jnp.float32)
    low = (loss - high - middle).astype(jnp.bfloat16).astype(jnp.float32)
    parts = jnp.where(lane == 0, high, jnp.where(lane == 1, middle, jnp.where(lane == 2, low, 0.0)))
    return jnp.where(here, parts, tail)


def store_total(out, columns, total):
    out[: ROWS - 16, columns] = total[: ROWS - 16].astype(jnp.bfloat16)
    last = jnp.concatenate([total[ROWS - 16 : ROWS - 8], split_loss(total)], axis=0)
    out[ROWS - 16 :, columns] = last.astype(jnp.bfloat16)


def pick_blocks(place, far, near, arrival):
    copies = []
    for index, offset in enumerate((1, 2, 3, 0)):
        block = lax.rem(place[0] + offset, SIDE)
        columns = pl.ds(pl.multiple_of(block * WIDTH, WIDTH), WIDTH)
        copies.append(
            pltpu.make_async_copy(far.at[:, columns], near.at[index], arrival.at[index])
        )
        copies[-1].start()
    for copy in copies:
        copy.wait()


def first_add(place, own, arrived, keep, one, two, three):
    for index, (offset, out) in enumerate(((1, one), (2, two), (3, three), (0, keep))):
        block = lax.rem(place[0] + offset, SIDE)
        columns = pl.ds(pl.multiple_of(block * WIDTH, WIDTH), WIDTH)
        total = own[index].astype(jnp.float32) + arrived[:, columns].astype(jnp.float32)
        store_total(out, slice(None), total)


def four_add(own, one, two, three, out):
    total = (own[...].astype(jnp.float32) + two[...].astype(jnp.float32)) + (
        one[...].astype(jnp.float32) + three[...].astype(jnp.float32)
    )
    store_total(out, slice(None), total)


def place_blocks(place, own, one, two, three, out):
    for offset, block in ((0, own), (1, one), (2, two), (3, three)):
        at = lax.rem(place[0] + SIDE - offset, SIDE)
        out[:, pl.ds(pl.multiple_of(at * WIDTH, WIDTH), WIDTH)] = block[...]


def write_half(at, part, one_far, two_far, one, two, leaving):
    half = part.shape[1]
    features = one.shape[0]
    classes = two.shape[0]
    columns = pl.ds(pl.multiple_of(at * half, half), half)
    two[...] = part[features:, :].astype(jnp.float32)[:classes]
    copies = [pltpu.make_async_copy(two, two_far.at[:, columns], leaving.at[0])]
    copies[0].start()
    step = features // 4
    for index in range(4):
        rows = slice(index * step, (index + 1) * step)
        one[rows, :] = part[rows, :].astype(jnp.float32)
        lines = pl.ds(index * step, step)
        copies.append(
            pltpu.make_async_copy(
                one.at[lines, :], one_far.at[lines, columns], leaving.at[index + 1]
            )
        )
        copies[-1].start()
    return copies


def read_loss(part):
    tail = part[ROWS - 16 :, :WIDTH].astype(jnp.float32)
    row = lax.broadcasted_iota(jnp.int32, tail.shape, 0)
    lane = lax.broadcasted_iota(jnp.int32, tail.shape, 1)
    mine = (row == LOSS_ROW - (ROWS - 16)) & (lane < 3)
    return jnp.sum(jnp.sum(jnp.where(mine, tail, 0.0), axis=1, keepdims=True), axis=0, keepdims=True)


def write_own(core, own, one_far, two_far, one, two, leaving):
    for copy in write_half(core[0], own, one_far, two_far, one, two, leaving):
        copy.wait()


def write_other(core, own, other, one_in, two_in, one_far, two_far, loss, one, two, leaving):
    copies = write_half(1 - core[0], other, one_far, two_far, one, two, leaving)
    loss[...] = jnp.where(core[0] == 0, read_loss(own), read_loss(other))
    for copy in copies:
        copy.wait()


def call(kernel, outs, scalars=0, arrays=0, limit=16 << 20, cost=None, scratch=()):
    vmem = pl.BlockSpec(memory_space=pltpu.VMEM)
    smem = pl.BlockSpec(memory_space=pltpu.SMEM)
    return pl.pallas_call(
        kernel,
        out_shape=outs,
        in_specs=[smem] * scalars + [vmem] * arrays,
        out_specs=jax.tree.map(lambda _: vmem, outs),
        scratch_shapes=list(scratch),
        compiler_params=pltpu.CompilerParams(vmem_limit_bytes=limit),
        cost_estimate=cost,
    )


def sum_over_devices(sent, own, features, classes):
    store, batch = lax.axis_index("store"), lax.axis_index("batch")
    core = lax.rem(store, 2)
    place = jnp.where(core == 0, store // (2 * SIDE), batch).astype(jnp.int32).reshape(1)
    core = core.astype(jnp.int32).reshape(1)
    bf = jnp.bfloat16
    block = jax.ShapeDtypeStruct((ROWS, WIDTH), bf)
    arrived = lax.ppermute(sent, AXES, swap_pairs())
    picked = pl.pallas_call(
        pick_blocks,
        out_shape=jax.ShapeDtypeStruct((SIDE, ROWS, WIDTH), bf),
        in_specs=[pl.BlockSpec(memory_space=pltpu.SMEM), pl.BlockSpec(memory_space=pl.ANY)],
        out_specs=pl.BlockSpec(memory_space=pltpu.VMEM),
        scratch_shapes=[pltpu.SemaphoreType.DMA((SIDE,))],
        compiler_params=pltpu.CompilerParams(vmem_limit_bytes=16 << 20),
    )(place, own)
    keep, *parts = call(first_add, [block] * 4, 1, 2)(place, picked, arrived)
    got = [lax.ppermute(part, AXES, shift_pairs(FIRST, k + 1)) for k, part in enumerate(parts)]
    total = call(four_add, block, 0, 4)(keep, *got)
    for axes in (SECOND, THIRD):
        got = [lax.ppermute(total, AXES, shift_pairs(axes, k)) for k in (1, 2, 3)]
        total = call(four_add, block, 0, 4)(total, *got)
    got = [lax.ppermute(total, AXES, shift_pairs(FIRST, k)) for k in (1, 2, 3)]
    strip = call(place_blocks, jax.ShapeDtypeStruct((ROWS, SIDE * WIDTH), bf), 1, 4)(
        place, total, *got
    )
    other = lax.ppermute(strip, AXES, swap_pairs())
    half = SIDE * WIDTH
    grads = [
        jax.ShapeDtypeStruct((features, 2 * half), jnp.float32),
        jax.ShapeDtypeStruct((classes, 2 * half), jnp.float32),
    ]
    anywhere = pl.BlockSpec(memory_space=pl.ANY)
    vmem = pl.BlockSpec(memory_space=pltpu.VMEM)
    smem = pl.BlockSpec(memory_space=pltpu.SMEM)
    scratch = [
        pltpu.VMEM((features, half), jnp.float32),
        pltpu.VMEM((classes, half), jnp.float32),
        pltpu.SemaphoreType.DMA((5,)),
    ]
    params = pltpu.CompilerParams(vmem_limit_bytes=16 << 20)
    grad_one, grad_two = pl.pallas_call(
        write_own,
        out_shape=grads,
        in_specs=[smem, vmem],
        out_specs=[anywhere] * 2,
        scratch_shapes=scratch,
        compiler_params=params,
    )(core, strip)
    return pl.pallas_call(
        write_other,
        out_shape=[*grads, jax.ShapeDtypeStruct((1, 1), jnp.float32)],
        in_specs=[smem, vmem, vmem, anywhere, anywhere],
        out_specs=[anywhere, anywhere, vmem],
        scratch_shapes=scratch,
        input_output_aliases={3: 0, 4: 1},
        compiler_params=params,
    )(core, strip, other, grad_one, grad_two)


def number_requests(parts, rows, requests, position):
    devices, capacity = requests.shape
    nodes = parts.shape[1]
    piece = 128
    owner = lax.broadcasted_iota(jnp.int32, (devices, nodes), 0)
    mine = jnp.where(owner == parts[...], 1.0, 0.0)
    line = lax.broadcasted_iota(jnp.int32, (piece, piece), 0)
    lane = lax.broadcasted_iota(jnp.int32, (piece, piece), 1)
    earlier = jnp.where(line < lane, 1.0, 0.0).astype(jnp.bfloat16)
    seen = jnp.zeros((devices, 1), jnp.float32)
    slots = []
    for start in range(0, nodes, piece):
        here = mine[:, start : start + piece]
        rank = jnp.dot(here.astype(jnp.bfloat16), earlier, preferred_element_type=jnp.float32)
        slots.append(jnp.sum(here * (rank + seen), axis=0, keepdims=True))
        seen = seen + jnp.sum(here, axis=1, keepdims=True)
    slot = jnp.concatenate(slots, axis=1).astype(jnp.int32)
    position[...] = parts[...] * capacity + slot
    placed = lax.broadcasted_iota(jnp.int32, (capacity, nodes), 0) == slot
    total = jnp.zeros((devices, capacity), jnp.float32)
    for scale, digit in ((64.0, lax.shift_right_logical(rows[...], 6)), (1.0, rows[...] & 63)):
        values = jnp.where(placed, digit.astype(jnp.float32), 0.0).astype(jnp.bfloat16)
        total += scale * lax.dot_general(
            mine.astype(jnp.bfloat16),
            values,
            (((1,), (1,)), ((), ())),
            preferred_element_type=jnp.float32,
        )
    requests[...] = total.astype(jnp.int32)


def fetch_rows(wanted_far, table, far, wanted, narrow, wide, some, out, listed, arrival, leaving):
    stored, width = table.shape
    pieces = width // 128
    step = stored // arrival.shape[0]

    def load(block):
        rows = pl.ds(block * step, step)
        return pltpu.make_async_copy(table.at[rows, :], narrow.at[rows, :], arrival.at[block])

    listing = pltpu.make_async_copy(wanted_far, wanted, listed)
    listing.start()
    for block in range(arrival.shape[0]):
        load(block).start()
    for block in range(arrival.shape[0]):
        load(block).wait()

        @pl.loop(0, step // 64)
        def _(part):
            start = pl.multiple_of(block * step + part * 64, 64)
            values = narrow[pl.ds(start, 64), :].astype(jnp.float32)
            for line in range(0, 64, 8):
                for piece in range(pieces):
                    lines = pl.ds((start + line) * PITCH + piece, 8, stride=PITCH)
                    wide[lines, :] = values[line : line + 8, piece * 128 : (piece + 1) * 128]

    listing.wait()
    devices, capacity = wanted.shape
    group = out.shape[0] // leaving.shape[0]
    owners = group // capacity

    def send(block):
        rows = pl.ds(pl.multiple_of(block * group, group), group)
        return pltpu.make_async_copy(out.at[rows, :], far.at[rows, :], leaving.at[block])

    @pl.loop(0, devices // owners)
    def _(block):
        for line in range(group):
            row = wanted[block * owners + line // capacity, line % capacity]
            some[pl.ds(line * PITCH, pieces), :] = wide[pl.ds(row * PITCH, pieces), :]
        for line in range(0, group, 16):
            rows = pl.ds(pl.multiple_of(block * group + line, 16), 16)
            for piece in range(pieces):
                halves = [
                    some[pl.ds((line + half) * PITCH + piece, 8, stride=PITCH), :] for half in (0, 8)
                ]
                out[rows, piece * 128 : (piece + 1) * 128] = jnp.concatenate(halves, axis=0).astype(
                    jnp.bfloat16
                )
        send(block).start()

    @pl.loop(0, devices // owners)
    def _(block):
        send(block).wait()


def build_spread(row, column, count, tiles, position, dense, moved):
    nodes = dense.shape[0]
    tile = tiles.shape[1]
    dense[...] = jnp.zeros_like(dense)

    @pl.loop(0, count[0])
    def _(t):
        at_row = pl.ds(pl.multiple_of(row[t] * tile, tile), tile)
        at_column = pl.ds(pl.multiple_of(column[t] * tile, tile), tile)
        dense[at_row, at_column] = tiles[t]

    width = 256

    @pl.loop(0, moved.shape[1] // width)
    def _(step):
        start = pl.multiple_of(step * width, width)
        slot = lax.broadcasted_iota(jnp.int32, (width, nodes), 0) + start
        chosen = jnp.where(slot == position[...], 1.0, 0.0).astype(jnp.bfloat16)
        moved[:, pl.ds(start, width)] = lax.dot_general(
            dense[...], chosen, (((1,), (1,)), ((), ())), preferred_element_type=jnp.float32
        ).astype(jnp.bfloat16)


def train(
    core,
    arrived_far,
    moved_far,
    dense_far,
    one_far,
    two_far,
    labels_far,
    sent_far,
    own_far,
    arrived,
    moved,
    dense,
    layer_one,
    layer_two,
    labels,
    sent,
    own,
    mixed_turned,
    slope,
    hidden,
    scored,
    upstream_turned,
    back_turned,
    arrival,
    leaving,
    *,
    classes,
):
    nodes = dense.shape[0]
    features = mixed_turned.shape[0]
    step = 256
    tiles = range(0, nodes, step)

    def load(index, far, near):
        return pltpu.make_async_copy(far, near, arrival.at[index])

    part = arrived.shape[0] // SIDE
    get_arrived = [
        load(at, arrived_far.at[pl.ds(at * part, part), :], arrived.at[pl.ds(at * part, part), :])
        for at in range(SIDE)
    ]
    get_one = load(4, one_far, layer_one)
    get_dense = load(5, dense_far, dense)
    get_two = load(6, two_far, layer_two)
    get_labels = load(7, labels_far, labels)
    get_moved = [
        load(8 + at, moved_far.at[pl.ds(start, step), :], moved.at[pl.ds(start, step), :])
        for at, start in enumerate(tiles)
    ]
    get_moved[0].start()
    for copy in get_arrived:
        copy.start()
    get_one.start()
    get_two.start()
    get_moved[0].wait()
    for at, start in enumerate(tiles):
        rows = slice(start, start + step)
        if at > 0:
            get_moved[at].wait()
            mixed = jnp.dot(moved[rows, :], arrived[...], preferred_element_type=jnp.float32)
        else:
            mixed = 0.0
            for index, copy in enumerate(get_arrived):
                copy.wait()
                slots = slice(index * part, (index + 1) * part)
                mixed += jnp.dot(
                    moved[rows, slots], arrived[slots, :], preferred_element_type=jnp.float32
                )
            for copy in get_moved[1:]:
                copy.start()
        mixed = mixed.astype(jnp.bfloat16)
        mixed_turned[:, rows] = mixed.T
        if at == 0:
            get_one.wait()
            get_two.wait()
            get_dense.start()
            get_labels.start()
        before = jnp.dot(mixed, layer_one[...], preferred_element_type=jnp.float32)
        square = before * before
        rate = 0.7978845608028654
        bend = jnp.tanh(rate * before * (1.0 + 0.044715 * square))
        rise = 0.5 * (1.0 + bend)
        active = (before * rise).astype(jnp.bfloat16)
        hidden[rows, :] = active
        slope[rows, :] = rise + 0.5 * before * (1.0 - bend * bend) * (
            rate + (3.0 * 0.044715 * rate) * square
        )
        scored[rows, :] = lax.dot_general(
            active, layer_two[...], (((1,), (1,)), ((), ())), preferred_element_type=jnp.float32
        ).astype(jnp.bfloat16)
    get_dense.wait()
    get_labels.wait()
    loss = jnp.zeros((1, 1), jnp.float32)
    for start in tiles:
        rows = slice(start, start + step)
        logits = jnp.dot(dense[rows, :], scored[...], preferred_element_type=jnp.float32)
        lane = lax.broadcasted_iota(jnp.int32, logits.shape, 1)
        logits = jnp.where(lane < classes, logits, -jnp.inf)
        largest = jnp.max(logits, axis=1, keepdims=True)
        logsum = jnp.log(jnp.sum(jnp.exp(logits - largest), axis=1, keepdims=True)) + largest
        truth = lane == labels[rows, :]
        picked = jnp.sum(jnp.where(truth, logits, 0.0), axis=1, keepdims=True)
        loss += jnp.sum(logsum - picked, axis=0, keepdims=True)
        gap = (jnp.exp(logits - logsum) - jnp.where(truth, 1.0, 0.0)) * (1.0 / nodes)
        upstream_turned[:, rows] = gap.astype(jnp.bfloat16).T
    loss = loss * (1.0 / nodes)
    high = loss.astype(jnp.bfloat16).astype(jnp.float32)
    middle = (loss - high).astype(jnp.bfloat16).astype(jnp.float32)
    low = loss - high - middle
    half = SIDE * WIDTH
    back_turned[...] = jnp.dot(
        upstream_turned[...], dense[...], preferred_element_type=jnp.float32
    ).astype(jnp.bfloat16)
    back = back_turned[...].T
    stores = []
    for offset, out, far in ((1, sent, sent_far), (0, own, own_far)):
        side = lax.rem(core[0] + offset, 2)
        columns = pl.ds(pl.multiple_of(side * half, half), half)
        second = jnp.dot(
            back_turned[: ROWS - features, :], hidden[:, columns], preferred_element_type=jnp.float32
        )
        row = lax.broadcasted_iota(jnp.int32, second.shape, 0)
        lane = lax.broadcasted_iota(jnp.int32, second.shape, 1)
        here = (row == LOSS_ROW - features) & (side == 0)
        second += jnp.where(here & (lane == 0), high, 0.0)
        second += jnp.where(here & (lane == 1), middle, 0.0)
        second += jnp.where(here & (lane == 2), low, 0.0)
        out[features:, :] = second.astype(out.dtype)
        back_hidden = jnp.dot(back, layer_two[:, columns], preferred_element_type=jnp.float32)
        back_before = (slope[:, columns] * back_hidden).astype(jnp.bfloat16)
        out[:features, :] = jnp.dot(
            mixed_turned[...], back_before, preferred_element_type=jnp.float32
        ).astype(out.dtype)
        stores.append(pltpu.make_async_copy(out, far, leaving.at[len(stores)]))
        stores[-1].start()
    for copy in stores:
        copy.wait()


def on_device(
    features,
    source_part,
    source_row,
    adj_tiles,
    tile_row,
    tile_col,
    tile_count,
    labels,
    layer_one,
    layer_two,
):
    devices = lax.axis_size(AXES)
    nodes = source_part.shape[0]
    width, hidden = layer_one.shape
    classes = layer_two.shape[1]
    capacity = max(2, 2 * nodes // devices)
    slots = devices * capacity
    bf = jnp.bfloat16
    requests, position = call(
        number_requests,
        [
            jax.ShapeDtypeStruct((devices, capacity), jnp.int32),
            jax.ShapeDtypeStruct((1, nodes), jnp.int32),
        ],
        0,
        2,
        limit=56 << 20,
    )(source_part.reshape(1, nodes), source_row.reshape(1, nodes))
    wanted = lax.all_to_all(requests, AXES, split_axis=0, concat_axis=0, tiled=True)
    anywhere = pl.BlockSpec(memory_space=pl.ANY)
    vmem = pl.BlockSpec(memory_space=pltpu.VMEM)
    smem = pl.BlockSpec(memory_space=pltpu.SMEM)
    found = pl.pallas_call(
        fetch_rows,
        out_shape=jax.ShapeDtypeStruct((slots, width), bf),
        in_specs=[anywhere, anywhere],
        out_specs=anywhere,
        scratch_shapes=[
            pltpu.SMEM(wanted.shape, jnp.int32),
            pltpu.VMEM(features.shape, bf),
            pltpu.VMEM((features.shape[0] * PITCH + 64, 128), jnp.float32),
            pltpu.VMEM((128 * PITCH + 64, 128), jnp.float32),
            pltpu.VMEM((slots, width), bf),
            pltpu.SemaphoreType.DMA,
            pltpu.SemaphoreType.DMA((8,)),
            pltpu.SemaphoreType.DMA((slots // 128,)),
        ],
        compiler_params=pltpu.CompilerParams(vmem_limit_bytes=56 << 20),
    )(wanted, features)
    arrived = lax.all_to_all(found, AXES, split_axis=0, concat_axis=0, tiled=True)
    dense, moved = call(
        build_spread,
        [
            jax.ShapeDtypeStruct((nodes, nodes), bf),
            jax.ShapeDtypeStruct((nodes, slots), bf),
        ],
        3,
        2,
        cost=pl.CostEstimate(
            flops=2 * nodes * nodes * slots, bytes_accessed=12 << 20, transcendentals=0
        ),
    )(tile_row, tile_col, tile_count, adj_tiles, position)
    padded = jnp.pad(layer_two.T, ((0, 256 - classes), (0, 0)))
    core = lax.rem(lax.axis_index("store"), 2).astype(jnp.int32).reshape(1)
    half = SIDE * WIDTH
    sent, own = pl.pallas_call(
        partial(train, classes=classes),
        out_shape=[
            jax.ShapeDtypeStruct((ROWS, half), bf),
            jax.ShapeDtypeStruct((ROWS, half), bf),
        ],
        in_specs=[smem] + [anywhere] * 6,
        out_specs=[anywhere] * 2,
        scratch_shapes=[
            pltpu.VMEM((slots, width), bf),
            pltpu.VMEM((nodes, slots), bf),
            pltpu.VMEM((nodes, nodes), bf),
            pltpu.VMEM((width, hidden), bf),
            pltpu.VMEM((256, hidden), bf),
            pltpu.VMEM((nodes, 1), jnp.int32),
            pltpu.VMEM((ROWS, half), bf),
            pltpu.VMEM((ROWS, half), bf),
            pltpu.VMEM((width, nodes), bf),
            pltpu.VMEM((nodes, hidden), jnp.float32),
            pltpu.VMEM((nodes, hidden), bf),
            pltpu.VMEM((nodes, 256), bf),
            pltpu.VMEM((256, nodes), bf),
            pltpu.VMEM((256, nodes), bf),
            pltpu.SemaphoreType.DMA((12,)),
            pltpu.SemaphoreType.DMA((2,)),
        ],
        compiler_params=pltpu.CompilerParams(vmem_limit_bytes=56 << 20),
        cost_estimate=pl.CostEstimate(
            flops=12 * nodes * nodes * hidden, bytes_accessed=16 << 20, transcendentals=nodes * hidden
        ),
    )(
        core,
        arrived.reshape(slots, width),
        moved,
        dense,
        layer_one,
        padded,
        labels.reshape(nodes, 1),
    )
    grad_one, grad_two, loss = sum_over_devices(sent, own, width, classes)
    return (grad_one, grad_two.T, loss.reshape(()))


def solution(mesh):
    return jax.shard_map(
        on_device,
        mesh=mesh,
        in_specs=(
            P(("store", "batch"), None),
            P(("store", "batch")),
            P(("store", "batch")),
            P(("store", "batch"), None, None),
            P(("store", "batch")),
            P(("store", "batch")),
            P(("store", "batch")),
            P(("store", "batch")),
            P(),
            P(),
        ),
        out_specs=(P(), P(), P()),
        check_vma=False,
    )
```

```python
from functools import partial

import jax
import jax.numpy as jnp
from jax import lax
from jax.experimental import pallas as pl
from jax.experimental.pallas import tpu as pltpu
from jax.sharding import PartitionSpec as P

AXES = ("store", "batch")
SIDE = 4
WIDTH = 128
LOSS_ROW = 921
ROWS = 928
PITCH = 7


def flat(x, y, z, core):
    return ((x * SIDE + z) * 2 + core) * SIDE + y


def shift_pairs(axes, offset):
    pairs = []
    for x in range(SIDE):
        for y in range(SIDE):
            for z in range(SIDE):
                for core in range(2):
                    place = [x, y, z]
                    place[axes[core]] = (place[axes[core]] + offset) % SIDE
                    pairs.append((flat(x, y, z, core), flat(*place, core)))
    return pairs


def swap_pairs():
    return [
        (flat(x, y, z, core), flat(x, y, z, 1 - core))
        for x in range(SIDE)
        for y in range(SIDE)
        for z in range(SIDE)
        for core in range(2)
    ]


FIRST, SECOND, THIRD = (0, 1), (1, 2), (2, 0)


def split_loss(total):
    tail = total[ROWS - 8 :, :]
    row = lax.broadcasted_iota(jnp.int32, tail.shape, 0)
    lane = lax.broadcasted_iota(jnp.int32, tail.shape, 1)
    here = row == LOSS_ROW - (ROWS - 8)
    loss = jnp.sum(jnp.where(here & (lane < 3), tail, 0.0), axis=1, keepdims=True)
    high = loss.astype(jnp.bfloat16).astype(jnp.float32)
    middle = (loss - high).astype(jnp.bfloat16).astype(jnp.float32)
    low = (loss - high - middle).astype(jnp.bfloat16).astype(jnp.float32)
    parts = jnp.where(lane == 0, high, jnp.where(lane == 1, middle, jnp.where(lane == 2, low, 0.0)))
    return jnp.where(here, parts, tail)


def store_total(out, columns, total):
    out[: ROWS - 16, columns] = total[: ROWS - 16].astype(jnp.bfloat16)
    last = jnp.concatenate([total[ROWS - 16 : ROWS - 8], split_loss(total)], axis=0)
    out[ROWS - 16 :, columns] = last.astype(jnp.bfloat16)


def first_add(place, own, arrived, keep, one, two, three):
    for offset, out in ((1, one), (2, two), (3, three), (0, keep)):
        block = lax.rem(place[0] + offset, SIDE)
        columns = pl.ds(pl.multiple_of(block * WIDTH, WIDTH), WIDTH)
        total = own[:, columns].astype(jnp.float32) + arrived[:, columns].astype(jnp.float32)
        store_total(out, slice(None), total)


def four_add(own, one, two, three, out):
    total = (own[...].astype(jnp.float32) + two[...].astype(jnp.float32)) + (
        one[...].astype(jnp.float32) + three[...].astype(jnp.float32)
    )
    store_total(out, slice(None), total)


def place_blocks(place, own, one, two, three, out):
    for offset, block in ((0, own), (1, one), (2, two), (3, three)):
        at = lax.rem(place[0] + SIDE - offset, SIDE)
        out[:, pl.ds(pl.multiple_of(at * WIDTH, WIDTH), WIDTH)] = block[...]


def write_half(at, part, one_far, two_far, one, two, leaving):
    half = part.shape[1]
    features = one.shape[0]
    classes = two.shape[0]
    columns = pl.ds(pl.multiple_of(at * half, half), half)
    two[...] = part[features:, :].astype(jnp.float32)[:classes]
    copies = [pltpu.make_async_copy(two, two_far.at[:, columns], leaving.at[0])]
    copies[0].start()
    step = features // 4
    for index in range(4):
        rows = slice(index * step, (index + 1) * step)
        one[rows, :] = part[rows, :].astype(jnp.float32)
        lines = pl.ds(index * step, step)
        copies.append(
            pltpu.make_async_copy(
                one.at[lines, :], one_far.at[lines, columns], leaving.at[index + 1]
            )
        )
        copies[-1].start()
    return copies


def read_loss(part):
    tail = part[ROWS - 16 :, :WIDTH].astype(jnp.float32)
    row = lax.broadcasted_iota(jnp.int32, tail.shape, 0)
    lane = lax.broadcasted_iota(jnp.int32, tail.shape, 1)
    mine = (row == LOSS_ROW - (ROWS - 16)) & (lane < 3)
    return jnp.sum(jnp.sum(jnp.where(mine, tail, 0.0), axis=1, keepdims=True), axis=0, keepdims=True)


def write_own(core, own, one_far, two_far, one, two, leaving):
    for copy in write_half(core[0], own, one_far, two_far, one, two, leaving):
        copy.wait()


def write_other(core, own, other, one_in, two_in, one_far, two_far, loss, one, two, leaving):
    copies = write_half(1 - core[0], other, one_far, two_far, one, two, leaving)
    loss[...] = jnp.where(core[0] == 0, read_loss(own), read_loss(other))
    for copy in copies:
        copy.wait()


def call(kernel, outs, scalars=0, arrays=0, limit=16 << 20, cost=None, scratch=()):
    vmem = pl.BlockSpec(memory_space=pltpu.VMEM)
    smem = pl.BlockSpec(memory_space=pltpu.SMEM)
    return pl.pallas_call(
        kernel,
        out_shape=outs,
        in_specs=[smem] * scalars + [vmem] * arrays,
        out_specs=jax.tree.map(lambda _: vmem, outs),
        scratch_shapes=list(scratch),
        compiler_params=pltpu.CompilerParams(vmem_limit_bytes=limit),
        cost_estimate=cost,
    )


def sum_over_devices(sent, own, features, classes):
    store, batch = lax.axis_index("store"), lax.axis_index("batch")
    core = lax.rem(store, 2)
    place = jnp.where(core == 0, store // (2 * SIDE), batch).astype(jnp.int32).reshape(1)
    core = core.astype(jnp.int32).reshape(1)
    bf = jnp.bfloat16
    block = jax.ShapeDtypeStruct((ROWS, WIDTH), bf)
    arrived = lax.ppermute(sent, AXES, swap_pairs())
    keep, *parts = call(first_add, [block] * 4, 1, 2)(place, own, arrived)
    got = [lax.ppermute(part, AXES, shift_pairs(FIRST, k + 1)) for k, part in enumerate(parts)]
    total = call(four_add, block, 0, 4)(keep, *got)
    for axes in (SECOND, THIRD):
        got = [lax.ppermute(total, AXES, shift_pairs(axes, k)) for k in (1, 2, 3)]
        total = call(four_add, block, 0, 4)(total, *got)
    got = [lax.ppermute(total, AXES, shift_pairs(FIRST, k)) for k in (1, 2, 3)]
    strip = call(place_blocks, jax.ShapeDtypeStruct((ROWS, SIDE * WIDTH), bf), 1, 4)(
        place, total, *got
    )
    other = lax.ppermute(strip, AXES, swap_pairs())
    half = SIDE * WIDTH
    grads = [
        jax.ShapeDtypeStruct((features, 2 * half), jnp.float32),
        jax.ShapeDtypeStruct((classes, 2 * half), jnp.float32),
    ]
    anywhere = pl.BlockSpec(memory_space=pl.ANY)
    vmem = pl.BlockSpec(memory_space=pltpu.VMEM)
    smem = pl.BlockSpec(memory_space=pltpu.SMEM)
    scratch = [
        pltpu.VMEM((features, half), jnp.float32),
        pltpu.VMEM((classes, half), jnp.float32),
        pltpu.SemaphoreType.DMA((5,)),
    ]
    params = pltpu.CompilerParams(vmem_limit_bytes=16 << 20)
    grad_one, grad_two = pl.pallas_call(
        write_own,
        out_shape=grads,
        in_specs=[smem, vmem],
        out_specs=[anywhere] * 2,
        scratch_shapes=scratch,
        compiler_params=params,
    )(core, strip)
    return pl.pallas_call(
        write_other,
        out_shape=[*grads, jax.ShapeDtypeStruct((1, 1), jnp.float32)],
        in_specs=[smem, vmem, vmem, anywhere, anywhere],
        out_specs=[anywhere, anywhere, vmem],
        scratch_shapes=scratch,
        input_output_aliases={3: 0, 4: 1},
        compiler_params=params,
    )(core, strip, other, grad_one, grad_two)


def number_requests(parts, rows, requests, position):
    devices, capacity = requests.shape
    nodes = parts.shape[1]
    piece = 128
    owner = lax.broadcasted_iota(jnp.int32, (devices, nodes), 0)
    mine = jnp.where(owner == parts[...], 1.0, 0.0)
    line = lax.broadcasted_iota(jnp.int32, (piece, piece), 0)
    lane = lax.broadcasted_iota(jnp.int32, (piece, piece), 1)
    earlier = jnp.where(line < lane, 1.0, 0.0).astype(jnp.bfloat16)
    seen = jnp.zeros((devices, 1), jnp.float32)
    slots = []
    for start in range(0, nodes, piece):
        here = mine[:, start : start + piece]
        rank = jnp.dot(here.astype(jnp.bfloat16), earlier, preferred_element_type=jnp.float32)
        slots.append(jnp.sum(here * (rank + seen), axis=0, keepdims=True))
        seen = seen + jnp.sum(here, axis=1, keepdims=True)
    slot = jnp.concatenate(slots, axis=1).astype(jnp.int32)
    position[...] = parts[...] * capacity + slot
    placed = lax.broadcasted_iota(jnp.int32, (capacity, nodes), 0) == slot
    total = jnp.zeros((devices, capacity), jnp.float32)
    for scale, digit in ((64.0, lax.shift_right_logical(rows[...], 6)), (1.0, rows[...] & 63)):
        values = jnp.where(placed, digit.astype(jnp.float32), 0.0).astype(jnp.bfloat16)
        total += scale * lax.dot_general(
            mine.astype(jnp.bfloat16),
            values,
            (((1,), (1,)), ((), ())),
            preferred_element_type=jnp.float32,
        )
    requests[...] = total.astype(jnp.int32)


def fetch_rows(wanted_far, table, far, wanted, narrow, wide, some, out, listed, arrival, leaving):
    stored, width = table.shape
    pieces = width // 128
    step = stored // arrival.shape[0]

    def load(block):
        rows = pl.ds(block * step, step)
        return pltpu.make_async_copy(table.at[rows, :], narrow.at[rows, :], arrival.at[block])

    listing = pltpu.make_async_copy(wanted_far, wanted, listed)
    listing.start()
    for block in range(arrival.shape[0]):
        load(block).start()
    for block in range(arrival.shape[0]):
        load(block).wait()

        @pl.loop(0, step // 64)
        def _(part):
            start = pl.multiple_of(block * step + part * 64, 64)
            values = narrow[pl.ds(start, 64), :].astype(jnp.float32)
            for line in range(0, 64, 8):
                for piece in range(pieces):
                    lines = pl.ds((start + line) * PITCH + piece, 8, stride=PITCH)
                    wide[lines, :] = values[line : line + 8, piece * 128 : (piece + 1) * 128]

    listing.wait()
    devices, capacity = wanted.shape
    group = out.shape[0] // leaving.shape[0]
    owners = group // capacity

    def send(block):
        rows = pl.ds(pl.multiple_of(block * group, group), group)
        return pltpu.make_async_copy(out.at[rows, :], far.at[rows, :], leaving.at[block])

    @pl.loop(0, devices // owners)
    def _(block):
        for line in range(group):
            row = wanted[block * owners + line // capacity, line % capacity]
            some[pl.ds(line * PITCH, pieces), :] = wide[pl.ds(row * PITCH, pieces), :]
        for line in range(0, group, 16):
            rows = pl.ds(pl.multiple_of(block * group + line, 16), 16)
            for piece in range(pieces):
                halves = [
                    some[pl.ds((line + half) * PITCH + piece, 8, stride=PITCH), :] for half in (0, 8)
                ]
                out[rows, piece * 128 : (piece + 1) * 128] = jnp.concatenate(halves, axis=0).astype(
                    jnp.bfloat16
                )
        send(block).start()

    @pl.loop(0, devices // owners)
    def _(block):
        send(block).wait()


def build_spread(row, column, count, tiles, position, dense, moved):
    nodes = dense.shape[0]
    tile = tiles.shape[1]
    dense[...] = jnp.zeros_like(dense)

    @pl.loop(0, count[0])
    def _(t):
        at_row = pl.ds(pl.multiple_of(row[t] * tile, tile), tile)
        at_column = pl.ds(pl.multiple_of(column[t] * tile, tile), tile)
        dense[at_row, at_column] = tiles[t]

    width = 256

    @pl.loop(0, moved.shape[1] // width)
    def _(step):
        start = pl.multiple_of(step * width, width)
        slot = lax.broadcasted_iota(jnp.int32, (width, nodes), 0) + start
        chosen = jnp.where(slot == position[...], 1.0, 0.0).astype(jnp.bfloat16)
        moved[:, pl.ds(start, width)] = lax.dot_general(
            dense[...], chosen, (((1,), (1,)), ((), ())), preferred_element_type=jnp.float32
        ).astype(jnp.bfloat16)


def train(
    core,
    arrived_far,
    moved_far,
    dense_far,
    one_far,
    two_far,
    labels_far,
    sent,
    own,
    arrived,
    moved,
    dense,
    layer_one,
    layer_two,
    labels,
    mixed_turned,
    slope,
    hidden,
    scored,
    upstream_turned,
    back_turned,
    arrival,
    *,
    classes,
):
    nodes = dense.shape[0]
    features = mixed_turned.shape[0]
    step = 256
    tiles = range(0, nodes, step)

    def load(index, far, near):
        return pltpu.make_async_copy(far, near, arrival.at[index])

    part = arrived.shape[0] // SIDE
    get_arrived = [
        load(at, arrived_far.at[pl.ds(at * part, part), :], arrived.at[pl.ds(at * part, part), :])
        for at in range(SIDE)
    ]
    get_one = load(4, one_far, layer_one)
    get_dense = load(5, dense_far, dense)
    get_two = load(6, two_far, layer_two)
    get_labels = load(7, labels_far, labels)
    get_moved = [
        load(8 + at, moved_far.at[pl.ds(start, step), :], moved.at[pl.ds(start, step), :])
        for at, start in enumerate(tiles)
    ]
    get_moved[0].start()
    for copy in get_arrived:
        copy.start()
    get_one.start()
    get_two.start()
    get_moved[0].wait()
    for at, start in enumerate(tiles):
        rows = slice(start, start + step)
        if at > 0:
            get_moved[at].wait()
            mixed = jnp.dot(moved[rows, :], arrived[...], preferred_element_type=jnp.float32)
        else:
            mixed = 0.0
            for index, copy in enumerate(get_arrived):
                copy.wait()
                slots = slice(index * part, (index + 1) * part)
                mixed += jnp.dot(
                    moved[rows, slots], arrived[slots, :], preferred_element_type=jnp.float32
                )
            for copy in get_moved[1:]:
                copy.start()
        mixed = mixed.astype(jnp.bfloat16)
        mixed_turned[:, rows] = mixed.T
        if at == 0:
            get_one.wait()
            get_two.wait()
            get_dense.start()
            get_labels.start()
        before = jnp.dot(mixed, layer_one[...], preferred_element_type=jnp.float32)
        square = before * before
        rate = 0.7978845608028654
        bend = jnp.tanh(rate * before * (1.0 + 0.044715 * square))
        rise = 0.5 * (1.0 + bend)
        active = (before * rise).astype(jnp.bfloat16)
        hidden[rows, :] = active
        slope[rows, :] = rise + 0.5 * before * (1.0 - bend * bend) * (
            rate + (3.0 * 0.044715 * rate) * square
        )
        scored[rows, :] = lax.dot_general(
            active, layer_two[...], (((1,), (1,)), ((), ())), preferred_element_type=jnp.float32
        ).astype(jnp.bfloat16)
    get_dense.wait()
    get_labels.wait()
    loss = jnp.zeros((1, 1), jnp.float32)
    for start in tiles:
        rows = slice(start, start + step)
        logits = jnp.dot(dense[rows, :], scored[...], preferred_element_type=jnp.float32)
        lane = lax.broadcasted_iota(jnp.int32, logits.shape, 1)
        logits = jnp.where(lane < classes, logits, -jnp.inf)
        largest = jnp.max(logits, axis=1, keepdims=True)
        logsum = jnp.log(jnp.sum(jnp.exp(logits - largest), axis=1, keepdims=True)) + largest
        truth = lane == labels[rows, :]
        picked = jnp.sum(jnp.where(truth, logits, 0.0), axis=1, keepdims=True)
        loss += jnp.sum(logsum - picked, axis=0, keepdims=True)
        gap = (jnp.exp(logits - logsum) - jnp.where(truth, 1.0, 0.0)) * (1.0 / nodes)
        upstream_turned[:, rows] = gap.astype(jnp.bfloat16).T
    loss = loss * (1.0 / nodes)
    high = loss.astype(jnp.bfloat16).astype(jnp.float32)
    middle = (loss - high).astype(jnp.bfloat16).astype(jnp.float32)
    low = loss - high - middle
    half = SIDE * WIDTH
    back_turned[...] = jnp.dot(
        upstream_turned[...], dense[...], preferred_element_type=jnp.float32
    ).astype(jnp.bfloat16)
    back = back_turned[...].T
    for offset, out in ((1, sent), (0, own)):
        side = lax.rem(core[0] + offset, 2)
        columns = pl.ds(pl.multiple_of(side * half, half), half)
        second = jnp.dot(
            back_turned[: ROWS - features, :], hidden[:, columns], preferred_element_type=jnp.float32
        )
        row = lax.broadcasted_iota(jnp.int32, second.shape, 0)
        lane = lax.broadcasted_iota(jnp.int32, second.shape, 1)
        here = (row == LOSS_ROW - features) & (side == 0)
        second += jnp.where(here & (lane == 0), high, 0.0)
        second += jnp.where(here & (lane == 1), middle, 0.0)
        second += jnp.where(here & (lane == 2), low, 0.0)
        out[features:, :] = second.astype(out.dtype)
        back_hidden = jnp.dot(back, layer_two[:, columns], preferred_element_type=jnp.float32)
        back_before = (slope[:, columns] * back_hidden).astype(jnp.bfloat16)
        out[:features, :] = jnp.dot(
            mixed_turned[...], back_before, preferred_element_type=jnp.float32
        ).astype(out.dtype)


def on_device(
    features,
    source_part,
    source_row,
    adj_tiles,
    tile_row,
    tile_col,
    tile_count,
    labels,
    layer_one,
    layer_two,
):
    devices = lax.axis_size(AXES)
    nodes = source_part.shape[0]
    width, hidden = layer_one.shape
    classes = layer_two.shape[1]
    capacity = max(2, 2 * nodes // devices)
    slots = devices * capacity
    bf = jnp.bfloat16
    requests, position = call(
        number_requests,
        [
            jax.ShapeDtypeStruct((devices, capacity), jnp.int32),
            jax.ShapeDtypeStruct((1, nodes), jnp.int32),
        ],
        0,
        2,
        limit=56 << 20,
    )(source_part.reshape(1, nodes), source_row.reshape(1, nodes))
    wanted = lax.all_to_all(requests, AXES, split_axis=0, concat_axis=0, tiled=True)
    anywhere = pl.BlockSpec(memory_space=pl.ANY)
    vmem = pl.BlockSpec(memory_space=pltpu.VMEM)
    smem = pl.BlockSpec(memory_space=pltpu.SMEM)
    found = pl.pallas_call(
        fetch_rows,
        out_shape=jax.ShapeDtypeStruct((slots, width), bf),
        in_specs=[anywhere, anywhere],
        out_specs=anywhere,
        scratch_shapes=[
            pltpu.SMEM(wanted.shape, jnp.int32),
            pltpu.VMEM(features.shape, bf),
            pltpu.VMEM((features.shape[0] * PITCH + 64, 128), jnp.float32),
            pltpu.VMEM((128 * PITCH + 64, 128), jnp.float32),
            pltpu.VMEM((slots, width), bf),
            pltpu.SemaphoreType.DMA,
            pltpu.SemaphoreType.DMA((8,)),
            pltpu.SemaphoreType.DMA((slots // 128,)),
        ],
        compiler_params=pltpu.CompilerParams(vmem_limit_bytes=56 << 20),
    )(wanted, features)
    arrived = lax.all_to_all(found, AXES, split_axis=0, concat_axis=0, tiled=True)
    dense, moved = call(
        build_spread,
        [
            jax.ShapeDtypeStruct((nodes, nodes), bf),
            jax.ShapeDtypeStruct((nodes, slots), bf),
        ],
        3,
        2,
        cost=pl.CostEstimate(
            flops=2 * nodes * nodes * slots, bytes_accessed=12 << 20, transcendentals=0
        ),
    )(tile_row, tile_col, tile_count, adj_tiles, position)
    padded = jnp.pad(layer_two.T, ((0, 256 - classes), (0, 0)))
    core = lax.rem(lax.axis_index("store"), 2).astype(jnp.int32).reshape(1)
    half = SIDE * WIDTH
    sent, own = pl.pallas_call(
        partial(train, classes=classes),
        out_shape=[
            jax.ShapeDtypeStruct((ROWS, half), bf),
            jax.ShapeDtypeStruct((ROWS, half), bf),
        ],
        in_specs=[smem] + [anywhere] * 6,
        out_specs=[vmem] * 2,
        scratch_shapes=[
            pltpu.VMEM((slots, width), bf),
            pltpu.VMEM((nodes, slots), bf),
            pltpu.VMEM((nodes, nodes), bf),
            pltpu.VMEM((width, hidden), bf),
            pltpu.VMEM((256, hidden), bf),
            pltpu.VMEM((nodes, 1), jnp.int32),
            pltpu.VMEM((width, nodes), bf),
            pltpu.VMEM((nodes, hidden), jnp.float32),
            pltpu.VMEM((nodes, hidden), bf),
            pltpu.VMEM((nodes, 256), bf),
            pltpu.VMEM((256, nodes), bf),
            pltpu.VMEM((256, nodes), bf),
            pltpu.SemaphoreType.DMA((12,)),
        ],
        compiler_params=pltpu.CompilerParams(vmem_limit_bytes=50 << 20),
        cost_estimate=pl.CostEstimate(
            flops=12 * nodes * nodes * hidden, bytes_accessed=16 << 20, transcendentals=nodes * hidden
        ),
    )(
        core,
        arrived.reshape(slots, width),
        moved,
        dense,
        layer_one,
        padded,
        labels.reshape(nodes, 1),
    )
    grad_one, grad_two, loss = sum_over_devices(sent, own, width, classes)
    return (grad_one, grad_two.T, loss.reshape(()))


def solution(mesh):
    return jax.shard_map(
        on_device,
        mesh=mesh,
        in_specs=(
            P(("store", "batch"), None),
            P(("store", "batch")),
            P(("store", "batch")),
            P(("store", "batch"), None, None),
            P(("store", "batch")),
            P(("store", "batch")),
            P(("store", "batch")),
            P(("store", "batch")),
            P(),
            P(),
        ),
        out_specs=(P(), P(), P()),
        check_vma=False,
    )
```

```python
from functools import partial

import jax
import jax.numpy as jnp
from jax import lax
from jax.experimental import pallas as pl
from jax.experimental.pallas import tpu as pltpu
from jax.sharding import PartitionSpec as P

AXES = ("store", "batch")
SIDE = 4
WIDTH = 128
LOSS_ROW = 921
ROWS = 928
PITCH = 7


def flat(x, y, z, core):
    return ((x * SIDE + z) * 2 + core) * SIDE + y


def shift_pairs(axes, offset):
    pairs = []
    for x in range(SIDE):
        for y in range(SIDE):
            for z in range(SIDE):
                for core in range(2):
                    place = [x, y, z]
                    place[axes[core]] = (place[axes[core]] + offset) % SIDE
                    pairs.append((flat(x, y, z, core), flat(*place, core)))
    return pairs


def swap_pairs():
    return [
        (flat(x, y, z, core), flat(x, y, z, 1 - core))
        for x in range(SIDE)
        for y in range(SIDE)
        for z in range(SIDE)
        for core in range(2)
    ]


FIRST, SECOND, THIRD = (0, 1), (1, 2), (2, 0)


def split_loss(total):
    tail = total[ROWS - 8 :, :]
    row = lax.broadcasted_iota(jnp.int32, tail.shape, 0)
    lane = lax.broadcasted_iota(jnp.int32, tail.shape, 1)
    here = row == LOSS_ROW - (ROWS - 8)
    loss = jnp.sum(jnp.where(here & (lane < 3), tail, 0.0), axis=1, keepdims=True)
    high = loss.astype(jnp.bfloat16).astype(jnp.float32)
    middle = (loss - high).astype(jnp.bfloat16).astype(jnp.float32)
    low = (loss - high - middle).astype(jnp.bfloat16).astype(jnp.float32)
    parts = jnp.where(lane == 0, high, jnp.where(lane == 1, middle, jnp.where(lane == 2, low, 0.0)))
    return jnp.where(here, parts, tail)


def store_total(out, columns, total):
    out[: ROWS - 16, columns] = total[: ROWS - 16].astype(jnp.bfloat16)
    last = jnp.concatenate([total[ROWS - 16 : ROWS - 8], split_loss(total)], axis=0)
    out[ROWS - 16 :, columns] = last.astype(jnp.bfloat16)


def first_add(place, own, arrived, keep, one, two, three):
    for offset, out in ((1, one), (2, two), (3, three), (0, keep)):
        block = lax.rem(place[0] + offset, SIDE)
        columns = pl.ds(pl.multiple_of(block * WIDTH, WIDTH), WIDTH)
        total = own[:, columns].astype(jnp.float32) + arrived[:, columns].astype(jnp.float32)
        store_total(out, slice(None), total)


def four_add(own, one, two, three, out):
    total = (own[...].astype(jnp.float32) + two[...].astype(jnp.float32)) + (
        one[...].astype(jnp.float32) + three[...].astype(jnp.float32)
    )
    store_total(out, slice(None), total)


def place_blocks(place, own, one, two, three, out):
    for offset, block in ((0, own), (1, one), (2, two), (3, three)):
        at = lax.rem(place[0] + SIDE - offset, SIDE)
        out[:, pl.ds(pl.multiple_of(at * WIDTH, WIDTH), WIDTH)] = block[...]


def write_half(at, part, one_far, two_far, one, two, leaving):
    half = part.shape[1]
    features = one.shape[0]
    classes = two.shape[0]
    columns = pl.ds(pl.multiple_of(at * half, half), half)
    two[...] = part[features:, :].astype(jnp.float32)[:classes]
    copies = [pltpu.make_async_copy(two, two_far.at[:, columns], leaving.at[0])]
    copies[0].start()
    step = features // 4
    for index in range(4):
        rows = slice(index * step, (index + 1) * step)
        one[rows, :] = part[rows, :].astype(jnp.float32)
        lines = pl.ds(index * step, step)
        copies.append(
            pltpu.make_async_copy(
                one.at[lines, :], one_far.at[lines, columns], leaving.at[index + 1]
            )
        )
        copies[-1].start()
    return copies


def read_loss(part):
    tail = part[ROWS - 16 :, :WIDTH].astype(jnp.float32)
    row = lax.broadcasted_iota(jnp.int32, tail.shape, 0)
    lane = lax.broadcasted_iota(jnp.int32, tail.shape, 1)
    mine = (row == LOSS_ROW - (ROWS - 16)) & (lane < 3)
    return jnp.sum(jnp.sum(jnp.where(mine, tail, 0.0), axis=1, keepdims=True), axis=0, keepdims=True)


def write_own(core, own, one_far, two_far, one, two, leaving):
    for copy in write_half(core[0], own, one_far, two_far, one, two, leaving):
        copy.wait()


def write_other(core, own, other, one_in, two_in, one_far, two_far, loss, one, two, leaving):
    copies = write_half(1 - core[0], other, one_far, two_far, one, two, leaving)
    loss[...] = jnp.where(core[0] == 0, read_loss(own), read_loss(other))
    for copy in copies:
        copy.wait()


def call(kernel, outs, scalars=0, arrays=0, limit=16 << 20, cost=None, scratch=()):
    vmem = pl.BlockSpec(memory_space=pltpu.VMEM)
    smem = pl.BlockSpec(memory_space=pltpu.SMEM)
    return pl.pallas_call(
        kernel,
        out_shape=outs,
        in_specs=[smem] * scalars + [vmem] * arrays,
        out_specs=jax.tree.map(lambda _: vmem, outs),
        scratch_shapes=list(scratch),
        compiler_params=pltpu.CompilerParams(vmem_limit_bytes=limit),
        cost_estimate=cost,
    )


def sum_over_devices(sent, own, features, classes):
    store, batch = lax.axis_index("store"), lax.axis_index("batch")
    core = lax.rem(store, 2)
    place = jnp.where(core == 0, store // (2 * SIDE), batch).astype(jnp.int32).reshape(1)
    core = core.astype(jnp.int32).reshape(1)
    bf = jnp.bfloat16
    block = jax.ShapeDtypeStruct((ROWS, WIDTH), bf)
    arrived = lax.ppermute(sent, AXES, swap_pairs())
    keep, *parts = call(first_add, [block] * 4, 1, 2)(place, own, arrived)
    got = [lax.ppermute(part, AXES, shift_pairs(FIRST, k + 1)) for k, part in enumerate(parts)]
    total = call(four_add, block, 0, 4)(keep, *got)
    for axes in (SECOND, THIRD):
        got = [lax.ppermute(total, AXES, shift_pairs(axes, k)) for k in (1, 2, 3)]
        total = call(four_add, block, 0, 4)(total, *got)
    got = [lax.ppermute(total, AXES, shift_pairs(FIRST, k)) for k in (1, 2, 3)]
    strip = call(place_blocks, jax.ShapeDtypeStruct((ROWS, SIDE * WIDTH), bf), 1, 4)(
        place, total, *got
    )
    other = lax.ppermute(strip, AXES, swap_pairs())
    half = SIDE * WIDTH
    grads = [
        jax.ShapeDtypeStruct((features, 2 * half), jnp.float32),
        jax.ShapeDtypeStruct((classes, 2 * half), jnp.float32),
    ]
    anywhere = pl.BlockSpec(memory_space=pl.ANY)
    vmem = pl.BlockSpec(memory_space=pltpu.VMEM)
    smem = pl.BlockSpec(memory_space=pltpu.SMEM)
    scratch = [
        pltpu.VMEM((features, half), jnp.float32),
        pltpu.VMEM((classes, half), jnp.float32),
        pltpu.SemaphoreType.DMA((5,)),
    ]
    params = pltpu.CompilerParams(vmem_limit_bytes=16 << 20)
    grad_one, grad_two = pl.pallas_call(
        write_own,
        out_shape=grads,
        in_specs=[smem, vmem],
        out_specs=[anywhere] * 2,
        scratch_shapes=scratch,
        compiler_params=params,
    )(core, strip)
    return pl.pallas_call(
        write_other,
        out_shape=[*grads, jax.ShapeDtypeStruct((1, 1), jnp.float32)],
        in_specs=[smem, vmem, vmem, anywhere, anywhere],
        out_specs=[anywhere, anywhere, vmem],
        scratch_shapes=scratch,
        input_output_aliases={3: 0, 4: 1},
        compiler_params=params,
    )(core, strip, other, grad_one, grad_two)


def number_requests(parts, rows, requests, position):
    devices, capacity = requests.shape
    nodes = parts.shape[1]
    piece = 128
    owner = lax.broadcasted_iota(jnp.int32, (devices, nodes), 0)
    mine = jnp.where(owner == parts[...], 1.0, 0.0)
    line = lax.broadcasted_iota(jnp.int32, (piece, piece), 0)
    lane = lax.broadcasted_iota(jnp.int32, (piece, piece), 1)
    earlier = jnp.where(line < lane, 1.0, 0.0).astype(jnp.bfloat16)
    seen = jnp.zeros((devices, 1), jnp.float32)
    slots = []
    for start in range(0, nodes, piece):
        here = mine[:, start : start + piece]
        rank = jnp.dot(here.astype(jnp.bfloat16), earlier, preferred_element_type=jnp.float32)
        slots.append(jnp.sum(here * (rank + seen), axis=0, keepdims=True))
        seen = seen + jnp.sum(here, axis=1, keepdims=True)
    slot = jnp.concatenate(slots, axis=1).astype(jnp.int32)
    position[...] = parts[...] * capacity + slot
    placed = lax.broadcasted_iota(jnp.int32, (capacity, nodes), 0) == slot
    total = jnp.zeros((devices, capacity), jnp.float32)
    for scale, digit in ((64.0, lax.shift_right_logical(rows[...], 6)), (1.0, rows[...] & 63)):
        values = jnp.where(placed, digit.astype(jnp.float32), 0.0).astype(jnp.bfloat16)
        total += scale * lax.dot_general(
            mine.astype(jnp.bfloat16),
            values,
            (((1,), (1,)), ((), ())),
            preferred_element_type=jnp.float32,
        )
    requests[...] = total.astype(jnp.int32)


def fetch_rows(wanted_far, table, far, wanted, narrow, wide, some, out, listed, arrival, leaving):
    stored, width = table.shape
    pieces = width // 128
    step = stored // arrival.shape[0]

    def load(block):
        rows = pl.ds(block * step, step)
        return pltpu.make_async_copy(table.at[rows, :], narrow.at[rows, :], arrival.at[block])

    listing = pltpu.make_async_copy(wanted_far, wanted, listed)
    listing.start()
    for block in range(arrival.shape[0]):
        load(block).start()
    for block in range(arrival.shape[0]):
        load(block).wait()

        @pl.loop(0, step // 64)
        def _(part):
            start = pl.multiple_of(block * step + part * 64, 64)
            values = narrow[pl.ds(start, 64), :].astype(jnp.float32)
            for line in range(0, 64, 8):
                for piece in range(pieces):
                    lines = pl.ds((start + line) * PITCH + piece, 8, stride=PITCH)
                    wide[lines, :] = values[line : line + 8, piece * 128 : (piece + 1) * 128]

    listing.wait()
    devices, capacity = wanted.shape
    group = out.shape[0] // leaving.shape[0]
    owners = group // capacity

    def send(block):
        rows = pl.ds(pl.multiple_of(block * group, group), group)
        return pltpu.make_async_copy(out.at[rows, :], far.at[rows, :], leaving.at[block])

    @pl.loop(0, devices // owners)
    def _(block):
        for line in range(group):
            row = wanted[block * owners + line // capacity, line % capacity]
            some[pl.ds(line * PITCH, pieces), :] = wide[pl.ds(row * PITCH, pieces), :]
        for line in range(0, group, 16):
            rows = pl.ds(pl.multiple_of(block * group + line, 16), 16)
            for piece in range(pieces):
                halves = [
                    some[pl.ds((line + half) * PITCH + piece, 8, stride=PITCH), :] for half in (0, 8)
                ]
                out[rows, piece * 128 : (piece + 1) * 128] = jnp.concatenate(halves, axis=0).astype(
                    jnp.bfloat16
                )
        send(block).start()

    @pl.loop(0, devices // owners)
    def _(block):
        send(block).wait()


def build_spread(row, column, count, tiles, position, dense, moved):
    nodes = dense.shape[0]
    tile = tiles.shape[1]
    dense[...] = jnp.zeros_like(dense)

    @pl.loop(0, count[0])
    def _(t):
        at_row = pl.ds(pl.multiple_of(row[t] * tile, tile), tile)
        at_column = pl.ds(pl.multiple_of(column[t] * tile, tile), tile)
        dense[at_row, at_column] = tiles[t]

    width = 256

    @pl.loop(0, moved.shape[1] // width)
    def _(step):
        start = pl.multiple_of(step * width, width)
        slot = lax.broadcasted_iota(jnp.int32, (width, nodes), 0) + start
        chosen = jnp.where(slot == position[...], 1.0, 0.0).astype(jnp.bfloat16)
        moved[:, pl.ds(start, width)] = lax.dot_general(
            dense[...], chosen, (((1,), (1,)), ((), ())), preferred_element_type=jnp.float32
        ).astype(jnp.bfloat16)


def train(
    core,
    arrived_far,
    moved_far,
    dense_far,
    one_far,
    two_far,
    labels_far,
    sent,
    own,
    arrived,
    moved,
    dense,
    layer_one,
    layer_two,
    labels,
    mixed_turned,
    slope,
    hidden,
    scored,
    upstream_turned,
    back_turned,
    arrival,
    *,
    classes,
):
    nodes = dense.shape[0]
    features = mixed_turned.shape[0]
    step = 256
    tiles = range(0, nodes, step)

    def load(index, far, near):
        return pltpu.make_async_copy(far, near, arrival.at[index])

    part = arrived.shape[0] // SIDE
    get_arrived = [
        load(at, arrived_far.at[pl.ds(at * part, part), :], arrived.at[pl.ds(at * part, part), :])
        for at in range(SIDE)
    ]
    get_one = load(4, one_far, layer_one)
    get_dense = load(5, dense_far, dense)
    get_two = load(6, two_far, layer_two)
    get_labels = load(7, labels_far, labels)
    get_moved = [
        load(8 + at, moved_far.at[pl.ds(start, step), :], moved.at[pl.ds(start, step), :])
        for at, start in enumerate(tiles)
    ]
    get_moved[0].start()
    for copy in get_arrived:
        copy.start()
    get_one.start()
    get_two.start()
    get_moved[0].wait()
    for at, start in enumerate(tiles):
        rows = slice(start, start + step)
        if at > 0:
            get_moved[at].wait()
            mixed = jnp.dot(moved[rows, :], arrived[...], preferred_element_type=jnp.float32)
        else:
            mixed = 0.0
            for index, copy in enumerate(get_arrived):
                copy.wait()
                slots = slice(index * part, (index + 1) * part)
                mixed += jnp.dot(
                    moved[rows, slots], arrived[slots, :], preferred_element_type=jnp.float32
                )
            for copy in get_moved[1:]:
                copy.start()
        mixed = mixed.astype(jnp.bfloat16)
        mixed_turned[:, rows] = mixed.T
        if at == 0:
            get_one.wait()
            get_two.wait()
            get_dense.start()
            get_labels.start()
        before = jnp.dot(mixed, layer_one[...], preferred_element_type=jnp.float32)
        square = before * before
        rate = 0.7978845608028654
        bend = jnp.tanh(before * (rate + (rate * 0.044715) * square))
        rise = 0.5 + 0.5 * bend
        active = (before * rise).astype(jnp.bfloat16)
        hidden[rows, :] = active
        slope[rows, :] = rise + 0.5 * before * (1.0 - bend * bend) * (
            rate + (3.0 * 0.044715 * rate) * square
        )
        scored[rows, :] = lax.dot_general(
            active, layer_two[...], (((1,), (1,)), ((), ())), preferred_element_type=jnp.float32
        ).astype(jnp.bfloat16)
    get_dense.wait()
    get_labels.wait()
    loss = jnp.zeros((1, 1), jnp.float32)
    for start in tiles:
        rows = slice(start, start + step)
        logits = jnp.dot(dense[rows, :], scored[...], preferred_element_type=jnp.float32)
        lane = lax.broadcasted_iota(jnp.int32, logits.shape, 1)
        logits = jnp.where(lane < classes, logits, -jnp.inf)
        largest = jnp.max(logits, axis=1, keepdims=True)
        logsum = jnp.log(jnp.sum(jnp.exp(logits - largest), axis=1, keepdims=True)) + largest
        truth = lane == labels[rows, :]
        picked = jnp.sum(jnp.where(truth, logits, 0.0), axis=1, keepdims=True)
        loss += jnp.sum(logsum - picked, axis=0, keepdims=True)
        gap = (jnp.exp(logits - logsum) - jnp.where(truth, 1.0, 0.0)) * (1.0 / nodes)
        upstream_turned[:, rows] = gap.astype(jnp.bfloat16).T
    loss = loss * (1.0 / nodes)
    high = loss.astype(jnp.bfloat16).astype(jnp.float32)
    middle = (loss - high).astype(jnp.bfloat16).astype(jnp.float32)
    low = loss - high - middle
    half = SIDE * WIDTH
    back_turned[...] = jnp.dot(
        upstream_turned[...], dense[...], preferred_element_type=jnp.float32
    ).astype(jnp.bfloat16)
    back = back_turned[...].T
    for offset, out in ((1, sent), (0, own)):
        side = lax.rem(core[0] + offset, 2)
        columns = pl.ds(pl.multiple_of(side * half, half), half)
        second = jnp.dot(
            back_turned[: ROWS - features, :], hidden[:, columns], preferred_element_type=jnp.float32
        )
        row = lax.broadcasted_iota(jnp.int32, second.shape, 0)
        lane = lax.broadcasted_iota(jnp.int32, second.shape, 1)
        here = (row == LOSS_ROW - features) & (side == 0)
        second += jnp.where(here & (lane == 0), high, 0.0)
        second += jnp.where(here & (lane == 1), middle, 0.0)
        second += jnp.where(here & (lane == 2), low, 0.0)
        out[features:, :] = second.astype(out.dtype)
        back_hidden = jnp.dot(back, layer_two[:, columns], preferred_element_type=jnp.float32)
        back_before = (slope[:, columns] * back_hidden).astype(jnp.bfloat16)
        out[:features, :] = jnp.dot(
            mixed_turned[...], back_before, preferred_element_type=jnp.float32
        ).astype(out.dtype)


def on_device(
    features,
    source_part,
    source_row,
    adj_tiles,
    tile_row,
    tile_col,
    tile_count,
    labels,
    layer_one,
    layer_two,
):
    devices = lax.axis_size(AXES)
    nodes = source_part.shape[0]
    width, hidden = layer_one.shape
    classes = layer_two.shape[1]
    capacity = max(2, 2 * nodes // devices)
    slots = devices * capacity
    bf = jnp.bfloat16
    requests, position = call(
        number_requests,
        [
            jax.ShapeDtypeStruct((devices, capacity), jnp.int32),
            jax.ShapeDtypeStruct((1, nodes), jnp.int32),
        ],
        0,
        2,
        limit=56 << 20,
    )(source_part.reshape(1, nodes), source_row.reshape(1, nodes))
    wanted = lax.all_to_all(requests, AXES, split_axis=0, concat_axis=0, tiled=True)
    anywhere = pl.BlockSpec(memory_space=pl.ANY)
    vmem = pl.BlockSpec(memory_space=pltpu.VMEM)
    smem = pl.BlockSpec(memory_space=pltpu.SMEM)
    found = pl.pallas_call(
        fetch_rows,
        out_shape=jax.ShapeDtypeStruct((slots, width), bf),
        in_specs=[anywhere, anywhere],
        out_specs=anywhere,
        scratch_shapes=[
            pltpu.SMEM(wanted.shape, jnp.int32),
            pltpu.VMEM(features.shape, bf),
            pltpu.VMEM((features.shape[0] * PITCH + 64, 128), jnp.float32),
            pltpu.VMEM((256 * PITCH + 64, 128), jnp.float32),
            pltpu.VMEM((slots, width), bf),
            pltpu.SemaphoreType.DMA,
            pltpu.SemaphoreType.DMA((8,)),
            pltpu.SemaphoreType.DMA((slots // 256,)),
        ],
        compiler_params=pltpu.CompilerParams(vmem_limit_bytes=56 << 20),
    )(wanted, features)
    arrived = lax.all_to_all(found, AXES, split_axis=0, concat_axis=0, tiled=True)
    dense, moved = call(
        build_spread,
        [
            jax.ShapeDtypeStruct((nodes, nodes), bf),
            jax.ShapeDtypeStruct((nodes, slots), bf),
        ],
        3,
        2,
        cost=pl.CostEstimate(
            flops=2 * nodes * nodes * slots, bytes_accessed=12 << 20, transcendentals=0
        ),
    )(tile_row, tile_col, tile_count, adj_tiles, position)
    padded = jnp.pad(layer_two.T, ((0, 256 - classes), (0, 0)))
    core = lax.rem(lax.axis_index("store"), 2).astype(jnp.int32).reshape(1)
    half = SIDE * WIDTH
    sent, own = pl.pallas_call(
        partial(train, classes=classes),
        out_shape=[
            jax.ShapeDtypeStruct((ROWS, half), bf),
            jax.ShapeDtypeStruct((ROWS, half), bf),
        ],
        in_specs=[smem] + [anywhere] * 6,
        out_specs=[vmem] * 2,
        scratch_shapes=[
            pltpu.VMEM((slots, width), bf),
            pltpu.VMEM((nodes, slots), bf),
            pltpu.VMEM((nodes, nodes), bf),
            pltpu.VMEM((width, hidden), bf),
            pltpu.VMEM((256, hidden), bf),
            pltpu.VMEM((nodes, 1), jnp.int32),
            pltpu.VMEM((width, nodes), bf),
            pltpu.VMEM((nodes, hidden), jnp.float32),
            pltpu.VMEM((nodes, hidden), bf),
            pltpu.VMEM((nodes, 256), bf),
            pltpu.VMEM((256, nodes), bf),
            pltpu.VMEM((256, nodes), bf),
            pltpu.SemaphoreType.DMA((12,)),
        ],
        compiler_params=pltpu.CompilerParams(vmem_limit_bytes=50 << 20),
        cost_estimate=pl.CostEstimate(
            flops=12 * nodes * nodes * hidden, bytes_accessed=16 << 20, transcendentals=nodes * hidden
        ),
    )(
        core,
        arrived.reshape(slots, width),
        moved,
        dense,
        layer_one,
        padded,
        labels.reshape(nodes, 1),
    )
    grad_one, grad_two, loss = sum_over_devices(sent, own, width, classes)
    return (grad_one, grad_two.T, loss.reshape(()))


def solution(mesh):
    return jax.shard_map(
        on_device,
        mesh=mesh,
        in_specs=(
            P(("store", "batch"), None),
            P(("store", "batch")),
            P(("store", "batch")),
            P(("store", "batch"), None, None),
            P(("store", "batch")),
            P(("store", "batch")),
            P(("store", "batch")),
            P(("store", "batch")),
            P(),
            P(),
        ),
        out_specs=(P(), P(), P()),
        check_vma=False,
    )
```
